128 devices in a mesh: table: 2 (over z_lo), batch: 64 (over y, z_hi, x, core).
Axes of the slice: x: 4, y: 4, z: 4 (z_hi: 2, z_lo: 2; z = z_hi * 2 + z_lo), core: 2. Of those that a mesh axis runs over, the one named last changes fastest.
Arguments:
- x_first: bfloat16 [8192, 4096], P('batch', 'table'), may hold values from -6 to 6
- x_layer: bfloat16 [8192, 4096], P('batch', 'table'), may hold values from -6 to 6
- pre_act: bfloat16 [8192, 4096], P('batch', 'table'), may hold values from -8 to 8
- gamma: float32 [4096], P('table'), may hold values from 0.3 to 3
- weight: float32 [4096, 4096], P('table', 'batch'), may hold values from -0.09375 to 0.09375
- cotangent: bfloat16 [8192, 4096], P('batch', 'table'), may hold values from -12 to 12
Outputs:
- grad_first: bfloat16 [8192, 4096], P('batch', 'table')
- grad_layer: bfloat16 [8192, 4096], P('batch', 'table')
- grad_weight: float32 [4096, 4096], P('table', 'batch')
- grad_bias: float32 [4096], P('table')
- grad_gamma: float32 [4096], P('table')
The draws below stay inside these ranges and needn't reach their ends.
All inputs are finite; a program needn't handle non-finite values.
Results may differ from the reference program's by a relative error of at most 0.005.
Values may be sent and summed in bfloat16 or wider, within the bound.
No kernel may reach another device: no remote copies, remote signals or barrier semaphores. Data moves between devices by JAX's collectives and lax.ppermute only.
A program may use at most 128 MiB of HBM per device.

```python
import math
import jax
import jax.numpy as jnp
from jax import lax

D = 4096
SAMPLES = 8192


def draw_cotangent(key, part):
    key_one = jax.random.fold_in(key, 11)
    row_scale = 1.0 + 2.0 * jnp.arange(SAMPLES, dtype=jnp.float32) / SAMPLES
    base = jnp.clip(jax.random.normal(key_one, (SAMPLES, D), jnp.float32), -4.0, 4.0)
    values = base * row_scale[:, None]
    return values.astype(jnp.bfloat16)


def block_levels(key, extent, pieces, least, largest):
    factor_of = 1.0
    for position, parts in pieces:
        draws = jax.random.uniform(jax.random.fold_in(jax.random.fold_in(key, 6), position), (parts,), jnp.float32, least / len(pieces), largest / len(pieces))
        factor_of = factor_of * jnp.repeat(jnp.exp(draws), extent[position] // parts).reshape((-1,) + (1,) * (len(extent) - 1 - position))
    return factor_of


def scatter_about(rng, dims, width, limit, split=(), kind=jnp.bfloat16):
    array = width * jax.random.normal(rng, dims, jnp.float32)
    if split:
        array = array * block_levels(rng, dims, split, -0.22, 0.18)
    return jnp.clip(array, -limit, limit).astype(kind)


def setup_inputs(seed: int = 0) -> dict:
    streams_of = jax.random.split(jax.random.key(seed), 7)
    x_first = scatter_about(streams_of[0], (SAMPLES, D), 1.0, 6.0, ((0, 64), (1, 2)))
    x_layer = scatter_about(streams_of[1], (SAMPLES, D), 1.0, 6.0, ((0, 64), (1, 2)))
    pre_act = scatter_about(streams_of[2], (SAMPLES, D), 1.5, 8.0, ((0, 64), (1, 2)))
    gamma = jnp.clip(jnp.exp(math.log(3.0) - 2.3025851 * jax.random.uniform(streams_of[3], (D,), jnp.float32) ** block_levels(streams_of[3], (D,), ((0, 2),), -0.2, 0.2)), 0.3, 3.0)
    weight = scatter_about(streams_of[4], (D, D), D ** -0.5, 0.09375, ((0, 2), (1, 64)), jnp.float32)
    cotangent = draw_cotangent(jax.random.fold_in(streams_of[6], 71), 0)
    return {"x_first": x_first, "x_layer": x_layer, "pre_act": pre_act, "gamma": gamma, "weight": weight, "cotangent": cotangent}


def reference(x_first, x_layer, pre_act, gamma, weight, cotangent):
    weight_bf = weight.astype(jnp.bfloat16)
    pre_full = pre_act.astype(jnp.float32)
    gate_tanh = jnp.tanh(gamma[None, :] * pre_full)
    hidden = pre_full * gate_tanh
    cot_full = cotangent.astype(jnp.float32)
    grad_hidden = cot_full * x_first.astype(jnp.float32)
    grad_first = (cot_full * hidden).astype(jnp.bfloat16)
    slope = 1.0 - gate_tanh * gate_tanh
    grad_pre = (grad_hidden * (gate_tanh + gamma[None, :] * pre_full * slope)).astype(jnp.bfloat16)
    grad_gamma = jnp.sum(grad_hidden * pre_full * pre_full * slope, axis=0)
    grad_bias = jnp.sum(grad_pre.astype(jnp.float32), axis=0)
    grad_weight = lax.dot_general(grad_pre, x_layer, (((0,), (0,)), ((), ())), preferred_element_type=jnp.float32)
    grad_layer = (cot_full + jnp.dot(grad_pre, weight_bf, preferred_element_type=jnp.float32)).astype(jnp.bfloat16)
    return grad_first, grad_layer, grad_weight, grad_bias, grad_gamma
```

```python
import functools
import jax
import jax.numpy as jnp
from jax import lax
from jax.experimental import pallas as pl
from jax.experimental.pallas import tpu as pltpu
from jax.sharding import Mesh, PartitionSpec as P

BF = jnp.bfloat16
F32 = jnp.float32
PARAMS = pltpu.CompilerParams(vmem_limit_bytes=48 * 1024 * 1024)


def gate_body(first_ref, pre_ref, gamma_ref, cot_ref, gfirst_ref, gpre_ref, sums_ref):
    gamma = gamma_ref[...]
    pre = pre_ref[...].astype(F32)
    cot = cot_ref[...].astype(F32)
    gate = jnp.tanh(gamma * pre)
    gfirst_ref[...] = (cot * (pre * gate)).astype(BF)
    hidden = cot * first_ref[...].astype(F32)
    slope = 1.0 - gate * gate
    turn = pre * slope
    gpre = (hidden * (gate + gamma * turn)).astype(BF)
    gpre_ref[...] = gpre
    sums_ref[0:1, :] = jnp.sum(gpre.astype(F32), axis=0, keepdims=True)
    sums_ref[1:2, :] = jnp.sum(hidden * pre * turn, axis=0, keepdims=True)


def gate_step(x_first, pre_act, gamma, cotangent):
    rows, width = x_first.shape
    tile = 512
    block = pl.BlockSpec((rows, tile), lambda j: (0, j))
    return pl.pallas_call(
        gate_body,
        grid=(width // tile,),
        in_specs=[block, block, pl.BlockSpec((1, tile), lambda j: (0, j)), block],
        out_specs=[block, block, pl.BlockSpec((2, tile), lambda j: (0, j))],
        out_shape=[
            jax.ShapeDtypeStruct((rows, width), BF),
            jax.ShapeDtypeStruct((rows, width), BF),
            jax.ShapeDtypeStruct((2, width), F32),
        ],
        compiler_params=PARAMS,
        cost_estimate=pl.CostEstimate(flops=rows * width * 20, bytes_accessed=rows * width * 10, transcendentals=rows * width),
        name="gate",
    )(x_first, pre_act, gamma, cotangent)


def layer_body(weight_ref, gpre_ref, out_ref):
    part = lax.dot_general(
        weight_ref[...], gpre_ref[...], (((1,), (1,)), ((), ())), preferred_element_type=F32
    ).astype(BF)
    pairs, owners, deep, wide = out_ref.shape
    for p in range(pairs):
        for a in range(owners):
            out_ref[p, a] = part[p * deep : (p + 1) * deep, a * wide : (a + 1) * wide]


def layer_product(weight_rows, gpre, pairs, owners):
    deep = weight_rows.shape[0] // pairs
    samples, width = gpre.shape
    wide = samples // owners
    step = 2
    return pl.pallas_call(
        layer_body,
        grid=(owners // step,),
        in_specs=[
            pl.BlockSpec(weight_rows.shape, lambda j: (0, 0)),
            pl.BlockSpec((step * wide, width), lambda j: (j, 0)),
        ],
        out_specs=pl.BlockSpec((pairs, step, deep, wide), lambda j: (0, j, 0, 0)),
        out_shape=jax.ShapeDtypeStruct((pairs, owners, deep, wide), BF),
        compiler_params=PARAMS,
        cost_estimate=pl.CostEstimate(
            flops=2 * weight_rows.size * samples, bytes_accessed=8 * 1024 * 1024, transcendentals=0
        ),
        name="layer_product",
    )(weight_rows, gpre)


def weight_body(cols_ref, gpre_ref, out_ref):
    out_ref[...] = lax.dot_general(
        cols_ref[...], gpre_ref[...], (((1,), (0,)), ((), ())), preferred_element_type=F32
    ).astype(BF)


def weight_product(cols, gpre):
    depth, samples = cols.shape
    width = gpre.shape[1]
    tile = 512
    return pl.pallas_call(
        weight_body,
        grid=(width // tile,),
        in_specs=[
            pl.BlockSpec(cols.shape, lambda j: (0, 0)),
            pl.BlockSpec((samples, tile), lambda j: (0, j)),
        ],
        out_specs=pl.BlockSpec((depth, tile), lambda j: (0, j)),
        out_shape=jax.ShapeDtypeStruct((depth, width), BF),
        compiler_params=PARAMS,
        cost_estimate=pl.CostEstimate(
            flops=2 * cols.size * width, bytes_accessed=8 * 1024 * 1024, transcendentals=0
        ),
        name="weight_product",
    )(cols, gpre)


def total_body(parts_ref, out_ref):
    total = parts_ref[0].astype(F32)
    for k in range(1, parts_ref.shape[0]):
        total = total + parts_ref[k].astype(F32)
    out_ref[...] = total


def total_parts(parts):
    count, rows, width = parts.shape
    tile = 512
    return pl.pallas_call(
        total_body,
        grid=(width // tile,),
        in_specs=[pl.BlockSpec((count, rows, tile), lambda j: (0, 0, j))],
        out_specs=pl.BlockSpec((rows, tile), lambda j: (0, j)),
        out_shape=jax.ShapeDtypeStruct((rows, width), F32),
        compiler_params=PARAMS,
        name="total",
    )(parts)


def finish_body(parts_ref, cot_ref, out_ref):
    owners, cols = parts_ref.shape[1], parts_ref.shape[3]
    total = parts_ref[0, :, 0].astype(F32) + parts_ref[1, :, 0].astype(F32)
    total = total.reshape(owners * cols, total.shape[2])
    out_ref[...] = (cot_ref[...].astype(F32) + total.T).astype(BF)


def finish(parts, cotangent):
    pairs, owners, blocks, cols, rows = parts.shape
    wide = owners * cols
    return pl.pallas_call(
        finish_body,
        grid=(blocks,),
        in_specs=[
            pl.BlockSpec((pairs, owners, 1, cols, rows), lambda j: (0, 0, j, 0, 0)),
            pl.BlockSpec((rows, wide), lambda j: (0, j)),
        ],
        out_specs=pl.BlockSpec((rows, wide), lambda j: (0, j)),
        out_shape=jax.ShapeDtypeStruct((rows, blocks * wide), BF),
        compiler_params=PARAMS,
        name="finish",
    )(parts, cotangent)


def shards(x_first, x_layer, pre_act, gamma, weight, cotangent):
    near, far, both = ("x", "c"), ("y", "h"), ("t", "x", "c")
    n_near, n_far, pairs = 8, 8, 2
    samples, half = x_first.shape
    cols = weight.shape[1]
    blocks = half // (n_near * cols)
    by_owner = x_layer.T.reshape(blocks, n_near, cols, samples).transpose(1, 0, 2, 3)
    by_owner = by_owner.reshape(n_near, blocks * cols, samples)
    sent = jnp.concatenate([by_owner] * pairs, axis=0)
    came = lax.all_to_all(sent, both, 0, 0, tiled=True)
    layer_cols = came.reshape(pairs, n_near, blocks * cols, samples).transpose(0, 2, 1, 3)
    layer_cols = layer_cols.reshape(pairs * blocks * cols, n_near * samples)

    weight_rows = lax.all_gather(weight.T.astype(BF), far, axis=0, tiled=True)

    grad_first, gpre, sums = gate_step(x_first, pre_act, gamma[None, :], cotangent)
    gpre_all = lax.all_gather(gpre, near, axis=0, tiled=True)

    partial_layer = layer_product(weight_rows, gpre_all, pairs, n_near)
    partial_layer = partial_layer.reshape(pairs * n_near, blocks * cols, samples)
    partial_weight = weight_product(layer_cols, gpre_all).reshape(n_far, cols, half)

    weight_parts = lax.all_to_all(partial_weight, far, 0, 0, tiled=True)
    layer_parts = lax.all_to_all(partial_layer, both, 0, 0, tiled=True)
    grad_layer = finish(layer_parts.reshape(pairs, n_near, blocks, cols, samples), cotangent)
    grad_weight = total_parts(weight_parts).T

    sums = jnp.sum(lax.all_gather(sums, near, axis=0), axis=0)
    sums = jnp.sum(lax.all_gather(sums, far, axis=0), axis=0)
    return grad_first, grad_layer, grad_weight, sums[0], sums[1]


def solution(mesh):
    fine = Mesh(mesh.devices.reshape(2, 4, 2, 4, 2), ("t", "y", "h", "x", "c"))
    batch = ("y", "h", "x", "c")
    wide = P(batch, "t")
    return jax.shard_map(
        shards,
        mesh=fine,
        in_specs=(wide, wide, wide, P("t"), P("t", batch), wide),
        out_specs=(wide, wide, P("t", batch), P("t"), P("t")),
        check_vma=False,
    )
```

```python
import jax
import jax.numpy as jnp
from jax import lax
from jax.experimental import pallas as pl
from jax.experimental.pallas import tpu as pltpu
from jax.sharding import Mesh, PartitionSpec as P

BF = jnp.bfloat16
F32 = jnp.float32
PARAMS = pltpu.CompilerParams(vmem_limit_bytes=24 * 1024 * 1024)
ANY = pl.BlockSpec(memory_space=pl.ANY)


def gate_body(first_ref, pre_ref, gamma_ref, cot_ref, gfirst_ref, gpre_ref, sums_ref):
    gamma = gamma_ref[...]
    pre = pre_ref[...].astype(F32)
    cot = cot_ref[...].astype(F32)
    gate = jnp.tanh(gamma * pre)
    gfirst_ref[...] = (cot * (pre * gate)).astype(BF)
    hidden = cot * first_ref[...].astype(F32)
    slope = 1.0 - gate * gate
    turn = pre * slope
    gpre = (hidden * (gate + gamma * turn)).astype(BF)
    gpre_ref[...] = gpre
    sums_ref[0:1, :] = jnp.sum(gpre.astype(F32), axis=0, keepdims=True)
    sums_ref[1:2, :] = jnp.sum(hidden * pre * turn, axis=0, keepdims=True)


def gate_step(x_first, pre_act, gamma, cotangent):
    rows, width = x_first.shape
    tile = 512
    block = pl.BlockSpec((rows, tile), lambda j: (0, j))
    return pl.pallas_call(
        gate_body,
        grid=(width // tile,),
        in_specs=[block, block, pl.BlockSpec((1, tile), lambda j: (0, j)), block],
        out_specs=[block, block, pl.BlockSpec((2, tile), lambda j: (0, j))],
        out_shape=[
            jax.ShapeDtypeStruct((rows, width), BF),
            jax.ShapeDtypeStruct((rows, width), BF),
            jax.ShapeDtypeStruct((2, width), F32),
        ],
        compiler_params=pltpu.CompilerParams(vmem_limit_bytes=60 * 1024 * 1024),
        cost_estimate=pl.CostEstimate(flops=rows * width * 20, bytes_accessed=rows * width * 10, transcendentals=rows * width),
        name="gate",
    )(x_first, pre_act, gamma, cotangent)


def load_samples(pieces, samples_ref, sems):
    rows = pieces[0].shape[0]
    x, c = lax.axis_index("x"), lax.axis_index("c")
    copies = []
    for k in range(4):
        for s in range(2):
            owner = lax.rem(x + 4 - k, 4) * 2 + (c if s == 0 else 1 - c)
            place = pl.ds(pl.multiple_of(owner * rows, rows), rows)
            copies.append(pltpu.make_async_copy(pieces[2 * k + s], samples_ref.at[place], sems.at[2 * k + s]))
    for copy in copies:
        copy.start()
    return copies


def product_body(*refs):
    pieces, weights, cols_ref = refs[:8], refs[8:12], refs[12]
    wpart_ref, lpart_ref, samples_ref, grid_ref, rows_ref, sems, more, last = refs[13:]
    pairs, owners, deep, rows = cols_ref.shape
    copies = load_samples(pieces, samples_ref, sems)
    for p in range(pairs):
        for a in range(owners):
            target = grid_ref.at[p * deep : (p + 1) * deep, a * rows : (a + 1) * rows]
            copies.append(pltpu.make_async_copy(cols_ref.at[p, a], target, more.at[p * owners + a]))
            copies[-1].start()
    y, h = lax.axis_index("y"), lax.axis_index("h")
    short = weights[0].shape[0] // 2
    moves = []
    for k in range(4):
        for s in range(2):
            block = lax.rem(y + 4 - k, 4) * 2 + (h if s == 0 else 1 - h)
            place = pl.ds(pl.multiple_of(block * short, short), short)
            moves.append(
                pltpu.make_async_copy(weights[k].at[s * short : (s + 1) * short], rows_ref.at[place], last.at[2 * k + s])
            )
            moves[-1].start()
    for copy in copies:
        copy.wait()
    tile = 512
    for j in range(wpart_ref.shape[1] // tile):
        part = jnp.dot(grid_ref[...], samples_ref[:, j * tile : (j + 1) * tile], preferred_element_type=F32)
        wpart_ref[:, j * tile : (j + 1) * tile] = part.astype(BF)
    for move in moves:
        move.wait()
    for j in range(owners // 2):
        part = lax.dot_general(
            rows_ref[...],
            samples_ref[2 * j * rows : 2 * (j + 1) * rows, :],
            (((1,), (1,)), ((), ())),
            preferred_element_type=F32,
        ).astype(BF)
        for p in range(pairs):
            for a in range(2):
                lpart_ref[p, 2 * j + a] = part[p * deep : (p + 1) * deep, a * rows : (a + 1) * rows]


def products(pieces, weights, cols):
    rows, width = pieces[0].shape
    pairs, owners, deep, _ = cols.shape
    depth = pairs * deep
    return pl.pallas_call(
        product_body,
        in_specs=[ANY] * 13,
        out_specs=[pl.BlockSpec(memory_space=pltpu.VMEM)] * 2,
        out_shape=[
            jax.ShapeDtypeStruct((depth, width), BF),
            jax.ShapeDtypeStruct((pairs, owners, deep, rows), BF),
        ],
        scratch_shapes=[
            pltpu.VMEM((owners * rows, width), BF),
            pltpu.VMEM((depth, owners * rows), BF),
            pltpu.VMEM((depth, width), BF),
            pltpu.SemaphoreType.DMA((8,)),
            pltpu.SemaphoreType.DMA((16,)),
            pltpu.SemaphoreType.DMA((8,)),
        ],
        compiler_params=PARAMS,
        cost_estimate=pl.CostEstimate(
            flops=4 * owners * rows * width * depth, bytes_accessed=12 * 1024 * 1024, transcendentals=0
        ),
        name="products",
    )(*pieces, *weights, cols)


def total_body(parts_ref, out_ref):
    total = parts_ref[0].astype(F32)
    for k in range(1, parts_ref.shape[0]):
        total = total + parts_ref[k].astype(F32)
    out_ref[...] = total


def total_parts(parts):
    count, rows, width = parts.shape
    tile = 512
    return pl.pallas_call(
        total_body,
        grid=(width // tile,),
        in_specs=[pl.BlockSpec((count, rows, tile), lambda j: (0, 0, j))],
        out_specs=pl.BlockSpec((rows, tile), lambda j: (0, j)),
        out_shape=jax.ShapeDtypeStruct((rows, width), F32),
        compiler_params=PARAMS,
        name="total",
    )(parts)


def finish_body(parts_ref, cot_ref, out_ref):
    owners, cols = parts_ref.shape[1], parts_ref.shape[3]
    total = parts_ref[0, :, 0].astype(F32) + parts_ref[1, :, 0].astype(F32)
    total = total.reshape(owners * cols, total.shape[2])
    out_ref[...] = (cot_ref[...].astype(F32) + total.T).astype(BF)


def finish(parts, cotangent):
    pairs, owners, blocks, cols, rows = parts.shape
    wide = owners * cols
    return pl.pallas_call(
        finish_body,
        grid=(blocks,),
        in_specs=[
            pl.BlockSpec((pairs, owners, 1, cols, rows), lambda j: (0, 0, j, 0, 0)),
            pl.BlockSpec((rows, wide), lambda j: (0, j)),
        ],
        out_specs=pl.BlockSpec((rows, wide), lambda j: (0, j)),
        out_shape=jax.ShapeDtypeStruct((rows, blocks * wide), BF),
        compiler_params=PARAMS,
        name="finish",
    )(parts, cotangent)


def ahead(value, axis, size, steps):
    return lax.ppermute(value, axis, [(i, (i + steps) % size) for i in range(size)])


def swap(value, axis, size, bit):
    return lax.ppermute(value, axis, [(i, i ^ bit) for i in range(size)])


def shards(x_first, x_layer, pre_act, gamma, weight, cotangent):
    far, both = ("y", "h"), ("t", "x", "c")
    n_near, n_far, pairs = 8, 8, 2
    samples, half = x_first.shape
    cols = weight.shape[1]
    blocks = half // (n_near * cols)

    grad_first, gpre, sums = gate_step(x_first, pre_act, gamma[None, :], cotangent)
    mine = [gpre] + [ahead(gpre, "x", 4, k) for k in (1, 2, 3)]
    pieces = []
    for piece in mine:
        pieces += [piece, swap(piece, "c", 2, 1)]

    by_owner = x_layer.T.reshape(blocks, n_near, cols, samples).transpose(1, 0, 2, 3)
    by_owner = by_owner.reshape(n_near, blocks * cols, samples)
    sent = jnp.concatenate([by_owner] * pairs, axis=0)
    came = lax.all_to_all(sent, both, 0, 0, tiled=True).reshape(pairs, n_near, blocks * cols, samples)

    weight_bf = weight.T.astype(BF)
    weight_two = jnp.concatenate([weight_bf, swap(weight_bf, "h", 2, 1)], axis=0)
    weights = [weight_two] + [ahead(weight_two, "y", 4, k) for k in (1, 2, 3)]

    sums, _ = lax.optimization_barrier((sums, mine[1]))
    for axis, size, bit in (("c", 2, 1), ("x", 4, 1), ("x", 4, 2)):
        sums = sums + swap(sums, axis, size, bit)
    weights[0], sums = lax.optimization_barrier((weights[0], sums))

    partial_weight, partial_layer = products(pieces, weights, came)
    weight_parts = lax.all_to_all(partial_weight.reshape(n_far, cols, half), far, 0, 0, tiled=True)
    partial_layer = partial_layer.reshape(pairs * n_near, blocks * cols, samples)
    layer_parts = lax.all_to_all(partial_layer, both, 0, 0, tiled=True)
    sums, _ = lax.optimization_barrier((sums, partial_layer))
    for axis, size, bit in (("y", 4, 1), ("y", 4, 2), ("h", 2, 1)):
        sums = sums + swap(sums, axis, size, bit)
    grad_layer = finish(layer_parts.reshape(pairs, n_near, blocks, cols, samples), cotangent)
    grad_weight = total_parts(weight_parts).T

    return grad_first, grad_layer, grad_weight, sums[0], sums[1]


def solution(mesh):
    fine = Mesh(mesh.devices.reshape(2, 4, 2, 4, 2), ("t", "y", "h", "x", "c"))
    batch = ("y", "h", "x", "c")
    wide = P(batch, "t")
    return jax.shard_map(
        shards,
        mesh=fine,
        in_specs=(wide, wide, wide, P("t"), P("t", batch), wide),
        out_specs=(wide, wide, P("t", batch), P("t"), P("t")),
        check_vma=False,
    )
```

```python
import jax
import jax.numpy as jnp
from jax import lax
from jax.experimental import pallas as pl
from jax.experimental.pallas import tpu as pltpu
from jax.sharding import Mesh, PartitionSpec as P

BF = jnp.bfloat16
F32 = jnp.float32
PARAMS = pltpu.CompilerParams(vmem_limit_bytes=24 * 1024 * 1024)
LARGE = pltpu.CompilerParams(vmem_limit_bytes=60 * 1024 * 1024)
ANY = pl.BlockSpec(memory_space=pl.ANY)
VMEM = pl.BlockSpec(memory_space=pltpu.VMEM)
BRIEF = pl.CostEstimate(flops=1000, bytes_accessed=1000, transcendentals=0)
CHUNKS = 1


def gate_body(first_ref, pre_ref, gamma_ref, cot_ref, gpre_ref, sums_ref):
    gamma = gamma_ref[...]
    pre = pre_ref[...].astype(F32)
    gate = jnp.tanh(gamma * pre)
    hidden = cot_ref[...].astype(F32) * first_ref[...].astype(F32)
    turn = pre * (1.0 - gate * gate)
    gpre = (hidden * (gate + gamma * turn)).astype(BF)
    gpre_ref[...] = gpre
    sums_ref[0:1, :] = jnp.sum(gpre.astype(F32), axis=0, keepdims=True)
    sums_ref[1:2, :] = jnp.sum(hidden * pre * turn, axis=0, keepdims=True)


def gate_step(chunk, x_first, pre_act, gamma, cotangent):
    rows, width = x_first.shape
    width //= CHUNKS
    tile = 512
    steps = width // tile
    taken = pl.BlockSpec((rows, tile), lambda j: (0, j + chunk * steps))
    return pl.pallas_call(
        gate_body,
        grid=(steps,),
        in_specs=[taken, taken, pl.BlockSpec((1, tile), lambda j: (0, j + chunk * steps)), taken],
        out_specs=[pl.BlockSpec((rows, tile), lambda j: (0, j)), pl.BlockSpec((2, tile), lambda j: (0, j))],
        out_shape=[
            jax.ShapeDtypeStruct((rows, width), BF),
            jax.ShapeDtypeStruct((2, width), F32),
        ],
        compiler_params=LARGE,
        cost_estimate=pl.CostEstimate(flops=rows * width * 20, bytes_accessed=rows * width * 8, transcendentals=rows * width),
        name="gate",
    )(x_first, pre_act, gamma, cotangent)


def first_body(pre_ref, gamma_ref, cot_ref, out_ref):
    pre = pre_ref[...].astype(F32)
    out_ref[...] = (cot_ref[...].astype(F32) * (pre * jnp.tanh(gamma_ref[...] * pre))).astype(BF)


def first_step(pre_act, gamma, cotangent):
    rows, width = pre_act.shape
    tile = 512
    block = pl.BlockSpec((rows, tile), lambda j: (0, j))
    return pl.pallas_call(
        first_body,
        grid=(width // tile,),
        in_specs=[block, pl.BlockSpec((1, tile), lambda j: (0, j)), block],
        out_specs=block,
        out_shape=jax.ShapeDtypeStruct((rows, width), BF),
        compiler_params=LARGE,
        cost_estimate=BRIEF,
        name="first",
    )(pre_act, gamma, cotangent)


def weight_body(*refs):
    pieces, (same_ref, other_ref, out_ref, samples_ref, grid_ref, sems, more) = refs[:8], refs[8:]
    owners, deep, rows = same_ref.shape
    x, c, t = lax.axis_index("x"), lax.axis_index("c"), lax.axis_index("t")
    copies = []
    for k in range(4):
        for s in range(2):
            owner = lax.rem(x + 4 - k, 4) * 2 + (c if s == 0 else 1 - c)
            place = pl.ds(pl.multiple_of(owner * rows, rows), rows)
            copies.append(pltpu.make_async_copy(pieces[2 * k + s], samples_ref.at[place], sems.at[2 * k + s]))
            copies[-1].start()
    for p, ref in enumerate((same_ref, other_ref)):
        half = pl.ds(pl.multiple_of((t if p == 0 else 1 - t) * deep, deep), deep)
        for a in range(owners):
            target = grid_ref.at[half, a * rows : (a + 1) * rows]
            copies.append(pltpu.make_async_copy(ref.at[a], target, more.at[p * owners + a]))
            copies[-1].start()
    for copy in copies:
        copy.wait()
    tile = 512
    for j in range(out_ref.shape[1] // tile):
        part = jnp.dot(grid_ref[...], samples_ref[:, j * tile : (j + 1) * tile], preferred_element_type=F32)
        out_ref[:, j * tile : (j + 1) * tile] = part.astype(BF)


def weight_product(pieces, same, other):
    rows, width = pieces[0].shape
    owners, deep, _ = same.shape
    return pl.pallas_call(
        weight_body,
        in_specs=[ANY] * 10,
        out_specs=VMEM,
        out_shape=jax.ShapeDtypeStruct((2 * deep, width), BF),
        scratch_shapes=[
            pltpu.VMEM((owners * rows, width), BF),
            pltpu.VMEM((2 * deep, owners * rows), BF),
            pltpu.SemaphoreType.DMA((8,)),
            pltpu.SemaphoreType.DMA((16,)),
        ],
        compiler_params=PARAMS,
        cost_estimate=pl.CostEstimate(
            flops=4 * owners * rows * width * deep, bytes_accessed=8 * 1024 * 1024, transcendentals=0
        ),
        name="weight_product",
    )(*pieces, same, other)


def layer_body(*refs):
    count = 8 * CHUNKS
    pieces, weights = refs[:count], refs[count : count + 4]
    keep_ref, send_ref, samples_ref, grid_ref, sems, more = refs[count + 4 :]
    rows, width = pieces[0].shape
    short = weights[0].shape[0] // 2
    y, h, t = lax.axis_index("y"), lax.axis_index("h"), lax.axis_index("t")
    copies = []
    for q in range(CHUNKS):
        for k in range(8):
            target = samples_ref.at[k * rows : (k + 1) * rows, q * width : (q + 1) * width]
            copies.append(pltpu.make_async_copy(pieces[8 * q + k], target, sems.at[8 * q + k]))
            copies[-1].start()
    for k in range(4):
        place_y = lax.rem(y + 4 - k, 4)
        side = lax.rem(place_y // 2 + t, 2)
        for s in range(2):
            block = side * 4 + lax.rem(place_y, 2) * 2 + (h if s == 0 else 1 - h)
            place = pl.ds(pl.multiple_of(block * short, short), short)
            copies.append(
                pltpu.make_async_copy(weights[k].at[s * short : (s + 1) * short], grid_ref.at[place], more.at[2 * k + s])
            )
            copies[-1].start()
    for copy in copies:
        copy.wait()
    tall = 4 * short
    for j in range(4):
        part = lax.dot_general(
            grid_ref[...],
            samples_ref[2 * j * rows : 2 * (j + 1) * rows, :],
            (((1,), (1,)), ((), ())),
            preferred_element_type=F32,
        )
        for s in range(2):
            keep_ref[s, j] = part[:tall, s * rows : (s + 1) * rows]
            send_ref[s, j] = part[tall:, s * rows : (s + 1) * rows].astype(BF)


def layer_product(pieces, weights):
    rows, width = pieces[0].shape
    deep = 4 * weights[0].shape[0]
    return pl.pallas_call(
        layer_body,
        in_specs=[ANY] * (8 * CHUNKS + 4),
        out_specs=[VMEM, VMEM],
        out_shape=[
            jax.ShapeDtypeStruct((2, 4, deep // 2, rows), F32),
            jax.ShapeDtypeStruct((2, 4, deep // 2, rows), BF),
        ],
        scratch_shapes=[
            pltpu.VMEM((8 * rows, CHUNKS * width), BF),
            pltpu.VMEM((deep, CHUNKS * width), BF),
            pltpu.SemaphoreType.DMA((8 * CHUNKS,)),
            pltpu.SemaphoreType.DMA((8,)),
        ],
        compiler_params=PARAMS,
        cost_estimate=BRIEF,
        name="layer_product",
    )(*pieces, *weights)


def pair_body(keep_ref, came_ref, same_ref, swap_ref):
    same_ref[...] = (keep_ref[0] + came_ref[0].astype(F32)).astype(BF)
    swap_ref[...] = (keep_ref[1] + came_ref[1].astype(F32)).astype(BF)


def pair_sum(keep, came):
    shape = jax.ShapeDtypeStruct(keep.shape[1:], BF)
    return pl.pallas_call(
        pair_body,
        in_specs=[VMEM] * 2,
        out_specs=[VMEM] * 2,
        out_shape=[shape, shape],
        compiler_params=PARAMS,
        cost_estimate=BRIEF,
        name="pair_sum",
    )(keep, came)


def total_body(*refs):
    out_ref = refs[-1]
    for q, ref in enumerate(refs[:-1]):
        total = ref[0].astype(F32)
        for k in range(1, ref.shape[0]):
            total = total + ref[k].astype(F32)
        width = ref.shape[2]
        out_ref[:, q * width : (q + 1) * width] = total


def total_parts(parts):
    rows, width = parts[0].shape[1:]
    return pl.pallas_call(
        total_body,
        in_specs=[VMEM] * len(parts),
        out_specs=VMEM,
        out_shape=jax.ShapeDtypeStruct((rows, width * len(parts)), F32),
        compiler_params=PARAMS,
        cost_estimate=BRIEF,
        name="total",
    )(*parts)


def finish_body(*refs):
    parts, (cot_ref, out_ref, all_ref) = refs[:8], refs[8:]
    x, c = lax.axis_index("x"), lax.axis_index("c")
    blocks, owners, cols, rows = all_ref.shape
    for k in range(4):
        for s in range(2):
            owner = lax.rem(x + k, 4) * 2 + (c if s == 0 else 1 - c)
            for b in range(blocks):
                all_ref[b, owner] = parts[2 * k + s][b * cols : (b + 1) * cols, :].astype(F32)
    wide = owners * cols
    for b in range(blocks):
        total = all_ref[b].reshape(wide, rows).T
        span = slice(b * wide, (b + 1) * wide)
        out_ref[:, span] = (cot_ref[:, span].astype(F32) + total).astype(BF)


def finish(parts, cotangent, cols):
    tall, rows = parts[0].shape
    return pl.pallas_call(
        finish_body,
        in_specs=[VMEM] * 9,
        out_specs=VMEM,
        out_shape=jax.ShapeDtypeStruct(cotangent.shape, BF),
        scratch_shapes=[pltpu.VMEM((tall // cols, 8, cols, rows), F32)],
        compiler_params=PARAMS,
        cost_estimate=BRIEF,
        name="finish",
    )(*parts, cotangent)


def ahead(value, axis, size, steps):
    return lax.ppermute(value, axis, [(i, (i + steps) % size) for i in range(size)])


def swap(value, axis, size, bit):
    return lax.ppermute(value, axis, [(i, i ^ bit) for i in range(size)])


def shards(x_first, x_layer, pre_act, gamma, weight, cotangent):
    far, near = ("y", "h"), ("x", "c")
    n_near, n_far = 8, 8
    samples, half = x_first.shape
    cols = weight.shape[1]
    blocks = half // (n_near * cols)
    gamma = gamma[None, :]

    by_owner = x_layer.T.reshape(blocks, n_near, cols, samples).transpose(1, 0, 2, 3)
    by_owner = by_owner.reshape(n_near, blocks * cols, samples)
    same = lax.all_to_all(by_owner, near, 0, 0, tiled=True)
    other = swap(same, "t", 2, 1)

    own, sums = [], []
    for q in range(CHUNKS):
        gpre, part = gate_step(q, x_first, pre_act, gamma, cotangent)
        sums.append(part)
        own.append([gpre] + [ahead(gpre, "x", 4, k) for k in (1, 2, 3)])
    sums = jnp.concatenate(sums, axis=1)

    weight_bf = weight.T.astype(BF)
    weight_two = jnp.concatenate([weight_bf, swap(weight_bf, "h", 2, 1)], axis=0)
    weights = [weight_two] + [ahead(weight_two, "y", 4, k) for k in (1, 2, 3)]

    for axis, size, bit in (("y", 4, 1), ("y", 4, 2), ("h", 2, 1), ("c", 2, 1)):
        sums = sums + swap(sums, axis, size, bit)

    own, weights, sums, other = lax.optimization_barrier((own, weights, sums, other))
    pieces = []
    for q in range(CHUNKS):
        group = []
        for piece in own[q]:
            group += [piece, swap(piece, "c", 2, 1)]
        pieces.append(group)

    keep, sent = layer_product([piece for group in pieces for piece in group], weights)
    pieces, sent = lax.optimization_barrier((pieces, sent))
    weight_parts = []
    for q in range(CHUNKS):
        part = weight_product(pieces[q], same, other)
        weight_parts.append(lax.all_to_all(part.reshape(n_far, cols, half // CHUNKS), far, 0, 0, tiled=True))
    keep, part = lax.optimization_barrier((keep, part))
    mine, passed = pair_sum(keep, swap(sent, "t", 2, 1))
    passed = swap(passed, "c", 2, 1)
    parts = [mine[0], passed[0]]
    for k in (1, 2, 3):
        both = jnp.stack([mine[k], passed[k]])
        both = ahead(both, "x", 4, -k)
        parts += [both[0], both[1]]
    grad_layer = finish(parts, cotangent, cols)
    grad_weight = total_parts(weight_parts).T
    pre_act, sent = lax.optimization_barrier((pre_act, sent))
    grad_first = first_step(pre_act, gamma, cotangent)

    sums, _ = lax.optimization_barrier((sums, passed))
    for axis, size, bit in (("x", 4, 1), ("x", 4, 2)):
        sums = sums + swap(sums, axis, size, bit)
    return grad_first, grad_layer, grad_weight, sums[0], sums[1]


def solution(mesh):
    fine = Mesh(mesh.devices.reshape(2, 4, 2, 4, 2), ("t", "y", "h", "x", "c"))
    batch = ("y", "h", "x", "c")
    wide = P(batch, "t")
    return jax.shard_map(
        shards,
        mesh=fine,
        in_specs=(wide, wide, wide, P("t"), P("t", batch), wide),
        out_specs=(wide, wide, P("t", batch), P("t"), P("t")),
        check_vma=False,
    )
```

```python
import jax
import jax.numpy as jnp
from jax import lax
from jax.experimental import pallas as pl
from jax.experimental.pallas import tpu as pltpu
from jax.sharding import Mesh, PartitionSpec as P

BF = jnp.bfloat16
F32 = jnp.float32
PARAMS = pltpu.CompilerParams(vmem_limit_bytes=24 * 1024 * 1024)
LARGE = pltpu.CompilerParams(vmem_limit_bytes=60 * 1024 * 1024)
ANY = pl.BlockSpec(memory_space=pl.ANY)
VMEM = pl.BlockSpec(memory_space=pltpu.VMEM)
BRIEF = pl.CostEstimate(flops=1000, bytes_accessed=1000, transcendentals=0)
CHUNKS = 1


def gate_body(first_ref, pre_ref, gamma_ref, cot_ref, gpre_ref, sums_ref):
    gamma = gamma_ref[...]
    pre = pre_ref[...].astype(F32)
    gate = jnp.tanh(gamma * pre)
    hidden = cot_ref[...].astype(F32) * first_ref[...].astype(F32)
    turn = pre * (1.0 - gate * gate)
    gpre = (hidden * (gate + gamma * turn)).astype(BF)
    gpre_ref[...] = gpre
    sums_ref[0:1, :] = jnp.sum(gpre.astype(F32), axis=0, keepdims=True)
    sums_ref[1:2, :] = jnp.sum(hidden * pre * turn, axis=0, keepdims=True)


def gate_step(chunk, x_first, pre_act, gamma, cotangent):
    rows, width = x_first.shape
    width //= CHUNKS
    tile = 512
    steps = width // tile
    taken = pl.BlockSpec((rows, tile), lambda j: (0, j + chunk * steps))
    return pl.pallas_call(
        gate_body,
        grid=(steps,),
        in_specs=[taken, taken, pl.BlockSpec((1, tile), lambda j: (0, j + chunk * steps)), taken],
        out_specs=[pl.BlockSpec((rows, tile), lambda j: (0, j)), pl.BlockSpec((2, tile), lambda j: (0, j))],
        out_shape=[
            jax.ShapeDtypeStruct((rows, width), BF),
            jax.ShapeDtypeStruct((2, width), F32),
        ],
        compiler_params=LARGE,
        cost_estimate=pl.CostEstimate(flops=rows * width * 20, bytes_accessed=rows * width * 8, transcendentals=rows * width),
        name="gate",
    )(x_first, pre_act, gamma, cotangent)


def first_body(pre_ref, gamma_ref, cot_ref, out_ref):
    pre = pre_ref[...].astype(F32)
    out_ref[...] = (cot_ref[...].astype(F32) * (pre * jnp.tanh(gamma_ref[...] * pre))).astype(BF)


def first_step(pre_act, gamma, cotangent):
    rows, width = pre_act.shape
    tile = 512
    block = pl.BlockSpec((rows, tile), lambda j: (0, j))
    return pl.pallas_call(
        first_body,
        grid=(width // tile,),
        in_specs=[block, pl.BlockSpec((1, tile), lambda j: (0, j)), block],
        out_specs=block,
        out_shape=jax.ShapeDtypeStruct((rows, width), BF),
        compiler_params=LARGE,
        cost_estimate=BRIEF,
        name="first",
    )(pre_act, gamma, cotangent)


LAY = ((0, 0, 2), (1, 0, 2), (3, 0, 2), (2, 0, 1), (2, 1, 1))


def ring_gather(value, axis):
    rows = value.shape[0]
    left, right = ahead(value, axis, 4, 1), ahead(value, axis, 4, 3)
    far_low = ahead(left[: rows // 2], axis, 4, 1)
    far_high = ahead(right[rows // 2 :], axis, 4, 3)
    return [value, left, right, far_low, far_high]


def weight_body(*refs):
    pieces, (same_ref, other_ref, out_ref, samples_ref, grid_ref, tile_ref, sems, more, last) = refs[:10], refs[10:]
    owners, deep, rows = same_ref.shape
    x, c, t = lax.axis_index("x"), lax.axis_index("c"), lax.axis_index("t")
    copies = []
    for n, (back, start, size) in enumerate(LAY):
        for s in range(2):
            owner = lax.rem(x + 4 - back, 4) * 2 + (c if s == 0 else 1 - c)
            place = pl.ds(pl.multiple_of(owner * rows + start * rows // 2, rows // 2), size * rows // 2)
            copies.append(pltpu.make_async_copy(pieces[2 * n + s], samples_ref.at[place], sems.at[2 * n + s]))
            copies[-1].start()
    for p, ref in enumerate((same_ref, other_ref)):
        half = pl.ds(pl.multiple_of((t if p == 0 else 1 - t) * deep, deep), deep)
        for a in range(owners):
            target = grid_ref.at[half, a * rows : (a + 1) * rows]
            copies.append(pltpu.make_async_copy(ref.at[a], target, more.at[p * owners + a]))
            copies[-1].start()
    for copy in copies:
        copy.wait()
    tile = 512
    outs = []
    for j in range(out_ref.shape[1] // tile):
        span = slice(j * tile, (j + 1) * tile)
        part = jnp.dot(grid_ref[...], samples_ref[:, span], preferred_element_type=F32)
        tile_ref[:, span] = part.astype(BF)
        outs.append(pltpu.make_async_copy(tile_ref.at[:, span], out_ref.at[:, span], last.at[j]))
        outs[-1].start()
    for copy in outs:
        copy.wait()


def weight_product(pieces, same, other):
    rows, width = pieces[0].shape
    owners, deep, _ = same.shape
    return pl.pallas_call(
        weight_body,
        in_specs=[ANY] * 12,
        out_specs=ANY,
        out_shape=jax.ShapeDtypeStruct((2 * deep, width), BF),
        scratch_shapes=[
            pltpu.VMEM((owners * rows, width), BF),
            pltpu.VMEM((2 * deep, owners * rows), BF),
            pltpu.VMEM((2 * deep, width), BF),
            pltpu.SemaphoreType.DMA((10,)),
            pltpu.SemaphoreType.DMA((16,)),
            pltpu.SemaphoreType.DMA((width // 512,)),
        ],
        compiler_params=LARGE,
        cost_estimate=BRIEF,
        name="weight_product",
    )(*pieces, same, other)


def layer_body(*refs):
    count = 10 * CHUNKS
    pieces, weights = refs[:count], refs[count : count + 5]
    keep_ref, send_ref, samples_ref, grid_ref, sems, more = refs[count + 5 :]
    rows, width = pieces[0].shape
    short = weights[0].shape[0] // 2
    y, h, t = lax.axis_index("y"), lax.axis_index("h"), lax.axis_index("t")
    copies = []
    for q in range(CHUNKS):
        for n, (back, start, size) in enumerate(LAY):
            for s in range(2):
                first = (2 * back + s) * rows + start * rows // 2
                target = samples_ref.at[first : first + size * rows // 2, q * width : (q + 1) * width]
                copies.append(pltpu.make_async_copy(pieces[10 * q + 2 * n + s], target, sems.at[10 * q + 2 * n + s]))
                copies[-1].start()
    for n, (back, start, size) in enumerate(LAY):
        place_y = lax.rem(y + 4 - back, 4)
        side = lax.rem(place_y // 2 + t, 2)
        for s in range(size):
            block = side * 4 + lax.rem(place_y, 2) * 2 + (h if start + s == 0 else 1 - h)
            place = pl.ds(pl.multiple_of(block * short, short), short)
            copies.append(
                pltpu.make_async_copy(weights[n].at[s * short : (s + 1) * short], grid_ref.at[place], more.at[2 * n + s])
            )
            copies[-1].start()
    for copy in copies:
        copy.wait()
    tall = 4 * short
    for j in range(4):
        part = lax.dot_general(
            grid_ref[...],
            samples_ref[2 * j * rows : 2 * (j + 1) * rows, :],
            (((1,), (1,)), ((), ())),
            preferred_element_type=F32,
        )
        for s in range(2):
            keep_ref[s, j] = part[:tall, s * rows : (s + 1) * rows]
            send_ref[s, j] = part[tall:, s * rows : (s + 1) * rows].astype(BF)


def layer_product(pieces, weights):
    rows, width = pieces[0].shape
    deep = 4 * weights[0].shape[0]
    return pl.pallas_call(
        layer_body,
        in_specs=[ANY] * (10 * CHUNKS + 5),
        out_specs=[VMEM, VMEM],
        out_shape=[
            jax.ShapeDtypeStruct((2, 4, deep // 2, rows), F32),
            jax.ShapeDtypeStruct((2, 4, deep // 2, rows), BF),
        ],
        scratch_shapes=[
            pltpu.VMEM((8 * rows, CHUNKS * width), BF),
            pltpu.VMEM((deep, CHUNKS * width), BF),
            pltpu.SemaphoreType.DMA((10 * CHUNKS,)),
            pltpu.SemaphoreType.DMA((10,)),
        ],
        compiler_params=LARGE,
        cost_estimate=BRIEF,
        name="layer_product",
    )(*pieces, *weights)


def pair_body(keep_ref, came_ref, same_ref, swap_ref):
    same_ref[...] = (keep_ref[0] + came_ref[0].astype(F32)).astype(BF)
    swap_ref[...] = (keep_ref[1] + came_ref[1].astype(F32)).astype(BF)


def pair_sum(keep, came):
    shape = jax.ShapeDtypeStruct(keep.shape[1:], BF)
    return pl.pallas_call(
        pair_body,
        in_specs=[VMEM] * 2,
        out_specs=[VMEM] * 2,
        out_shape=[shape, shape],
        compiler_params=PARAMS,
        cost_estimate=BRIEF,
        name="pair_sum",
    )(keep, came)


def total_body(*refs):
    out_ref = refs[-1]
    for q, ref in enumerate(refs[:-1]):
        total = ref[0].astype(F32)
        for k in range(1, ref.shape[0]):
            total = total + ref[k].astype(F32)
        width = ref.shape[2]
        out_ref[:, q * width : (q + 1) * width] = total


def total_parts(parts):
    rows, width = parts[0].shape[1:]
    return pl.pallas_call(
        total_body,
        in_specs=[VMEM] * len(parts),
        out_specs=VMEM,
        out_shape=jax.ShapeDtypeStruct((rows, width * len(parts)), F32),
        compiler_params=PARAMS,
        cost_estimate=BRIEF,
        name="total",
    )(*parts)


def finish_body(*refs):
    parts, (cot_ref, out_ref, all_ref) = refs[:8], refs[8:]
    x, c = lax.axis_index("x"), lax.axis_index("c")
    blocks, owners, cols, rows = all_ref.shape
    for k in range(4):
        for s in range(2):
            owner = lax.rem(x + k, 4) * 2 + (c if s == 0 else 1 - c)
            for b in range(blocks):
                all_ref[b, owner] = parts[2 * k + s][b * cols : (b + 1) * cols, :].astype(F32)
    wide = owners * cols
    for b in range(blocks):
        total = all_ref[b].reshape(wide, rows).T
        span = slice(b * wide, (b + 1) * wide)
        out_ref[:, span] = (cot_ref[:, span].astype(F32) + total).astype(BF)


def finish(parts, cotangent, cols):
    tall, rows = parts[0].shape
    return pl.pallas_call(
        finish_body,
        in_specs=[VMEM] * 9,
        out_specs=VMEM,
        out_shape=jax.ShapeDtypeStruct(cotangent.shape, BF),
        scratch_shapes=[pltpu.VMEM((tall // cols, 8, cols, rows), F32)],
        compiler_params=PARAMS,
        cost_estimate=BRIEF,
        name="finish",
    )(*parts, cotangent)


def ahead(value, axis, size, steps):
    return lax.ppermute(value, axis, [(i, (i + steps) % size) for i in range(size)])


def swap(value, axis, size, bit):
    return lax.ppermute(value, axis, [(i, i ^ bit) for i in range(size)])


def shards(x_first, x_layer, pre_act, gamma, weight, cotangent):
    far, near = ("y", "h"), ("x", "c")
    n_near, n_far = 8, 8
    samples, half = x_first.shape
    cols = weight.shape[1]
    blocks = half // (n_near * cols)
    gamma = gamma[None, :]

    by_owner = x_layer.T.reshape(blocks, n_near, cols, samples).transpose(1, 0, 2, 3)
    by_owner = by_owner.reshape(n_near, blocks * cols, samples)
    same = lax.all_to_all(by_owner, near, 0, 0, tiled=True)
    other = swap(same, "t", 2, 1)

    own, sums = [], []
    for q in range(CHUNKS):
        gpre, part = gate_step(q, x_first, pre_act, gamma, cotangent)
        sums.append(part)
        own.append(ring_gather(gpre, "x"))
    sums = jnp.concatenate(sums, axis=1)

    weight_bf = weight.T.astype(BF)
    weight_two = jnp.concatenate([weight_bf, swap(weight_bf, "h", 2, 1)], axis=0)
    weights = ring_gather(weight_two, "y")

    for axis, size, bit in (("y", 4, 1), ("y", 4, 2), ("h", 2, 1), ("c", 2, 1), ("x", 4, 1), ("x", 4, 2)):
        sums = sums + swap(sums, axis, size, bit)

    own, weights, sums, other = lax.optimization_barrier((own, weights, sums, other))
    pieces = []
    for q in range(CHUNKS):
        group = []
        for piece in own[q]:
            group += [piece, swap(piece, "c", 2, 1)]
        pieces.append(group)

    weight_parts = []
    for q in range(CHUNKS):
        part = weight_product(pieces[q], same, other)
        weight_parts.append(lax.all_to_all(part.reshape(n_far, cols, half // CHUNKS), far, 0, 0, tiled=True))
    pieces, part = lax.optimization_barrier((pieces, part))
    keep, sent = layer_product([piece for group in pieces for piece in group], weights)
    mine, passed = pair_sum(keep, swap(sent, "t", 2, 1))
    passed = swap(passed, "c", 2, 1)
    parts = [mine[0], passed[0]]
    for k in (1, 2, 3):
        both = jnp.stack([mine[k], passed[k]])
        both = ahead(both, "x", 4, -k)
        parts += [both[0], both[1]]
    grad_layer = finish(parts, cotangent, cols)
    grad_weight = total_parts(weight_parts).T
    pre_act, sent = lax.optimization_barrier((pre_act, sent))
    grad_first = first_step(pre_act, gamma, cotangent)

    return grad_first, grad_layer, grad_weight, sums[0], sums[1]


def solution(mesh):
    fine = Mesh(mesh.devices.reshape(2, 4, 2, 4, 2), ("t", "y", "h", "x", "c"))
    batch = ("y", "h", "x", "c")
    wide = P(batch, "t")
    return jax.shard_map(
        shards,
        mesh=fine,
        in_specs=(wide, wide, wide, P("t"), P("t", batch), wide),
        out_specs=(wide, wide, P("t", batch), P("t"), P("t")),
        check_vma=False,
    )
```

```python
import jax
import jax.numpy as jnp
from jax import lax
from jax.experimental import pallas as pl
from jax.experimental.pallas import tpu as pltpu
from jax.sharding import Mesh, PartitionSpec as P

BF = jnp.bfloat16
F32 = jnp.float32
PARAMS = pltpu.CompilerParams(vmem_limit_bytes=24 * 1024 * 1024)
LARGE = pltpu.CompilerParams(vmem_limit_bytes=60 * 1024 * 1024)
ANY = pl.BlockSpec(memory_space=pl.ANY)
VMEM = pl.BlockSpec(memory_space=pltpu.VMEM)
BRIEF = pl.CostEstimate(flops=1000, bytes_accessed=1000, transcendentals=0)


def gate_body(first_ref, pre_ref, gamma_ref, cot_ref, gpre_ref, sums_ref):
    gamma = gamma_ref[...]
    pre = pre_ref[...].astype(F32)
    gate = jnp.tanh(gamma * pre)
    hidden = cot_ref[...].astype(F32) * first_ref[...].astype(F32)
    turn = pre * (1.0 - gate * gate)
    gpre = (hidden * (gate + gamma * turn)).astype(BF)
    for k in range(gpre_ref.shape[0]):
        gpre_ref[k] = gpre
    sums_ref[0:1, :] = jnp.sum(gpre.astype(F32), axis=0, keepdims=True)
    sums_ref[1:2, :] = jnp.sum(hidden * pre * turn, axis=0, keepdims=True)


def gate_step(x_first, pre_act, gamma, cotangent):
    rows, width = x_first.shape
    tile = 512
    block = pl.BlockSpec((rows, tile), lambda j: (0, j))
    return pl.pallas_call(
        gate_body,
        grid=(width // tile,),
        in_specs=[block, block, pl.BlockSpec((1, tile), lambda j: (0, j)), block],
        out_specs=[pl.BlockSpec((4, rows, tile), lambda j: (0, 0, j)), pl.BlockSpec((2, tile), lambda j: (0, j))],
        out_shape=[
            jax.ShapeDtypeStruct((4, rows, width), BF),
            jax.ShapeDtypeStruct((2, width), F32),
        ],
        compiler_params=LARGE,
        cost_estimate=pl.CostEstimate(flops=rows * width * 20, bytes_accessed=rows * width * 14, transcendentals=rows * width),
        name="gate",
    )(x_first, pre_act, gamma, cotangent)


def first_body(pre_ref, gamma_ref, cot_ref, out_ref):
    pre = pre_ref[...].astype(F32)
    out_ref[...] = (cot_ref[...].astype(F32) * (pre * jnp.tanh(gamma_ref[...] * pre))).astype(BF)


def first_step(pre_act, gamma, cotangent):
    rows, width = pre_act.shape
    tile = 512
    block = pl.BlockSpec((rows, tile), lambda j: (0, j))
    return pl.pallas_call(
        first_body,
        grid=(width // tile,),
        in_specs=[block, pl.BlockSpec((1, tile), lambda j: (0, j)), block],
        out_specs=block,
        out_shape=jax.ShapeDtypeStruct((rows, width), BF),
        compiler_params=LARGE,
        cost_estimate=BRIEF,
        name="first",
    )(pre_act, gamma, cotangent)


def weight_body(here_ref, there_ref, same_ref, other_ref, out_ref, samples_ref, grid_ref, sems, more):
    owners, deep, rows = same_ref.shape
    c, t = lax.axis_index("c"), lax.axis_index("t")
    copies = []
    for s, ref in enumerate((here_ref, there_ref)):
        for k in range(4):
            place = pl.ds(pl.multiple_of((2 * k + (s ^ c)) * rows, rows), rows)
            copies.append(pltpu.make_async_copy(ref.at[k], samples_ref.at[place], sems.at[2 * k + s]))
            copies[-1].start()
    for p, ref in enumerate((same_ref, other_ref)):
        half = pl.ds(pl.multiple_of((p ^ t) * deep, deep), deep)
        for a in range(owners):
            target = grid_ref.at[half, a * rows : (a + 1) * rows]
            copies.append(pltpu.make_async_copy(ref.at[a], target, more.at[p * owners + a]))
            copies[-1].start()
    for copy in copies:
        copy.wait()
    tile = 512
    for j in range(out_ref.shape[1] // tile):
        part = jnp.dot(grid_ref[...], samples_ref[:, j * tile : (j + 1) * tile], preferred_element_type=F32)
        out_ref[:, j * tile : (j + 1) * tile] = part.astype(BF)


def weight_product(here, there, same, other):
    _, rows, width = here.shape
    owners, deep, _ = same.shape
    return pl.pallas_call(
        weight_body,
        in_specs=[ANY] * 4,
        out_specs=VMEM,
        out_shape=jax.ShapeDtypeStruct((2 * deep, width), BF),
        scratch_shapes=[
            pltpu.VMEM((owners * rows, width), BF),
            pltpu.VMEM((2 * deep, owners * rows), BF),
            pltpu.SemaphoreType.DMA((8,)),
            pltpu.SemaphoreType.DMA((16,)),
        ],
        compiler_params=PARAMS,
        cost_estimate=BRIEF,
        name="weight_product",
    )(here, there, same, other)


def layer_body(here_ref, there_ref, *refs):
    weights, (keep_ref, send_ref, samples_ref, grid_ref, sems, more) = refs[:4], refs[4:]
    _, rows, width = here_ref.shape
    short = weights[0].shape[0] // 2
    x, y, h, t = (lax.axis_index(name) for name in ("x", "y", "h", "t"))
    copies = []
    for k in range(4):
        owner = lax.rem(x + 4 - k, 4)
        for s, ref in enumerate((here_ref, there_ref)):
            target = samples_ref.at[(2 * k + s) * rows : (2 * k + s + 1) * rows]
            copies.append(pltpu.make_async_copy(ref.at[owner], target, sems.at[2 * k + s]))
            copies[-1].start()
    for k in range(4):
        place_y = lax.rem(y + 4 - k, 4)
        side = lax.rem(place_y // 2 + t, 2)
        for s in range(2):
            block = side * 4 + lax.rem(place_y, 2) * 2 + (s ^ h)
            place = pl.ds(pl.multiple_of(block * short, short), short)
            copies.append(
                pltpu.make_async_copy(weights[k].at[s * short : (s + 1) * short], grid_ref.at[place], more.at[2 * k + s])
            )
            copies[-1].start()
    for copy in copies:
        copy.wait()
    tall = 4 * short
    for j in range(4):
        part = lax.dot_general(
            grid_ref[...],
            samples_ref[2 * j * rows : 2 * (j + 1) * rows, :],
            (((1,), (1,)), ((), ())),
            preferred_element_type=F32,
        )
        for s in range(2):
            keep_ref[s, j] = part[:tall, s * rows : (s + 1) * rows]
            send_ref[s, j] = part[tall:, s * rows : (s + 1) * rows].astype(BF)


def layer_product(here, there, weights):
    _, rows, width = here.shape
    deep = 4 * weights[0].shape[0]
    return pl.pallas_call(
        layer_body,
        in_specs=[ANY] * 6,
        out_specs=[VMEM, VMEM],
        out_shape=[
            jax.ShapeDtypeStruct((2, 4, deep // 2, rows), F32),
            jax.ShapeDtypeStruct((2, 4, deep // 2, rows), BF),
        ],
        scratch_shapes=[
            pltpu.VMEM((8 * rows, width), BF),
            pltpu.VMEM((deep, width), BF),
            pltpu.SemaphoreType.DMA((8,)),
            pltpu.SemaphoreType.DMA((8,)),
        ],
        compiler_params=PARAMS,
        cost_estimate=BRIEF,
        name="layer_product",
    )(here, there, *weights)


def pair_body(keep_ref, came_ref, same_ref, swap_ref):
    same_ref[...] = (keep_ref[0] + came_ref[0].astype(F32)).astype(BF)
    swap_ref[...] = (keep_ref[1] + came_ref[1].astype(F32)).astype(BF)


def pair_sum(keep, came):
    shape = jax.ShapeDtypeStruct(keep.shape[1:], BF)
    return pl.pallas_call(
        pair_body,
        in_specs=[VMEM] * 2,
        out_specs=[VMEM] * 2,
        out_shape=[shape, shape],
        compiler_params=PARAMS,
        cost_estimate=BRIEF,
        name="pair_sum",
    )(keep, came)


def total_body(*refs):
    out_ref = refs[-1]
    for q, ref in enumerate(refs[:-1]):
        total = ref[0].astype(F32)
        for k in range(1, ref.shape[0]):
            total = total + ref[k].astype(F32)
        width = ref.shape[2]
        out_ref[:, q * width : (q + 1) * width] = total


def total_parts(parts):
    rows, width = parts[0].shape[1:]
    return pl.pallas_call(
        total_body,
        in_specs=[VMEM] * len(parts),
        out_specs=VMEM,
        out_shape=jax.ShapeDtypeStruct((rows, width * len(parts)), F32),
        compiler_params=PARAMS,
        cost_estimate=BRIEF,
        name="total",
    )(*parts)


def finish_body(*refs):
    parts, (cot_ref, out_ref, all_ref) = refs[:8], refs[8:]
    x, c = lax.axis_index("x"), lax.axis_index("c")
    blocks, owners, cols, rows = all_ref.shape
    for k in range(4):
        for s in range(2):
            owner = lax.rem(x + k, 4) * 2 + (c if s == 0 else 1 - c)
            for b in range(blocks):
                all_ref[b, owner] = parts[2 * k + s][b * cols : (b + 1) * cols, :].astype(F32)
    wide = owners * cols
    for b in range(blocks):
        total = all_ref[b].reshape(wide, rows).T
        span = slice(b * wide, (b + 1) * wide)
        out_ref[:, span] = (cot_ref[:, span].astype(F32) + total).astype(BF)


def finish(parts, cotangent, cols):
    tall, rows = parts[0].shape
    return pl.pallas_call(
        finish_body,
        in_specs=[VMEM] * 9,
        out_specs=VMEM,
        out_shape=jax.ShapeDtypeStruct(cotangent.shape, BF),
        scratch_shapes=[pltpu.VMEM((tall // cols, 8, cols, rows), F32)],
        compiler_params=PARAMS,
        cost_estimate=BRIEF,
        name="finish",
    )(*parts, cotangent)


def ahead(value, axis, size, steps):
    return lax.ppermute(value, axis, [(i, (i + steps) % size) for i in range(size)])


def swap(value, axis, size, bit):
    return lax.ppermute(value, axis, [(i, i ^ bit) for i in range(size)])


def shards(x_first, x_layer, pre_act, gamma, weight, cotangent):
    far, near = ("y", "h"), ("x", "c")
    n_near, n_far = 8, 8
    samples, half = x_first.shape
    cols = weight.shape[1]
    blocks = half // (n_near * cols)
    gamma = gamma[None, :]

    by_owner = x_layer.T.reshape(blocks, n_near, cols, samples).transpose(1, 0, 2, 3)
    by_owner = by_owner.reshape(n_near, blocks * cols, samples)
    same = lax.all_to_all(by_owner, near, 0, 0, tiled=True)
    other = swap(same, "t", 2, 1)

    weight_bf = weight.T.astype(BF)
    x_first, by_owner, weight_bf = lax.optimization_barrier((x_first, by_owner, weight_bf))
    weight_two = jnp.concatenate([weight_bf, swap(weight_bf, "h", 2, 1)], axis=0)
    weights = [weight_two] + [ahead(weight_two, "y", 4, k) for k in (1, 2, 3)]

    gpre, sums = gate_step(x_first, pre_act, gamma, cotangent)
    gpre, weights[0] = lax.optimization_barrier((gpre, weights[0]))
    here = lax.all_to_all(gpre, "x", 0, 0, tiled=True)
    for axis, size, bit in (("c", 2, 1), ("x", 4, 1), ("x", 4, 2)):
        sums = sums + swap(sums, axis, size, bit)

    here, weights, sums, other = lax.optimization_barrier((here, weights, sums, other))
    there = swap(here, "c", 2, 1)

    sums_one = sums + swap(sums, "y", 4, 1)
    keep, sent = layer_product(here, there, weights)
    here, keep, sums_one = lax.optimization_barrier((here, keep, sums_one))
    sums_two = sums_one + swap(sums_one, "y", 4, 2)
    part = weight_product(here, there, same, other)
    part, sums_two = lax.optimization_barrier((part, sums_two))
    weight_part = lax.all_to_all(part.reshape(n_far, cols, half), far, 0, 0, tiled=True)
    sums = sums_two + swap(sums_two, "h", 2, 1)
    keep, part, sums = lax.optimization_barrier((keep, part, sums))
    mine, passed = pair_sum(keep, swap(sent, "t", 2, 1))
    passed = swap(passed, "c", 2, 1)
    parts = [mine[0], passed[0]]
    for k in (1, 2, 3):
        both = jnp.stack([mine[k], passed[k]])
        both = ahead(both, "x", 4, -k)
        parts += [both[0], both[1]]
    grad_layer = finish(parts, cotangent, cols)
    grad_weight = total_parts([weight_part]).T
    pre_act, mine = lax.optimization_barrier((pre_act, mine))
    grad_first = first_step(pre_act, gamma, cotangent)

    return grad_first, grad_layer, grad_weight, sums[0], sums[1]


def solution(mesh):
    fine = Mesh(mesh.devices.reshape(2, 4, 2, 4, 2), ("t", "y", "h", "x", "c"))
    batch = ("y", "h", "x", "c")
    wide = P(batch, "t")
    return jax.shard_map(
        shards,
        mesh=fine,
        in_specs=(wide, wide, wide, P("t"), P("t", batch), wide),
        out_specs=(wide, wide, P("t", batch), P("t"), P("t")),
        check_vma=False,
    )
```

```python
import jax
import jax.numpy as jnp
from jax import lax
from jax.experimental import pallas as pl
from jax.experimental.pallas import tpu as pltpu
from jax.sharding import Mesh, PartitionSpec as P

BF = jnp.bfloat16
F32 = jnp.float32
PARAMS = pltpu.CompilerParams(vmem_limit_bytes=20 * 1024 * 1024)
LARGE = pltpu.CompilerParams(vmem_limit_bytes=60 * 1024 * 1024)
ANY = pl.BlockSpec(memory_space=pl.ANY)
VMEM = pl.BlockSpec(memory_space=pltpu.VMEM)
EXTRA = 128
BRIEF = pl.CostEstimate(flops=1000, bytes_accessed=1000, transcendentals=0)


def gate_body(first_ref, pre_ref, gamma_ref, cot_ref, gpre_ref, *scratch):
    bufs, sems = scratch[:3], scratch[3]
    rows, width = first_ref.shape
    lanes = gpre_ref.shape[1] - width
    tile = 512
    copies = []
    for j in range(width // tile):
        span = slice(j * tile, (j + 1) * tile)
        for n, ref in enumerate((first_ref, pre_ref, cot_ref)):
            copies.append(pltpu.make_async_copy(ref.at[:, span], bufs[n].at[:, span], sems.at[3 * j + n]))
            copies[-1].start()
    gpre_ref[96:, width:] = jnp.zeros((rows - 96, lanes), BF)
    for j in range(width // tile):
        span = slice(j * tile, (j + 1) * tile)
        for copy in copies[3 * j : 3 * j + 3]:
            copy.wait()
        gamma = gamma_ref[:, span]
        pre = bufs[1][:, span].astype(F32)
        gate = jnp.tanh(gamma * pre)
        hidden = bufs[2][:, span].astype(F32) * bufs[0][:, span].astype(F32)
        turn = pre * (1.0 - gate * gate)
        gpre = (hidden * (gate + gamma * turn)).astype(BF)
        gpre_ref[:, span] = gpre
        sums = jnp.sum(gpre.astype(F32), axis=0, keepdims=True), jnp.sum(hidden * pre * turn, axis=0, keepdims=True)
        for n, rest in enumerate(sums):
            for p in range(3):
                piece = rest.astype(BF)
                rest = rest - piece.astype(F32)
                for i in range(tile // lanes):
                    row = 48 * n + 16 * p + j * (tile // lanes) + i
                    gpre_ref[row : row + 1, width:] = piece[:, i * lanes : (i + 1) * lanes]


def gate_step(x_first, pre_act, gamma, cotangent):
    rows, width = x_first.shape
    buf = pltpu.VMEM((rows, width), BF)
    return pl.pallas_call(
        gate_body,
        in_specs=[ANY, ANY, VMEM, ANY],
        out_specs=VMEM,
        out_shape=jax.ShapeDtypeStruct((rows, width + EXTRA), BF),
        scratch_shapes=[buf, buf, buf, pltpu.SemaphoreType.DMA((3 * width // 512,))],
        compiler_params=LARGE,
        cost_estimate=pl.CostEstimate(flops=rows * width * 20, bytes_accessed=rows * width * 8, transcendentals=rows * width),
        name="gate",
    )(x_first, pre_act, gamma, cotangent)


def first_body(pre_ref, gamma_ref, cot_ref, out_ref):
    pre = pre_ref[...].astype(F32)
    out_ref[...] = (cot_ref[...].astype(F32) * (pre * jnp.tanh(gamma_ref[...] * pre))).astype(BF)


def first_step(pre_act, gamma, cotangent):
    rows, width = pre_act.shape
    tile = 512
    block = pl.BlockSpec((rows, tile), lambda j: (0, j))
    return pl.pallas_call(
        first_body,
        grid=(width // tile,),
        in_specs=[block, pl.BlockSpec((1, tile), lambda j: (0, j)), block],
        out_specs=block,
        out_shape=jax.ShapeDtypeStruct((rows, width), BF),
        compiler_params=LARGE,
        cost_estimate=BRIEF,
        name="first",
    )(pre_act, gamma, cotangent)


LAY = ((0, 0, 2), (1, 0, 2), (3, 0, 2), (2, 0, 1), (2, 1, 1))


def ring_gather(value, axis):
    rows = value.shape[0]
    left, right = ahead(value, axis, 4, 1), ahead(value, axis, 4, 3)
    far_low = ahead(left[: rows // 2], axis, 4, 1)
    far_high = ahead(right[rows // 2 :], axis, 4, 3)
    return [value, left, right, far_low, far_high]


def load_samples(pieces, samples_ref, sems, place_of):
    rows = pieces[0].shape[0]
    width = samples_ref.shape[1]
    copies = []
    for n, (back, start, size) in enumerate(LAY):
        for s in range(2):
            place = pl.ds(place_of(back, s) * rows + start * rows // 2, size * rows // 2)
            source = pieces[2 * n + s].at[:, :width]
            copies.append(pltpu.make_async_copy(source, samples_ref.at[place], sems.at[2 * n + s]))
            copies[-1].start()
    return copies


def weight_body(*refs):
    pieces, (cols_ref, out_ref, samples_ref, grid_ref, sems, more) = refs[:10], refs[10:]
    pairs, owners, deep, rows = cols_ref.shape
    x, c = lax.axis_index("x"), lax.axis_index("c")
    copies = load_samples(pieces, samples_ref, sems, lambda back, s: lax.rem(x + 4 - back, 4) * 2 + (s ^ c))
    for p in range(pairs):
        for a in range(owners):
            target = grid_ref.at[p * deep : (p + 1) * deep, a * rows : (a + 1) * rows]
            copies.append(pltpu.make_async_copy(cols_ref.at[p, a], target, more.at[p * owners + a]))
            copies[-1].start()
    for copy in copies:
        copy.wait()
    width = out_ref.shape[1] - EXTRA
    total = samples_ref[:rows, width:].astype(F32)
    for a in range(1, owners):
        total = total + samples_ref[a * rows : (a + 1) * rows, width:].astype(F32)
    for n in range(2):
        value = total[48 * n : 48 * n + 16] + total[48 * n + 16 : 48 * n + 32] + total[48 * n + 32 : 48 * n + 48]
        high = value.astype(BF)
        low = (value - high.astype(F32)).astype(BF)
        for b in range(pairs * deep // 64):
            out_ref[64 * b + 32 * n : 64 * b + 32 * n + 16, width:] = high
            out_ref[64 * b + 32 * n + 16 : 64 * b + 32 * n + 32, width:] = low
    tile = 512
    for j in range(width // tile):
        part = jnp.dot(grid_ref[...], samples_ref[:, j * tile : (j + 1) * tile], preferred_element_type=F32)
        out_ref[:, j * tile : (j + 1) * tile] = part.astype(BF)


def weight_product(pieces, cols):
    rows, width = pieces[0].shape
    pairs, owners, deep, _ = cols.shape
    return pl.pallas_call(
        weight_body,
        in_specs=[ANY] * 11,
        out_specs=VMEM,
        out_shape=jax.ShapeDtypeStruct((pairs * deep, width), BF),
        scratch_shapes=[
            pltpu.VMEM((owners * rows, width), BF),
            pltpu.VMEM((pairs * deep, owners * rows), BF),
            pltpu.SemaphoreType.DMA((10,)),
            pltpu.SemaphoreType.DMA((16,)),
        ],
        compiler_params=PARAMS,
        cost_estimate=BRIEF,
        name="weight_product",
    )(*pieces, cols)


def layer_body(*refs):
    pieces, weights = refs[:10], refs[10:15]
    keep_ref, send_ref, samples_ref, grid_ref, sems, more = refs[15:]
    rows = pieces[0].shape[0]
    short = weights[0].shape[0] // 2
    y, h, t = lax.axis_index("y"), lax.axis_index("h"), lax.axis_index("t")
    copies = load_samples(pieces, samples_ref, sems, lambda back, s: 2 * back + s)
    for n, (back, start, size) in enumerate(LAY):
        place_y = lax.rem(y + 4 - back, 4)
        side = lax.rem(place_y // 2 + t, 2)
        for s in range(size):
            block = side * 4 + lax.rem(place_y, 2) * 2 + ((start + s) ^ h)
            place = pl.ds(pl.multiple_of(block * short, short), short)
            copies.append(
                pltpu.make_async_copy(weights[n].at[s * short : (s + 1) * short], grid_ref.at[place], more.at[2 * n + s])
            )
            copies[-1].start()
    for copy in copies:
        copy.wait()
    tall = 4 * short
    for j in range(4):
        part = lax.dot_general(
            grid_ref[...],
            samples_ref[2 * j * rows : 2 * (j + 1) * rows, :],
            (((1,), (1,)), ((), ())),
            preferred_element_type=F32,
        )
        for s in range(2):
            keep_ref[s, j] = part[:tall, s * rows : (s + 1) * rows]
            send_ref[s, j] = part[tall:, s * rows : (s + 1) * rows].astype(BF)


def layer_product(pieces, weights):
    rows = pieces[0].shape[0]
    width = weights[0].shape[1]
    deep = 4 * weights[0].shape[0]
    return pl.pallas_call(
        layer_body,
        in_specs=[ANY] * 15,
        out_specs=[VMEM, VMEM],
        out_shape=[
            jax.ShapeDtypeStruct((2, 4, deep // 2, rows), F32),
            jax.ShapeDtypeStruct((2, 4, deep // 2, rows), BF),
        ],
        scratch_shapes=[
            pltpu.VMEM((8 * rows, width), BF),
            pltpu.VMEM((deep, width), BF),
            pltpu.SemaphoreType.DMA((10,)),
            pltpu.SemaphoreType.DMA((10,)),
        ],
        compiler_params=PARAMS,
        cost_estimate=BRIEF,
        name="layer_product",
    )(*pieces, *weights)


def pair_body(keep_ref, came_ref, same_ref, swap_ref):
    same_ref[...] = (keep_ref[0] + came_ref[0].astype(F32)).astype(BF)
    swap_ref[...] = (keep_ref[1] + came_ref[1].astype(F32)).astype(BF)


def pair_sum(keep, came):
    shape = jax.ShapeDtypeStruct(keep.shape[1:], BF)
    return pl.pallas_call(
        pair_body,
        in_specs=[VMEM] * 2,
        out_specs=[VMEM] * 2,
        out_shape=[shape, shape],
        compiler_params=PARAMS,
        cost_estimate=BRIEF,
        name="pair_sum",
    )(keep, came)


def total_body(parts_ref, out_ref, sums_ref):
    width = out_ref.shape[1]
    total = parts_ref[0].astype(F32)
    for k in range(1, parts_ref.shape[0]):
        total = total + parts_ref[k].astype(F32)
    out_ref[...] = total[:, :width]
    for n in range(2):
        sums_ref[n] = total[32 * n : 32 * n + 16, width:] + total[32 * n + 16 : 32 * n + 32, width:]


def total_parts(parts):
    rows, width = parts.shape[1:]
    return pl.pallas_call(
        total_body,
        in_specs=[VMEM],
        out_specs=[VMEM, VMEM],
        out_shape=[
            jax.ShapeDtypeStruct((rows, width - EXTRA), F32),
            jax.ShapeDtypeStruct((2, 16, EXTRA), F32),
        ],
        compiler_params=PARAMS,
        cost_estimate=BRIEF,
        name="total",
    )(parts)


def finish_body(*refs):
    parts, (cot_ref, out_ref, all_ref) = refs[:8], refs[8:]
    x, c = lax.axis_index("x"), lax.axis_index("c")
    blocks, owners, cols, rows = all_ref.shape
    for k in range(4):
        for s in range(2):
            owner = lax.rem(x + k, 4) * 2 + (c if s == 0 else 1 - c)
            for b in range(blocks):
                all_ref[b, owner] = parts[2 * k + s][b * cols : (b + 1) * cols, :].astype(F32)
    wide = owners * cols
    for b in range(blocks):
        total = all_ref[b].reshape(wide, rows).T
        span = slice(b * wide, (b + 1) * wide)
        out_ref[:, span] = (cot_ref[:, span].astype(F32) + total).astype(BF)


def finish(parts, cotangent, cols):
    tall, rows = parts[0].shape
    return pl.pallas_call(
        finish_body,
        in_specs=[VMEM] * 9,
        out_specs=VMEM,
        out_shape=jax.ShapeDtypeStruct(cotangent.shape, BF),
        scratch_shapes=[pltpu.VMEM((tall // cols, 8, cols, rows), F32)],
        compiler_params=PARAMS,
        cost_estimate=BRIEF,
        name="finish",
    )(*parts, cotangent)


def ahead(value, axis, size, steps):
    return lax.ppermute(value, axis, [(i, (i + steps) % size) for i in range(size)])


def swap(value, axis, size, bit):
    return lax.ppermute(value, axis, [(i, i ^ bit) for i in range(size)])


def ring_gather(value, axis):
    rows = value.shape[0]
    left, right = ahead(value, axis, 4, 1), ahead(value, axis, 4, 3)
    far_low = ahead(left[: rows // 2], axis, 4, 1)
    far_high = ahead(right[rows // 2 :], axis, 4, 3)
    return [value, left, right, far_low, far_high]


def shards(x_first, x_layer, pre_act, gamma, weight, cotangent):
    far, both = ("y", "h"), ("t", "x", "c")
    n_near, n_far, pairs = 8, 8, 2
    samples, half = x_first.shape
    cols = weight.shape[1]
    blocks = half // (n_near * cols)
    gamma = gamma[None, :]

    gpre = gate_step(x_first, pre_act, gamma, cotangent)
    own = ring_gather(gpre, "x")

    by_owner = x_layer.T.reshape(blocks, n_near, cols, samples).transpose(1, 0, 2, 3)
    by_owner = by_owner.reshape(n_near, blocks * cols, samples)
    sent = jnp.concatenate([by_owner] * pairs, axis=0)
    came = lax.all_to_all(sent, both, 0, 0, tiled=True).reshape(pairs, n_near, blocks * cols, samples)

    weight_bf = weight.T.astype(BF)
    weight_two = jnp.concatenate([weight_bf, swap(weight_bf, "h", 2, 1)], axis=0)
    weights = ring_gather(weight_two, "y")

    own, weights, came = lax.optimization_barrier((own, weights, came))
    pieces = []
    for piece in own:
        pieces += [piece, swap(piece, "c", 2, 1)]

    keep, sent = layer_product(pieces, weights)
    pieces, keep = lax.optimization_barrier((pieces, keep))
    part = weight_product(pieces, came)
    weight_part = lax.all_to_all(part.reshape(n_far, cols, half + EXTRA), far, 0, 0, tiled=True)
    keep, part = lax.optimization_barrier((keep, part))
    mine, passed = pair_sum(keep, swap(sent, "t", 2, 1))
    passed = swap(passed, "c", 2, 1)
    parts = [mine[0], passed[0]]
    for k in (1, 2, 3):
        both = jnp.stack([mine[k], passed[k]])
        both = ahead(both, "x", 4, -k)
        parts += [both[0], both[1]]
    grad_layer = finish(parts, cotangent, cols)
    grad_weight, sums = total_parts(weight_part)
    pre_act, mine = lax.optimization_barrier((pre_act, mine))
    grad_first = first_step(pre_act, gamma, cotangent)

    return grad_first, grad_layer, grad_weight.T, sums[0].reshape(half), sums[1].reshape(half)


def solution(mesh):
    fine = Mesh(mesh.devices.reshape(2, 4, 2, 4, 2), ("t", "y", "h", "x", "c"))
    batch = ("y", "h", "x", "c")
    wide = P(batch, "t")
    return jax.shard_map(
        shards,
        mesh=fine,
        in_specs=(wide, wide, wide, P("t"), P("t", batch), wide),
        out_specs=(wide, wide, P("t", batch), P("t"), P("t")),
        check_vma=False,
    )
```

```python
import functools
import jax
import jax.numpy as jnp
from jax import lax
from jax.experimental import pallas as pl
from jax.experimental.pallas import tpu as pltpu
from jax.sharding import Mesh, PartitionSpec as P

BF = jnp.bfloat16
F32 = jnp.float32
PARAMS = pltpu.CompilerParams(vmem_limit_bytes=20 * 1024 * 1024)
LARGE = pltpu.CompilerParams(vmem_limit_bytes=60 * 1024 * 1024)
ANY = pl.BlockSpec(memory_space=pl.ANY)
VMEM = pl.BlockSpec(memory_space=pltpu.VMEM)
EXTRA = 128
BRIEF = pl.CostEstimate(flops=1000, bytes_accessed=1000, transcendentals=0)


def gate_body(first_ref, pre_ref, gamma_ref, cot_ref, gpre_ref, *scratch):
    bufs, sems = scratch[:3], scratch[3]
    rows, width = first_ref.shape
    lanes = gpre_ref.shape[1] - width
    tile = 512
    copies = []
    for j in range(width // tile):
        span = slice(j * tile, (j + 1) * tile)
        for n, ref in enumerate((first_ref, pre_ref, cot_ref)):
            copies.append(pltpu.make_async_copy(ref.at[:, span], bufs[n].at[:, span], sems.at[3 * j + n]))
            copies[-1].start()
    gpre_ref[96:, width:] = jnp.zeros((rows - 96, lanes), BF)
    for j in range(width // tile):
        span = slice(j * tile, (j + 1) * tile)
        for copy in copies[3 * j : 3 * j + 3]:
            copy.wait()
        gamma = gamma_ref[:, span]
        pre = bufs[1][:, span].astype(F32)
        gate = jnp.tanh(gamma * pre)
        hidden = bufs[2][:, span].astype(F32) * bufs[0][:, span].astype(F32)
        turn = pre * (1.0 - gate * gate)
        gpre = (hidden * (gate + gamma * turn)).astype(BF)
        gpre_ref[:, span] = gpre
        sums = jnp.sum(gpre.astype(F32), axis=0, keepdims=True), jnp.sum(hidden * pre * turn, axis=0, keepdims=True)
        for n, rest in enumerate(sums):
            for p in range(3):
                piece = rest.astype(BF)
                rest = rest - piece.astype(F32)
                for i in range(tile // lanes):
                    row = 48 * n + 16 * p + j * (tile // lanes) + i
                    gpre_ref[row : row + 1, width:] = piece[:, i * lanes : (i + 1) * lanes]


def gate_step(x_first, pre_act, gamma, cotangent):
    rows, width = x_first.shape
    buf = pltpu.VMEM((rows, width), BF)
    return pl.pallas_call(
        gate_body,
        in_specs=[ANY, ANY, VMEM, ANY],
        out_specs=VMEM,
        out_shape=jax.ShapeDtypeStruct((rows, width + EXTRA), BF),
        scratch_shapes=[buf, buf, buf, pltpu.SemaphoreType.DMA((3 * width // 512,))],
        compiler_params=LARGE,
        cost_estimate=pl.CostEstimate(flops=rows * width * 20, bytes_accessed=rows * width * 8, transcendentals=rows * width),
        name="gate",
    )(x_first, pre_act, gamma, cotangent)


def first_body(pre_ref, gamma_ref, cot_ref, out_ref):
    pre = pre_ref[...].astype(F32)
    out_ref[...] = (cot_ref[...].astype(F32) * (pre * jnp.tanh(gamma_ref[...] * pre))).astype(BF)


def first_step(pre_act, gamma, cotangent):
    rows, width = pre_act.shape
    tile = 512
    block = pl.BlockSpec((rows, tile), lambda j: (0, j))
    return pl.pallas_call(
        first_body,
        grid=(width // tile,),
        in_specs=[block, pl.BlockSpec((1, tile), lambda j: (0, j)), block],
        out_specs=block,
        out_shape=jax.ShapeDtypeStruct((rows, width), BF),
        compiler_params=LARGE,
        cost_estimate=BRIEF,
        name="first",
    )(pre_act, gamma, cotangent)


LAY = ((0, 0, 2), (1, 0, 2), (3, 0, 2), (2, 0, 1), (2, 1, 1))


def sample_rows(pieces, back, s, span):
    return [pieces[2 * n + s][:, span] for n, place in enumerate(LAY) if place[0] == back]


def weight_body(*refs):
    pieces, cols_ref, out_ref = refs[:10], refs[10], refs[11]
    pairs, owners, deep, rows = cols_ref.shape
    width = out_ref.shape[1] - EXTRA
    x, c = lax.axis_index("x"), lax.axis_index("c")
    order = [(back, s) for back in range(4) for s in range(2)]
    total = 0.0
    for back, s in order:
        total = total + jnp.concatenate(sample_rows(pieces, back, s, slice(width, width + EXTRA))).astype(F32)
    for n in range(2):
        value = total[48 * n : 48 * n + 16] + total[48 * n + 16 : 48 * n + 32] + total[48 * n + 32 : 48 * n + 48]
        high = value.astype(BF)
        low = (value - high.astype(F32)).astype(BF)
        for b in range(pairs * deep // 64):
            out_ref[64 * b + 32 * n : 64 * b + 32 * n + 16, width:] = high
            out_ref[64 * b + 32 * n + 16 : 64 * b + 32 * n + 32, width:] = low
    tile = 512
    for p in range(pairs):
        owner = [lax.rem(x + 4 - back, 4) * 2 + (s ^ c) for back, s in order]
        grid = jnp.concatenate([cols_ref[p, a] for a in owner], axis=1)
        for j in range(width // tile):
            span = slice(j * tile, (j + 1) * tile)
            samples = jnp.concatenate(sum((sample_rows(pieces, back, s, span) for back, s in order), []))
            part = jnp.dot(grid, samples, preferred_element_type=F32)
            out_ref[p * deep : (p + 1) * deep, span] = part.astype(BF)


def weight_product(pieces, cols):
    width = pieces[0].shape[1]
    pairs, _, deep, _ = cols.shape
    return pl.pallas_call(
        weight_body,
        in_specs=[VMEM] * 11,
        out_specs=VMEM,
        out_shape=jax.ShapeDtypeStruct((pairs * deep, width), BF),
        compiler_params=PARAMS,
        cost_estimate=BRIEF,
        name="weight_product",
    )(*pieces, cols)


def layer_body(half, *refs):
    pieces, weights, (out_ref, grid_ref, sems) = refs[:10], refs[10:15], refs[15:]
    tall = grid_ref.shape[0] // 2
    short = tall // 4
    y, h, t = lax.axis_index("y"), lax.axis_index("h"), lax.axis_index("t")
    copies = []
    for n, (back, start, size) in enumerate(LAY):
        place_y = lax.rem(y + 4 - back, 4)
        side = lax.rem(place_y // 2 + t, 2)
        for s in range(size):
            block = side * 4 + lax.rem(place_y, 2) * 2 + ((start + s) ^ h)
            place = pl.ds(pl.multiple_of(block * short, short), short)
            copies.append(
                pltpu.make_async_copy(weights[n].at[s * short : (s + 1) * short], grid_ref.at[place], sems.at[2 * n + s])
            )
            copies[-1].start()
    for copy in copies:
        copy.wait()
    width = grid_ref.shape[1]
    rows = out_ref.shape[3]
    for back in range(4):
        samples = jnp.concatenate(sum((sample_rows(pieces, back, s, slice(0, width)) for s in range(2)), []))
        part = lax.dot_general(
            grid_ref[half * tall : (half + 1) * tall],
            samples,
            (((1,), (1,)), ((), ())),
            preferred_element_type=F32,
        )
        for s in range(2):
            out_ref[s, back] = part[:, s * rows : (s + 1) * rows].astype(out_ref.dtype)


def layer_product(pieces, weights, half, kind):
    width = weights[0].shape[1]
    deep = 4 * weights[0].shape[0]
    return pl.pallas_call(
        functools.partial(layer_body, half),
        in_specs=[VMEM] * 10 + [ANY] * 5,
        out_specs=VMEM,
        out_shape=jax.ShapeDtypeStruct((2, 4, deep // 2, pieces[0].shape[0]), kind),
        scratch_shapes=[pltpu.VMEM((deep, width), BF), pltpu.SemaphoreType.DMA((10,))],
        compiler_params=PARAMS,
        cost_estimate=BRIEF,
        name="layer_send" if half else "layer_keep",
    )(*pieces, *weights)


def pair_body(keep_ref, came_ref, same_ref, swap_ref):
    same_ref[...] = (keep_ref[0] + came_ref[0].astype(F32)).astype(BF)
    swap_ref[...] = (keep_ref[1] + came_ref[1].astype(F32)).astype(BF)


def pair_sum(keep, came):
    shape = jax.ShapeDtypeStruct(keep.shape[1:], BF)
    return pl.pallas_call(
        pair_body,
        in_specs=[VMEM] * 2,
        out_specs=[VMEM] * 2,
        out_shape=[shape, shape],
        compiler_params=PARAMS,
        cost_estimate=BRIEF,
        name="pair_sum",
    )(keep, came)


def total_body(parts_ref, out_ref, sums_ref):
    width = out_ref.shape[1]
    total = parts_ref[0].astype(F32)
    for k in range(1, parts_ref.shape[0]):
        total = total + parts_ref[k].astype(F32)
    out_ref[...] = total[:, :width]
    for n in range(2):
        sums_ref[n] = total[32 * n : 32 * n + 16, width:] + total[32 * n + 16 : 32 * n + 32, width:]


def total_parts(parts):
    rows, width = parts.shape[1:]
    return pl.pallas_call(
        total_body,
        in_specs=[VMEM],
        out_specs=[VMEM, VMEM],
        out_shape=[
            jax.ShapeDtypeStruct((rows, width - EXTRA), F32),
            jax.ShapeDtypeStruct((2, 16, EXTRA), F32),
        ],
        compiler_params=PARAMS,
        cost_estimate=BRIEF,
        name="total",
    )(parts)


def finish_body(*refs):
    parts, (cot_ref, out_ref, all_ref) = refs[:8], refs[8:]
    x, c = lax.axis_index("x"), lax.axis_index("c")
    blocks, owners, cols, rows = all_ref.shape
    for k in range(4):
        for s in range(2):
            owner = lax.rem(x + k, 4) * 2 + (c if s == 0 else 1 - c)
            for b in range(blocks):
                all_ref[b, owner] = parts[2 * k + s][b * cols : (b + 1) * cols, :].astype(F32)
    wide = owners * cols
    for b in range(blocks):
        total = all_ref[b].reshape(wide, rows).T
        span = slice(b * wide, (b + 1) * wide)
        out_ref[:, span] = (cot_ref[:, span].astype(F32) + total).astype(BF)


def finish(parts, cotangent, cols):
    tall, rows = parts[0].shape
    return pl.pallas_call(
        finish_body,
        in_specs=[VMEM] * 9,
        out_specs=VMEM,
        out_shape=jax.ShapeDtypeStruct(cotangent.shape, BF),
        scratch_shapes=[pltpu.VMEM((tall // cols, 8, cols, rows), F32)],
        compiler_params=PARAMS,
        cost_estimate=BRIEF,
        name="finish",
    )(*parts, cotangent)


def ahead(value, axis, size, steps):
    return lax.ppermute(value, axis, [(i, (i + steps) % size) for i in range(size)])


def swap(value, axis, size, bit):
    return lax.ppermute(value, axis, [(i, i ^ bit) for i in range(size)])


def ring_gather(value, axis):
    rows = value.shape[0]
    left, right = ahead(value, axis, 4, 1), ahead(value, axis, 4, 3)
    far_low = ahead(left[: rows // 2], axis, 4, 1)
    far_high = ahead(right[rows // 2 :], axis, 4, 3)
    return [value, left, right, far_low, far_high]


def shards(x_first, x_layer, pre_act, gamma, weight, cotangent):
    far, both = ("y", "h"), ("t", "x", "c")
    n_near, n_far, pairs = 8, 8, 2
    samples, half = x_first.shape
    cols = weight.shape[1]
    blocks = half // (n_near * cols)
    gamma = gamma[None, :]

    gpre = gate_step(x_first, pre_act, gamma, cotangent)
    own = ring_gather(gpre, "x")

    weight_bf = weight.T.astype(BF)
    weight_two = jnp.concatenate([weight_bf, swap(weight_bf, "h", 2, 1)], axis=0)
    x_layer, weight_two = lax.optimization_barrier((x_layer, weight_two))
    weights = ring_gather(weight_two, "y")

    by_owner = x_layer.T.reshape(blocks, n_near, cols, samples).transpose(1, 0, 2, 3)
    by_owner = by_owner.reshape(n_near, blocks * cols, samples)
    sent = jnp.concatenate([by_owner] * pairs, axis=0)
    came = lax.all_to_all(sent, both, 0, 0, tiled=True).reshape(pairs, n_near, blocks * cols, samples)
    grad_first = first_step(pre_act, gamma, cotangent)

    pieces = []
    for piece in own[:3]:
        pieces += [piece, swap(piece, "c", 2, 1)]
    pieces, late, weights, came, grad_first = lax.optimization_barrier((pieces, own[3:], weights, came, grad_first))
    for piece in late:
        pieces += [piece, swap(piece, "c", 2, 1)]

    sent = layer_product(pieces, weights, 1, BF)
    pieces, sent = lax.optimization_barrier((pieces, sent))
    part = weight_product(pieces, came)
    weight_part = lax.all_to_all(part.reshape(n_far, cols, half + EXTRA), far, 0, 0, tiled=True)
    weights, part = lax.optimization_barrier((weights, part))
    keep = layer_product(pieces, weights, 0, F32)
    mine, passed = pair_sum(keep, swap(sent, "t", 2, 1))
    passed = swap(passed, "c", 2, 1)
    parts = [mine[0], passed[0]]
    for k in (1, 2, 3):
        both = jnp.stack([mine[k], passed[k]])
        both = ahead(both, "x", 4, -k)
        parts += [both[0], both[1]]
    grad_layer = finish(parts, cotangent, cols)
    grad_weight, sums = total_parts(weight_part)
    return grad_first, grad_layer, grad_weight.T, sums[0].reshape(half), sums[1].reshape(half)


def solution(mesh):
    fine = Mesh(mesh.devices.reshape(2, 4, 2, 4, 2), ("t", "y", "h", "x", "c"))
    batch = ("y", "h", "x", "c")
    wide = P(batch, "t")
    return jax.shard_map(
        shards,
        mesh=fine,
        in_specs=(wide, wide, wide, P("t"), P("t", batch), wide),
        out_specs=(wide, wide, P("t", batch), P("t"), P("t")),
        check_vma=False,
    )
```

```python
import functools
import jax
import jax.numpy as jnp
from jax import lax
from jax.experimental import pallas as pl
from jax.experimental.pallas import tpu as pltpu
from jax.sharding import Mesh, PartitionSpec as P

BF = jnp.bfloat16
F32 = jnp.float32
PARAMS = pltpu.CompilerParams(vmem_limit_bytes=20 * 1024 * 1024)
LARGE = pltpu.CompilerParams(vmem_limit_bytes=60 * 1024 * 1024)
ANY = pl.BlockSpec(memory_space=pl.ANY)
VMEM = pl.BlockSpec(memory_space=pltpu.VMEM)
HBM = pl.BlockSpec(memory_space=pltpu.HBM)
EXTRA = 128
BRIEF = pl.CostEstimate(flops=1000, bytes_accessed=1000, transcendentals=0)


def gate_body(first_ref, pre_ref, gamma_ref, cot_ref, gpre_ref, *scratch):
    bufs, sems = scratch[:3], scratch[3]
    rows, width = first_ref.shape
    lanes = gpre_ref.shape[1] - width
    tile = 512
    copies = []
    for j in range(width // tile):
        span = slice(j * tile, (j + 1) * tile)
        for n, ref in enumerate((first_ref, pre_ref, cot_ref)):
            copies.append(pltpu.make_async_copy(ref.at[:, span], bufs[n].at[:, span], sems.at[3 * j + n]))
            copies[-1].start()
    gpre_ref[96:, width:] = jnp.zeros((rows - 96, lanes), BF)
    for j in range(width // tile):
        span = slice(j * tile, (j + 1) * tile)
        for copy in copies[3 * j : 3 * j + 3]:
            copy.wait()
        gamma = gamma_ref[:, span]
        pre = bufs[1][:, span].astype(F32)
        gate = jnp.tanh(gamma * pre)
        hidden = bufs[2][:, span].astype(F32) * bufs[0][:, span].astype(F32)
        turn = pre * (1.0 - gate * gate)
        gpre = (hidden * (gate + gamma * turn)).astype(BF)
        gpre_ref[:, span] = gpre
        sums = jnp.sum(gpre.astype(F32), axis=0, keepdims=True), jnp.sum(hidden * pre * turn, axis=0, keepdims=True)
        for n, rest in enumerate(sums):
            for p in range(3):
                piece = rest.astype(BF)
                rest = rest - piece.astype(F32)
                for i in range(tile // lanes):
                    row = 48 * n + 16 * p + j * (tile // lanes) + i
                    gpre_ref[row : row + 1, width:] = piece[:, i * lanes : (i + 1) * lanes]


def gate_step(x_first, pre_act, gamma, cotangent):
    rows, width = x_first.shape
    buf = pltpu.VMEM((rows, width), BF)
    return pl.pallas_call(
        gate_body,
        in_specs=[ANY, ANY, VMEM, ANY],
        out_specs=VMEM,
        out_shape=jax.ShapeDtypeStruct((rows, width + EXTRA), BF),
        scratch_shapes=[buf, buf, buf, pltpu.SemaphoreType.DMA((3 * width // 512,))],
        compiler_params=LARGE,
        cost_estimate=pl.CostEstimate(flops=rows * width * 20, bytes_accessed=rows * width * 8, transcendentals=rows * width),
        name="gate",
    )(x_first, pre_act, gamma, cotangent)


def first_body(pre_ref, gamma_ref, cot_ref, out_ref):
    pre = pre_ref[...].astype(F32)
    out_ref[...] = (cot_ref[...].astype(F32) * (pre * jnp.tanh(gamma_ref[...] * pre))).astype(BF)


def first_step(pre_act, gamma, cotangent):
    rows, width = pre_act.shape
    tile = 512
    block = pl.BlockSpec((rows, tile), lambda j: (0, j))
    return pl.pallas_call(
        first_body,
        grid=(width // tile,),
        in_specs=[block, pl.BlockSpec((1, tile), lambda j: (0, j)), block],
        out_specs=block,
        out_shape=jax.ShapeDtypeStruct((rows, width), BF),
        compiler_params=LARGE,
        cost_estimate=BRIEF,
        name="first",
    )(pre_act, gamma, cotangent)


LAY = ((0, 0, 2), (1, 0, 2), (3, 0, 2), (2, 0, 1), (2, 1, 1))


def sample_rows(pieces, back, s, span):
    return [pieces[2 * n + s][:, span] for n, place in enumerate(LAY) if place[0] == back]


def weight_body(*refs):
    pieces, cols_ref, result_ref, out_ref, sems = refs[:10], *refs[10:]
    pairs, owners, deep, rows = cols_ref.shape
    width = out_ref.shape[1] - EXTRA
    x, c = lax.axis_index("x"), lax.axis_index("c")
    order = [(back, s) for back in range(4) for s in range(2)]
    total = 0.0
    for back, s in order:
        total = total + jnp.concatenate(sample_rows(pieces, back, s, slice(width, width + EXTRA))).astype(F32)
    for n in range(2):
        value = total[48 * n : 48 * n + 16] + total[48 * n + 16 : 48 * n + 32] + total[48 * n + 32 : 48 * n + 48]
        high = value.astype(BF)
        low = (value - high.astype(F32)).astype(BF)
        for b in range(pairs * deep // 64):
            out_ref[64 * b + 32 * n : 64 * b + 32 * n + 16, width:] = high
            out_ref[64 * b + 32 * n + 16 : 64 * b + 32 * n + 32, width:] = low
    tile = 512
    sends = [pltpu.make_async_copy(out_ref.at[:, width:], result_ref.at[:, width:], sems.at[0])]
    sends[0].start()
    for p in range(pairs):
        owner = [lax.rem(x + 4 - back, 4) * 2 + (s ^ c) for back, s in order]
        grid = jnp.concatenate([cols_ref[p, a] for a in owner], axis=1)
        for j in range(width // tile):
            span = slice(j * tile, (j + 1) * tile)
            samples = jnp.concatenate(sum((sample_rows(pieces, back, s, span) for back, s in order), []))
            part = jnp.dot(grid, samples, preferred_element_type=F32)
            block = slice(p * deep, (p + 1) * deep)
            out_ref[block, span] = part.astype(BF)
            sends.append(
                pltpu.make_async_copy(out_ref.at[block, span], result_ref.at[block, span], sems.at[len(sends)])
            )
            sends[-1].start()
    for send in sends:
        send.wait()


def weight_product(pieces, cols):
    width = pieces[0].shape[1]
    pairs, _, deep, _ = cols.shape
    return pl.pallas_call(
        weight_body,
        in_specs=[VMEM] * 11,
        out_specs=HBM,
        out_shape=jax.ShapeDtypeStruct((pairs * deep, width), BF),
        scratch_shapes=[pltpu.VMEM((pairs * deep, width), BF), pltpu.SemaphoreType.DMA((1 + pairs * (width // 512),))],
        compiler_params=PARAMS,
        cost_estimate=BRIEF,
        name="weight_product",
    )(*pieces, cols)


def layer_body(half, *refs):
    pieces, weights, (out_ref, samples_ref, grid_ref, sems, more) = refs[:10], refs[10:15], refs[15:]
    tall, width = grid_ref.shape
    tall //= 2
    short = tall // 4
    rows = out_ref.shape[3]
    y, h, t = lax.axis_index("y"), lax.axis_index("h"), lax.axis_index("t")
    moves, copies = [], []
    for n, (back, start, size) in enumerate(LAY):
        place_y = lax.rem(y + 4 - back, 4)
        side = lax.rem(place_y // 2 + t, 2)
        for s in range(size):
            block = side * 4 + lax.rem(place_y, 2) * 2 + ((start + s) ^ h)
            place = pl.ds(pl.multiple_of(block * short, short), short)
            moves.append(
                pltpu.make_async_copy(weights[n].at[s * short : (s + 1) * short], grid_ref.at[place], more.at[2 * n + s])
            )
            moves[-1].start()
    for n, (back, start, size) in enumerate(LAY):
        for s in range(2):
            first = (2 * back + s) * rows + start * rows // 2
            source = pieces[2 * n + s].at[:, :width]
            copies.append(
                pltpu.make_async_copy(source, samples_ref.at[first : first + size * rows // 2], sems.at[2 * n + s])
            )
            copies[-1].start()
    for move in moves:
        move.wait()
    for n, (back, start, size) in enumerate(LAY):
        for s in range(2):
            copies[2 * n + s].wait()
        if size == 1 and start == 0:
            continue
        part = lax.dot_general(
            grid_ref[half * tall : (half + 1) * tall],
            samples_ref[2 * back * rows : 2 * (back + 1) * rows],
            (((1,), (1,)), ((), ())),
            preferred_element_type=F32,
        )
        for s in range(2):
            out_ref[s, back] = part[:, s * rows : (s + 1) * rows].astype(out_ref.dtype)


def layer_product(pieces, weights, half, kind):
    rows = pieces[0].shape[0]
    width = weights[0].shape[1]
    deep = 4 * weights[0].shape[0]
    return pl.pallas_call(
        functools.partial(layer_body, half),
        in_specs=[HBM] * 15,
        out_specs=VMEM,
        out_shape=jax.ShapeDtypeStruct((2, 4, deep // 2, rows), kind),
        scratch_shapes=[
            pltpu.VMEM((8 * rows, width), BF),
            pltpu.VMEM((deep, width), BF),
            pltpu.SemaphoreType.DMA((10,)),
            pltpu.SemaphoreType.DMA((10,)),
        ],
        compiler_params=LARGE,
        cost_estimate=BRIEF,
        name="layer_send" if half else "layer_keep",
    )(*pieces, *weights)


def pair_body(keep_ref, came_ref, same_ref, swap_ref):
    same_ref[...] = (keep_ref[0] + came_ref[0].astype(F32)).astype(BF)
    swap_ref[...] = (keep_ref[1] + came_ref[1].astype(F32)).astype(BF)


def pair_sum(keep, came):
    shape = jax.ShapeDtypeStruct(keep.shape[1:], BF)
    return pl.pallas_call(
        pair_body,
        in_specs=[VMEM] * 2,
        out_specs=[VMEM] * 2,
        out_shape=[shape, shape],
        compiler_params=PARAMS,
        cost_estimate=BRIEF,
        name="pair_sum",
    )(keep, came)


def fold_body(parts_ref, keep_ref, send_ref, total_ref):
    short = keep_ref.shape[0]
    width = keep_ref.shape[1] - EXTRA
    h = lax.axis_index("h")
    total = parts_ref[0].astype(F32)
    for k in range(1, parts_ref.shape[0]):
        total = total + parts_ref[k].astype(F32)
    total_ref[...] = total
    keep_ref[...] = total_ref[pl.ds(pl.multiple_of(h * short, short), short)]
    send_ref[:, :width] = total_ref[pl.ds(pl.multiple_of((1 - h) * short, short), short), :width].astype(BF)
    for n in range(2):
        value = total[32 * n : 32 * n + 16, width:] + total[32 * n + 16 : 32 * n + 32, width:]
        high = value.astype(BF)
        send_ref[32 * n : 32 * n + 16, width:] = high
        send_ref[32 * n + 16 : 32 * n + 32, width:] = (value - high.astype(F32)).astype(BF)


def fold_parts(parts):
    _, rows, width = parts.shape
    return pl.pallas_call(
        fold_body,
        in_specs=[VMEM],
        out_specs=[VMEM, VMEM],
        out_shape=[
            jax.ShapeDtypeStruct((rows // 2, width), F32),
            jax.ShapeDtypeStruct((rows // 2, width), BF),
        ],
        scratch_shapes=[pltpu.VMEM((rows, width), F32)],
        compiler_params=PARAMS,
        cost_estimate=BRIEF,
        name="fold",
    )(parts)


def total_body(keep_ref, came_ref, out_ref, sums_ref):
    width = out_ref.shape[1]
    out_ref[...] = keep_ref[:, :width] + came_ref[:, :width].astype(F32)
    for n in range(2):
        both = keep_ref[32 * n : 32 * n + 32, width:] + came_ref[32 * n : 32 * n + 32, width:].astype(F32)
        sums_ref[n] = both[:16] + both[16:]


def total_parts(keep, came):
    rows, width = keep.shape
    return pl.pallas_call(
        total_body,
        in_specs=[VMEM, VMEM],
        out_specs=[VMEM, VMEM],
        out_shape=[
            jax.ShapeDtypeStruct((rows, width - EXTRA), F32),
            jax.ShapeDtypeStruct((2, 16, EXTRA), F32),
        ],
        compiler_params=PARAMS,
        cost_estimate=BRIEF,
        name="total",
    )(keep, came)


def finish_body(*refs):
    parts, (cot_ref, out_ref, all_ref) = refs[:8], refs[8:]
    x, c = lax.axis_index("x"), lax.axis_index("c")
    blocks, owners, cols, rows = all_ref.shape
    for k in range(4):
        for s in range(2):
            owner = lax.rem(x + k, 4) * 2 + (c if s == 0 else 1 - c)
            for b in range(blocks):
                all_ref[b, owner] = parts[2 * k + s][b * cols : (b + 1) * cols, :].astype(F32)
    wide = owners * cols
    for b in range(blocks):
        total = all_ref[b].reshape(wide, rows).T
        span = slice(b * wide, (b + 1) * wide)
        out_ref[:, span] = (cot_ref[:, span].astype(F32) + total).astype(BF)


def finish(parts, cotangent, cols):
    tall, rows = parts[0].shape
    return pl.pallas_call(
        finish_body,
        in_specs=[VMEM] * 9,
        out_specs=VMEM,
        out_shape=jax.ShapeDtypeStruct(cotangent.shape, BF),
        scratch_shapes=[pltpu.VMEM((tall // cols, 8, cols, rows), F32)],
        compiler_params=PARAMS,
        cost_estimate=BRIEF,
        name="finish",
    )(*parts, cotangent)


def ahead(value, axis, size, steps):
    return lax.ppermute(value, axis, [(i, (i + steps) % size) for i in range(size)])


def swap(value, axis, size, bit):
    return lax.ppermute(value, axis, [(i, i ^ bit) for i in range(size)])


def ring_gather(value, axis):
    rows = value.shape[0]
    left, right = ahead(value, axis, 4, 1), ahead(value, axis, 4, 3)
    far_low = ahead(left[: rows // 2], axis, 4, 1)
    far_high = ahead(right[rows // 2 :], axis, 4, 3)
    return [value, left, right, far_low, far_high]


def shards(x_first, x_layer, pre_act, gamma, weight, cotangent):
    both = ("t", "x", "c")
    n_near, pairs = 8, 2
    samples, half = x_first.shape
    cols = weight.shape[1]
    blocks = half // (n_near * cols)
    gamma = gamma[None, :]

    by_owner = x_layer.T.reshape(blocks, n_near, cols, samples).transpose(1, 0, 2, 3)
    by_owner = by_owner.reshape(n_near, blocks * cols, samples)
    sent = jnp.concatenate([by_owner] * pairs, axis=0)
    weight_bf = weight.T.astype(BF)
    x_first, sent, weight_bf = lax.optimization_barrier((x_first, sent, weight_bf))
    came = lax.all_to_all(sent, both, 0, 0, tiled=True).reshape(pairs, n_near, blocks * cols, samples)

    gpre = gate_step(x_first, pre_act, gamma, cotangent)
    own = ring_gather(gpre, "x")
    weight_two = jnp.concatenate([weight_bf, swap(weight_bf, "h", 2, 1)], axis=0)
    weights = ring_gather(weight_two, "y")
    grad_first = first_step(pre_act, gamma, cotangent)

    own, weights, came, grad_first = lax.optimization_barrier((own, weights, came, grad_first))
    pieces = []
    for piece in own:
        pieces += [piece, swap(piece, "c", 2, 1)]

    part = weight_product(pieces, came)
    weight_part = lax.all_to_all(part.reshape(4, 2 * cols, half + EXTRA), "y", 0, 0, tiled=True)
    pieces, part = lax.optimization_barrier((pieces, part))
    sent = layer_product(pieces, weights, 1, BF)
    weights, sent = lax.optimization_barrier((weights, sent))
    keep = layer_product(pieces, weights, 0, F32)
    mine, passed = pair_sum(keep, swap(sent, "t", 2, 1))
    passed = swap(passed, "c", 2, 1)
    parts = [mine[0], passed[0]]
    for k in (1, 2, 3):
        both = jnp.stack([mine[k], passed[k]])
        both = ahead(both, "x", 4, -k)
        parts += [both[0], both[1]]
    grad_layer = finish(parts, cotangent, cols)
    kept, folded = fold_parts(weight_part)
    grad_weight, sums = total_parts(kept, swap(folded, "h", 2, 1))
    return grad_first, grad_layer, grad_weight.T, sums[0].reshape(half), sums[1].reshape(half)


def solution(mesh):
    fine = Mesh(mesh.devices.reshape(2, 4, 2, 4, 2), ("t", "y", "h", "x", "c"))
    batch = ("y", "h", "x", "c")
    wide = P(batch, "t")
    return jax.shard_map(
        shards,
        mesh=fine,
        in_specs=(wide, wide, wide, P("t"), P("t", batch), wide),
        out_specs=(wide, wide, P("t", batch), P("t"), P("t")),
        check_vma=False,
    )
```

```python
import jax
import jax.numpy as jnp
from jax import lax
from jax.experimental import pallas as pl
from jax.experimental.pallas import tpu as pltpu
from jax.sharding import Mesh, PartitionSpec as P

BF = jnp.bfloat16
F32 = jnp.float32
PARAMS = pltpu.CompilerParams(vmem_limit_bytes=24 * 1024 * 1024)
LARGE = pltpu.CompilerParams(vmem_limit_bytes=60 * 1024 * 1024)
ANY = pl.BlockSpec(memory_space=pl.ANY)
VMEM = pl.BlockSpec(memory_space=pltpu.VMEM)
HBM = pl.BlockSpec(memory_space=pltpu.HBM)
EXTRA = 128
BRIEF = pl.CostEstimate(flops=1000, bytes_accessed=1000, transcendentals=0)


def gate_body(first_ref, pre_ref, gamma_ref, cot_ref, gpre_ref, *scratch):
    bufs, sems = scratch[:3], scratch[3]
    rows, width = first_ref.shape
    lanes = gpre_ref.shape[1] - width
    tile = 512
    copies = []
    for j in range(width // tile):
        span = slice(j * tile, (j + 1) * tile)
        for n, ref in enumerate((first_ref, pre_ref, cot_ref)):
            copies.append(pltpu.make_async_copy(ref.at[:, span], bufs[n].at[:, span], sems.at[3 * j + n]))
            copies[-1].start()
    gpre_ref[96:, width:] = jnp.zeros((rows - 96, lanes), BF)
    for j in range(width // tile):
        span = slice(j * tile, (j + 1) * tile)
        for copy in copies[3 * j : 3 * j + 3]:
            copy.wait()
        gamma = gamma_ref[:, span]
        pre = bufs[1][:, span].astype(F32)
        gate = jnp.tanh(gamma * pre)
        hidden = bufs[2][:, span].astype(F32) * bufs[0][:, span].astype(F32)
        turn = pre * (1.0 - gate * gate)
        gpre = (hidden * (gate + gamma * turn)).astype(BF)
        gpre_ref[:, span] = gpre
        sums = jnp.sum(gpre.astype(F32), axis=0, keepdims=True), jnp.sum(hidden * pre * turn, axis=0, keepdims=True)
        for n, rest in enumerate(sums):
            for p in range(3):
                piece = rest.astype(BF)
                rest = rest - piece.astype(F32)
                for i in range(tile // lanes):
                    row = 48 * n + 16 * p + j * (tile // lanes) + i
                    gpre_ref[row : row + 1, width:] = piece[:, i * lanes : (i + 1) * lanes]


def gate_step(x_first, pre_act, gamma, cotangent):
    rows, width = x_first.shape
    buf = pltpu.VMEM((rows, width), BF)
    return pl.pallas_call(
        gate_body,
        in_specs=[ANY, ANY, VMEM, ANY],
        out_specs=VMEM,
        out_shape=jax.ShapeDtypeStruct((rows, width + EXTRA), BF),
        scratch_shapes=[buf, buf, buf, pltpu.SemaphoreType.DMA((3 * width // 512,))],
        compiler_params=LARGE,
        cost_estimate=pl.CostEstimate(flops=rows * width * 20, bytes_accessed=rows * width * 8, transcendentals=rows * width),
        name="gate",
    )(x_first, pre_act, gamma, cotangent)


def first_body(pre_ref, gamma_ref, cot_ref, out_ref):
    pre = pre_ref[...].astype(F32)
    out_ref[...] = (cot_ref[...].astype(F32) * (pre * jnp.tanh(gamma_ref[...] * pre))).astype(BF)


def first_step(pre_act, gamma, cotangent):
    rows, width = pre_act.shape
    tile = 512
    block = pl.BlockSpec((rows, tile), lambda j: (0, j))
    return pl.pallas_call(
        first_body,
        grid=(width // tile,),
        in_specs=[block, pl.BlockSpec((1, tile), lambda j: (0, j)), block],
        out_specs=block,
        out_shape=jax.ShapeDtypeStruct((rows, width), BF),
        compiler_params=LARGE,
        cost_estimate=BRIEF,
        name="first",
    )(pre_act, gamma, cotangent)


LAY = ((0, 0, 2), (1, 0, 2), (3, 0, 2), (2, 0, 1), (2, 1, 1))


def sample_rows(pieces, back, s, span):
    return [pieces[2 * n + s][:, span] for n, place in enumerate(LAY) if place[0] == back]


def product_body(*refs):
    pieces, weights, cols = refs[:10], refs[10:15], refs[15:17]
    result_ref, send_ref, keep_ref, out_ref, grid_ref, sems, more = refs[17:]
    owners, deep, _ = cols[0].shape
    tall, width = grid_ref.shape
    tall //= 2
    short = tall // 4
    rows = send_ref.shape[3]
    x, c, y, h, t = (lax.axis_index(name) for name in ("x", "c", "y", "h", "t"))
    moves = []
    for n, (back, start, size) in enumerate(LAY):
        place_y = lax.rem(y + 4 - back, 4)
        side = lax.rem(place_y // 2 + t, 2)
        for s in range(size):
            block = side * 4 + lax.rem(place_y, 2) * 2 + ((start + s) ^ h)
            place = pl.ds(pl.multiple_of(block * short, short), short)
            moves.append(
                pltpu.make_async_copy(weights[n].at[s * short : (s + 1) * short], grid_ref.at[place], more.at[2 * n + s])
            )
            moves[-1].start()
    order = [(back, s) for back in range(4) for s in range(2)]
    total = 0.0
    for back, s in order:
        total = total + jnp.concatenate(sample_rows(pieces, back, s, slice(width, width + EXTRA))).astype(F32)
    for n in range(2):
        value = total[48 * n : 48 * n + 16] + total[48 * n + 16 : 48 * n + 32] + total[48 * n + 32 : 48 * n + 48]
        high = value.astype(BF)
        low = (value - high.astype(F32)).astype(BF)
        for b in range(2 * deep // 64):
            out_ref[64 * b + 32 * n : 64 * b + 32 * n + 16, width:] = high
            out_ref[64 * b + 32 * n + 16 : 64 * b + 32 * n + 32, width:] = low
    sends = [pltpu.make_async_copy(out_ref.at[:, width:], result_ref.at[:, width:], sems.at[0])]
    sends[0].start()
    tile = 512
    owner = [lax.rem(x + 4 - back, 4) * 2 + (s ^ c) for back, s in order]
    for p in range(2):
        block = pl.ds(pl.multiple_of((p ^ t) * deep, deep), deep)
        grid = jnp.concatenate([cols[p][a] for a in owner], axis=1)
        for j in range(width // tile):
            span = slice(j * tile, (j + 1) * tile)
            samples = jnp.concatenate(sum((sample_rows(pieces, back, s, span) for back, s in order), []))
            out_ref[block, span] = jnp.dot(grid, samples, preferred_element_type=F32).astype(BF)
            sends.append(
                pltpu.make_async_copy(out_ref.at[block, span], result_ref.at[block, span], sems.at[len(sends)])
            )
            sends[-1].start()
    for move in moves:
        move.wait()
    for half, target in ((1, send_ref), (0, keep_ref)):
        for back in range(4):
            samples = jnp.concatenate(sum((sample_rows(pieces, back, s, slice(0, width)) for s in range(2)), []))
            part = lax.dot_general(
                grid_ref[half * tall : (half + 1) * tall],
                samples,
                (((1,), (1,)), ((), ())),
                preferred_element_type=F32,
            )
            for s in range(2):
                target[s, back] = part[:, s * rows : (s + 1) * rows].astype(target.dtype)
    for send in sends:
        send.wait()


def products(pieces, weights, same, other):
    rows, wide = pieces[0].shape
    width = weights[0].shape[1]
    _, deep, _ = same.shape
    return pl.pallas_call(
        product_body,
        in_specs=[VMEM] * 10 + [HBM] * 5 + [VMEM] * 2,
        out_specs=[HBM, VMEM, VMEM],
        out_shape=[
            jax.ShapeDtypeStruct((2 * deep, wide), BF),
            jax.ShapeDtypeStruct((2, 4, deep, rows), BF),
            jax.ShapeDtypeStruct((2, 4, deep, rows), F32),
        ],
        scratch_shapes=[
            pltpu.VMEM((2 * deep, wide), BF),
            pltpu.VMEM((2 * deep, width), BF),
            pltpu.SemaphoreType.DMA((1 + 2 * (width // 512),)),
            pltpu.SemaphoreType.DMA((10,)),
        ],
        compiler_params=pltpu.CompilerParams(vmem_limit_bytes=57 * 1024 * 1024),
        cost_estimate=BRIEF,
        name="products",
    )(*pieces, *weights, same, other)


def pair_body(keep_ref, came_ref, same_ref, swap_ref):
    same_ref[...] = (keep_ref[0] + came_ref[0].astype(F32)).astype(BF)
    swap_ref[...] = (keep_ref[1] + came_ref[1].astype(F32)).astype(BF)


def pair_sum(keep, came):
    shape = jax.ShapeDtypeStruct(keep.shape[1:], BF)
    return pl.pallas_call(
        pair_body,
        in_specs=[VMEM] * 2,
        out_specs=[VMEM] * 2,
        out_shape=[shape, shape],
        compiler_params=PARAMS,
        cost_estimate=BRIEF,
        name="pair_sum",
    )(keep, came)


def fold_body(parts_ref, keep_ref, send_ref, total_ref):
    short = keep_ref.shape[0]
    width = keep_ref.shape[1] - EXTRA
    h = lax.axis_index("h")
    total = parts_ref[0].astype(F32)
    for k in range(1, parts_ref.shape[0]):
        total = total + parts_ref[k].astype(F32)
    total_ref[...] = total
    keep_ref[...] = total_ref[pl.ds(pl.multiple_of(h * short, short), short)]
    send_ref[:, :width] = total_ref[pl.ds(pl.multiple_of((1 - h) * short, short), short), :width].astype(BF)
    for n in range(2):
        value = total[32 * n : 32 * n + 16, width:] + total[32 * n + 16 : 32 * n + 32, width:]
        high = value.astype(BF)
        send_ref[32 * n : 32 * n + 16, width:] = high
        send_ref[32 * n + 16 : 32 * n + 32, width:] = (value - high.astype(F32)).astype(BF)


def fold_parts(parts):
    _, rows, width = parts.shape
    return pl.pallas_call(
        fold_body,
        in_specs=[VMEM],
        out_specs=[VMEM, VMEM],
        out_shape=[
            jax.ShapeDtypeStruct((rows // 2, width), F32),
            jax.ShapeDtypeStruct((rows // 2, width), BF),
        ],
        scratch_shapes=[pltpu.VMEM((rows, width), F32)],
        compiler_params=PARAMS,
        cost_estimate=BRIEF,
        name="fold",
    )(parts)


def total_body(keep_ref, came_ref, out_ref, sums_ref):
    width = out_ref.shape[1]
    out_ref[...] = keep_ref[:, :width] + came_ref[:, :width].astype(F32)
    for n in range(2):
        both = keep_ref[32 * n : 32 * n + 32, width:] + came_ref[32 * n : 32 * n + 32, width:].astype(F32)
        sums_ref[n] = both[:16] + both[16:]


def total_parts(keep, came):
    rows, width = keep.shape
    return pl.pallas_call(
        total_body,
        in_specs=[VMEM, VMEM],
        out_specs=[VMEM, VMEM],
        out_shape=[
            jax.ShapeDtypeStruct((rows, width - EXTRA), F32),
            jax.ShapeDtypeStruct((2, 16, EXTRA), F32),
        ],
        compiler_params=PARAMS,
        cost_estimate=BRIEF,
        name="total",
    )(keep, came)


def finish_body(*refs):
    parts, (cot_ref, out_ref, all_ref) = refs[:8], refs[8:]
    x, c = lax.axis_index("x"), lax.axis_index("c")
    blocks, owners, cols, rows = all_ref.shape
    for k in range(4):
        for s in range(2):
            owner = lax.rem(x + k, 4) * 2 + (c if s == 0 else 1 - c)
            for b in range(blocks):
                all_ref[b, owner] = parts[2 * k + s][b * cols : (b + 1) * cols, :].astype(F32)
    wide = owners * cols
    for b in range(blocks):
        total = all_ref[b].reshape(wide, rows).T
        span = slice(b * wide, (b + 1) * wide)
        out_ref[:, span] = (cot_ref[:, span].astype(F32) + total).astype(BF)


def finish(parts, cotangent, cols):
    tall, rows = parts[0].shape
    return pl.pallas_call(
        finish_body,
        in_specs=[VMEM] * 9,
        out_specs=VMEM,
        out_shape=jax.ShapeDtypeStruct(cotangent.shape, BF),
        scratch_shapes=[pltpu.VMEM((tall // cols, 8, cols, rows), F32)],
        compiler_params=PARAMS,
        cost_estimate=BRIEF,
        name="finish",
    )(*parts, cotangent)


def ahead(value, axis, size, steps):
    return lax.ppermute(value, axis, [(i, (i + steps) % size) for i in range(size)])


def swap(value, axis, size, bit):
    return lax.ppermute(value, axis, [(i, i ^ bit) for i in range(size)])


def ring_gather(value, axis):
    rows = value.shape[0]
    left, right = ahead(value, axis, 4, 1), ahead(value, axis, 4, 3)
    far_low = ahead(left[: rows // 2], axis, 4, 1)
    far_high = ahead(right[rows // 2 :], axis, 4, 3)
    return [value, left, right, far_low, far_high]


def shards(x_first, x_layer, pre_act, gamma, weight, cotangent):
    n_near = 8
    samples, half = x_first.shape
    cols = weight.shape[1]
    blocks = half // (n_near * cols)
    gamma = gamma[None, :]

    by_owner = x_layer.T.reshape(blocks, n_near, cols, samples).transpose(1, 0, 2, 3)
    by_owner = by_owner.reshape(n_near, blocks * cols, samples)
    weight_bf = weight.T.astype(BF)
    x_first, by_owner, weight_bf = lax.optimization_barrier((x_first, by_owner, weight_bf))
    same = lax.all_to_all(by_owner, ("x", "c"), 0, 0, tiled=True)
    other = swap(same, "t", 2, 1)

    gpre = gate_step(x_first, pre_act, gamma, cotangent)
    own = ring_gather(gpre, "x")
    weight_two = jnp.concatenate([weight_bf, swap(weight_bf, "h", 2, 1)], axis=0)
    weights = ring_gather(weight_two, "y")
    grad_first = first_step(pre_act, gamma, cotangent)

    own, weights, other, grad_first = lax.optimization_barrier((own, weights, other, grad_first))
    pieces = []
    for piece in own:
        pieces += [piece, swap(piece, "c", 2, 1)]

    part, sent, keep = products(pieces, weights, same, other)
    weight_part = lax.all_to_all(part.reshape(4, 2 * cols, half + EXTRA), "y", 0, 0, tiled=True)
    mine, passed = pair_sum(keep, swap(sent, "t", 2, 1))
    passed = swap(passed, "c", 2, 1)
    parts = [mine[0], passed[0]]
    for k in (1, 2, 3):
        both = jnp.stack([mine[k], passed[k]])
        both = ahead(both, "x", 4, -k)
        parts += [both[0], both[1]]
    grad_layer = finish(parts, cotangent, cols)
    kept, folded = fold_parts(weight_part)
    grad_weight, sums = total_parts(kept, swap(folded, "h", 2, 1))
    return grad_first, grad_layer, grad_weight.T, sums[0].reshape(half), sums[1].reshape(half)


def solution(mesh):
    fine = Mesh(mesh.devices.reshape(2, 4, 2, 4, 2), ("t", "y", "h", "x", "c"))
    batch = ("y", "h", "x", "c")
    wide = P(batch, "t")
    return jax.shard_map(
        shards,
        mesh=fine,
        in_specs=(wide, wide, wide, P("t"), P("t", batch), wide),
        out_specs=(wide, wide, P("t", batch), P("t"), P("t")),
        check_vma=False,
    )
```

```python
import jax
import jax.numpy as jnp
from jax import lax
from jax.experimental import pallas as pl
from jax.experimental.pallas import tpu as pltpu
from jax.sharding import Mesh, PartitionSpec as P

BF = jnp.bfloat16
F32 = jnp.float32
PARAMS = pltpu.CompilerParams(vmem_limit_bytes=20 * 1024 * 1024)
LARGE = pltpu.CompilerParams(vmem_limit_bytes=60 * 1024 * 1024)
ANY = pl.BlockSpec(memory_space=pl.ANY)
VMEM = pl.BlockSpec(memory_space=pltpu.VMEM)
HBM = pl.BlockSpec(memory_space=pltpu.HBM)
EXTRA = 128
BRIEF = pl.CostEstimate(flops=1000, bytes_accessed=1000, transcendentals=0)


def gate_body(first_ref, pre_ref, gamma_ref, cot_ref, gpre_ref, *scratch):
    bufs, sems = scratch[:3], scratch[3]
    rows, width = first_ref.shape
    lanes = gpre_ref.shape[1] - width
    tile = 512
    copies = []
    for j in range(width // tile):
        span = slice(j * tile, (j + 1) * tile)
        for n, ref in enumerate((first_ref, pre_ref, cot_ref)):
            copies.append(pltpu.make_async_copy(ref.at[:, span], bufs[n].at[:, span], sems.at[3 * j + n]))
            copies[-1].start()
    gpre_ref[96:, width:] = jnp.zeros((rows - 96, lanes), BF)
    for j in range(width // tile):
        span = slice(j * tile, (j + 1) * tile)
        for copy in copies[3 * j : 3 * j + 3]:
            copy.wait()
        gamma = gamma_ref[:, span]
        pre = bufs[1][:, span].astype(F32)
        gate = jnp.tanh(gamma * pre)
        hidden = bufs[2][:, span].astype(F32) * bufs[0][:, span].astype(F32)
        turn = pre * (1.0 - gate * gate)
        gpre = (hidden * (gate + gamma * turn)).astype(BF)
        gpre_ref[:, span] = gpre
        sums = jnp.sum(gpre.astype(F32), axis=0, keepdims=True), jnp.sum(hidden * pre * turn, axis=0, keepdims=True)
        for n, rest in enumerate(sums):
            for p in range(3):
                piece = rest.astype(BF)
                rest = rest - piece.astype(F32)
                for i in range(tile // lanes):
                    row = 48 * n + 16 * p + j * (tile // lanes) + i
                    gpre_ref[row : row + 1, width:] = piece[:, i * lanes : (i + 1) * lanes]


def gate_step(x_first, pre_act, gamma, cotangent):
    rows, width = x_first.shape
    buf = pltpu.VMEM((rows, width), BF)
    return pl.pallas_call(
        gate_body,
        in_specs=[ANY, ANY, VMEM, ANY],
        out_specs=VMEM,
        out_shape=jax.ShapeDtypeStruct((rows, width + EXTRA), BF),
        scratch_shapes=[buf, buf, buf, pltpu.SemaphoreType.DMA((3 * width // 512,))],
        compiler_params=LARGE,
        cost_estimate=pl.CostEstimate(flops=rows * width * 20, bytes_accessed=rows * width * 8, transcendentals=rows * width),
        name="gate",
    )(x_first, pre_act, gamma, cotangent)


def first_body(pre_ref, gamma_ref, cot_ref, out_ref):
    pre = pre_ref[...].astype(F32)
    out_ref[...] = (cot_ref[...].astype(F32) * (pre * jnp.tanh(gamma_ref[...] * pre))).astype(BF)


def first_step(pre_act, gamma, cotangent):
    rows, width = pre_act.shape
    tile = 512
    block = pl.BlockSpec((rows, tile), lambda j: (0, j))
    return pl.pallas_call(
        first_body,
        grid=(width // tile,),
        in_specs=[block, pl.BlockSpec((1, tile), lambda j: (0, j)), block],
        out_specs=block,
        out_shape=jax.ShapeDtypeStruct((rows, width), BF),
        compiler_params=LARGE,
        cost_estimate=BRIEF,
        name="first",
    )(pre_act, gamma, cotangent)


LAY = ((0, 0, 2), (1, 0, 2), (3, 0, 2), (2, 0, 1), (2, 1, 1))


def sample_rows(pieces, back, s, span):
    return [pieces[2 * n + s][:, span] for n, place in enumerate(LAY) if place[0] == back]


def load_weights(weights, grid_ref, sems):
    short = grid_ref.shape[0] // 8
    y, h, t = lax.axis_index("y"), lax.axis_index("h"), lax.axis_index("t")
    moves = []
    for n, (back, start, size) in enumerate(LAY):
        place_y = lax.rem(y + 4 - back, 4)
        side = lax.rem(place_y // 2 + t, 2)
        for s in range(size):
            block = side * 4 + lax.rem(place_y, 2) * 2 + ((start + s) ^ h)
            place = pl.ds(pl.multiple_of(block * short, short), short)
            source = weights[n].at[s * short : (s + 1) * short]
            moves.append(pltpu.make_async_copy(source, grid_ref.at[place], sems.at[2 * n + s]))
            moves[-1].start()
    return moves


def product_body(*refs):
    pieces, weights, cols_ref = refs[:10], refs[10:15], refs[15]
    results, (send_ref, out_ref, grid_ref, sems, more) = refs[16:20], refs[20:]
    pairs, owners, deep, rows = cols_ref.shape
    width = grid_ref.shape[1]
    tall = grid_ref.shape[0] // 2
    x, c, y = lax.axis_index("x"), lax.axis_index("c"), lax.axis_index("y")
    moves = load_weights(weights, grid_ref, more)
    sends = []

    def hand_out(span):
        for k, result_ref in enumerate(results):
            block = pl.ds(pl.multiple_of(lax.rem(y + k, 4) * 2 * 64, 128), 128)
            sends.append(pltpu.make_async_copy(out_ref.at[block, span], result_ref.at[:, span], sems.at[len(sends)]))
            sends[-1].start()

    order = [(back, s) for back in range(4) for s in range(2)]
    total = 0.0
    for back, s in order:
        total = total + jnp.concatenate(sample_rows(pieces, back, s, slice(width, width + EXTRA))).astype(F32)
    for n in range(2):
        value = total[48 * n : 48 * n + 16] + total[48 * n + 16 : 48 * n + 32] + total[48 * n + 32 : 48 * n + 48]
        high = value.astype(BF)
        low = (value - high.astype(F32)).astype(BF)
        for b in range(pairs * deep // 64):
            out_ref[64 * b + 32 * n : 64 * b + 32 * n + 16, width:] = high
            out_ref[64 * b + 32 * n + 16 : 64 * b + 32 * n + 32, width:] = low
    hand_out(slice(width, width + EXTRA))
    tile = 512
    owner = [lax.rem(x + 4 - back, 4) * 2 + (s ^ c) for back, s in order]
    for j in range(width // tile):
        span = slice(j * tile, (j + 1) * tile)
        samples = jnp.concatenate(sum((sample_rows(pieces, back, s, span) for back, s in order), []))
        for p in range(pairs):
            grid = jnp.concatenate([cols_ref[p, a] for a in owner], axis=1)
            out_ref[p * deep : (p + 1) * deep, span] = jnp.dot(grid, samples, preferred_element_type=F32).astype(BF)
        hand_out(span)
    for move in moves:
        move.wait()
    for back in range(4):
        samples = jnp.concatenate(sum((sample_rows(pieces, back, s, slice(0, width)) for s in range(2)), []))
        part = lax.dot_general(
            grid_ref[tall:],
            samples,
            (((1,), (1,)), ((), ())),
            preferred_element_type=F32,
        ).astype(BF)
        for s in range(2):
            send_ref[s, back] = part[:, s * rows : (s + 1) * rows]
    for send in sends:
        send.wait()


def products(pieces, weights, cols):
    rows, wide = pieces[0].shape
    width = weights[0].shape[1]
    pairs, _, deep, _ = cols.shape
    return pl.pallas_call(
        product_body,
        in_specs=[VMEM] * 10 + [HBM] * 5 + [VMEM],
        out_specs=[HBM] * 4 + [VMEM],
        out_shape=[jax.ShapeDtypeStruct((pairs * deep // 4, wide), BF)] * 4
        + [jax.ShapeDtypeStruct((2, 4, deep, rows), BF)],
        scratch_shapes=[
            pltpu.VMEM((pairs * deep, wide), BF),
            pltpu.VMEM((pairs * deep, width), BF),
            pltpu.SemaphoreType.DMA((4 + 4 * (width // 512),)),
            pltpu.SemaphoreType.DMA((10,)),
        ],
        compiler_params=pltpu.CompilerParams(vmem_limit_bytes=24 * 1024 * 1024),
        cost_estimate=BRIEF,
        name="products",
    )(*pieces, *weights, cols)


def layer_body(*refs):
    pieces, weights, (out_ref, samples_ref, grid_ref, sems, more) = refs[:10], refs[10:15], refs[15:]
    tall, width = grid_ref.shape
    tall //= 2
    rows = out_ref.shape[3]
    moves, copies = load_weights(weights, grid_ref, more), []
    for n, (back, start, size) in enumerate(LAY):
        for s in range(2):
            first = (2 * back + s) * rows + start * rows // 2
            source = pieces[2 * n + s].at[:, :width]
            copies.append(
                pltpu.make_async_copy(source, samples_ref.at[first : first + size * rows // 2], sems.at[2 * n + s])
            )
            copies[-1].start()
    for move in moves:
        move.wait()
    for n, (back, start, size) in enumerate(LAY):
        for s in range(2):
            copies[2 * n + s].wait()
        if size == 1 and start == 0:
            continue
        part = lax.dot_general(
            grid_ref[:tall],
            samples_ref[2 * back * rows : 2 * (back + 1) * rows],
            (((1,), (1,)), ((), ())),
            preferred_element_type=F32,
        )
        for s in range(2):
            out_ref[s, back] = part[:, s * rows : (s + 1) * rows].astype(out_ref.dtype)


def layer_product(pieces, weights):
    rows = pieces[0].shape[0]
    width = weights[0].shape[1]
    deep = 4 * weights[0].shape[0]
    return pl.pallas_call(
        layer_body,
        in_specs=[HBM] * 15,
        out_specs=VMEM,
        out_shape=jax.ShapeDtypeStruct((2, 4, deep // 2, rows), F32),
        scratch_shapes=[
            pltpu.VMEM((8 * rows, width), BF),
            pltpu.VMEM((deep, width), BF),
            pltpu.SemaphoreType.DMA((10,)),
            pltpu.SemaphoreType.DMA((10,)),
        ],
        compiler_params=LARGE,
        cost_estimate=BRIEF,
        name="layer_keep",
    )(*pieces, *weights)


def pair_body(keep_ref, came_ref, same_ref, swap_ref):
    same_ref[...] = (keep_ref[0] + came_ref[0].astype(F32)).astype(BF)
    swap_ref[...] = (keep_ref[1] + came_ref[1].astype(F32)).astype(BF)


def pair_sum(keep, came):
    shape = jax.ShapeDtypeStruct(keep.shape[1:], BF)
    return pl.pallas_call(
        pair_body,
        in_specs=[VMEM] * 2,
        out_specs=[VMEM] * 2,
        out_shape=[shape, shape],
        compiler_params=PARAMS,
        cost_estimate=BRIEF,
        name="pair_sum",
    )(keep, came)


def fold_body(one, two, three, four, keep_ref, send_ref, total_ref):
    short = keep_ref.shape[0]
    width = keep_ref.shape[1] - EXTRA
    h = lax.axis_index("h")
    total = one[...].astype(F32)
    for ref in (two, three, four):
        total = total + ref[...].astype(F32)
    total_ref[...] = total
    keep_ref[...] = total_ref[pl.ds(pl.multiple_of(h * short, short), short)]
    send_ref[:, :width] = total_ref[pl.ds(pl.multiple_of((1 - h) * short, short), short), :width].astype(BF)
    for n in range(2):
        value = total[32 * n : 32 * n + 16, width:] + total[32 * n + 16 : 32 * n + 32, width:]
        high = value.astype(BF)
        send_ref[32 * n : 32 * n + 16, width:] = high
        send_ref[32 * n + 16 : 32 * n + 32, width:] = (value - high.astype(F32)).astype(BF)


def fold_parts(parts):
    rows, width = parts[0].shape
    return pl.pallas_call(
        fold_body,
        in_specs=[VMEM] * 4,
        out_specs=[VMEM, VMEM],
        out_shape=[
            jax.ShapeDtypeStruct((rows // 2, width), F32),
            jax.ShapeDtypeStruct((rows // 2, width), BF),
        ],
        scratch_shapes=[pltpu.VMEM((rows, width), F32)],
        compiler_params=PARAMS,
        cost_estimate=BRIEF,
        name="fold",
    )(*parts)


def total_body(keep_ref, came_ref, out_ref, sums_ref):
    width = out_ref.shape[1]
    out_ref[...] = keep_ref[:, :width] + came_ref[:, :width].astype(F32)
    for n in range(2):
        both = keep_ref[32 * n : 32 * n + 32, width:] + came_ref[32 * n : 32 * n + 32, width:].astype(F32)
        sums_ref[n] = both[:16] + both[16:]


def total_parts(keep, came):
    rows, width = keep.shape
    return pl.pallas_call(
        total_body,
        in_specs=[VMEM, VMEM],
        out_specs=[VMEM, VMEM],
        out_shape=[
            jax.ShapeDtypeStruct((rows, width - EXTRA), F32),
            jax.ShapeDtypeStruct((2, 16, EXTRA), F32),
        ],
        compiler_params=PARAMS,
        cost_estimate=BRIEF,
        name="total",
    )(keep, came)


def finish_body(*refs):
    parts, (cot_ref, out_ref, all_ref) = refs[:8], refs[8:]
    x, c = lax.axis_index("x"), lax.axis_index("c")
    blocks, owners, cols, rows = all_ref.shape
    for k in range(4):
        for s in range(2):
            owner = lax.rem(x + k, 4) * 2 + (c if s == 0 else 1 - c)
            for b in range(blocks):
                all_ref[b, owner] = parts[2 * k + s][b * cols : (b + 1) * cols, :].astype(F32)
    wide = owners * cols
    for b in range(blocks):
        total = all_ref[b].reshape(wide, rows).T
        span = slice(b * wide, (b + 1) * wide)
        out_ref[:, span] = (cot_ref[:, span].astype(F32) + total).astype(BF)


def finish(parts, cotangent, cols):
    tall, rows = parts[0].shape
    return pl.pallas_call(
        finish_body,
        in_specs=[VMEM] * 9,
        out_specs=VMEM,
        out_shape=jax.ShapeDtypeStruct(cotangent.shape, BF),
        scratch_shapes=[pltpu.VMEM((tall // cols, 8, cols, rows), F32)],
        compiler_params=PARAMS,
        cost_estimate=BRIEF,
        name="finish",
    )(*parts, cotangent)


def ahead(value, axis, size, steps):
    return lax.ppermute(value, axis, [(i, (i + steps) % size) for i in range(size)])


def swap(value, axis, size, bit):
    return lax.ppermute(value, axis, [(i, i ^ bit) for i in range(size)])


def ring_gather(value, axis):
    rows = value.shape[0]
    left, right = ahead(value, axis, 4, 1), ahead(value, axis, 4, 3)
    far_low = ahead(left[: rows // 2], axis, 4, 1)
    far_high = ahead(right[rows // 2 :], axis, 4, 3)
    return [value, left, right, far_low, far_high]


def shards(x_first, x_layer, pre_act, gamma, weight, cotangent):
    both = ("t", "x", "c")
    n_near, pairs = 8, 2
    samples, half = x_first.shape
    cols = weight.shape[1]
    blocks = half // (n_near * cols)
    gamma = gamma[None, :]

    by_owner = x_layer.T.reshape(blocks, n_near, cols, samples).transpose(1, 0, 2, 3)
    by_owner = by_owner.reshape(n_near, blocks * cols, samples)
    sent = jnp.concatenate([by_owner] * pairs, axis=0)
    weight_bf = weight.T.astype(BF)
    x_first, sent, weight_bf = lax.optimization_barrier((x_first, sent, weight_bf))
    came = lax.all_to_all(sent, both, 0, 0, tiled=True).reshape(pairs, n_near, blocks * cols, samples)

    gpre = gate_step(x_first, pre_act, gamma, cotangent)
    own = ring_gather(gpre, "x")
    weight_two = jnp.concatenate([weight_bf, swap(weight_bf, "h", 2, 1)], axis=0)
    weights = ring_gather(weight_two, "y")
    grad_first = first_step(pre_act, gamma, cotangent)

    own, weights, came, grad_first = lax.optimization_barrier((own, weights, came, grad_first))
    pieces = []
    for piece in own:
        pieces += [piece, swap(piece, "c", 2, 1)]

    *parts, sent = products(pieces, weights, came)
    weight_part = parts[:1] + [ahead(parts[k], "y", 4, k) for k in (1, 2, 3)]
    weights, sent = lax.optimization_barrier((weights, sent))
    keep = layer_product(pieces, weights)
    mine, passed = pair_sum(keep, swap(sent, "t", 2, 1))
    passed = swap(passed, "c", 2, 1)
    parts = [mine[0], passed[0]]
    for k in (1, 2, 3):
        both = jnp.stack([mine[k], passed[k]])
        both = ahead(both, "x", 4, -k)
        parts += [both[0], both[1]]
    grad_layer = finish(parts, cotangent, cols)
    kept, folded = fold_parts(weight_part)
    grad_weight, sums = total_parts(kept, swap(folded, "h", 2, 1))
    return grad_first, grad_layer, grad_weight.T, sums[0].reshape(half), sums[1].reshape(half)


def solution(mesh):
    fine = Mesh(mesh.devices.reshape(2, 4, 2, 4, 2), ("t", "y", "h", "x", "c"))
    batch = ("y", "h", "x", "c")
    wide = P(batch, "t")
    return jax.shard_map(
        shards,
        mesh=fine,
        in_specs=(wide, wide, wide, P("t"), P("t", batch), wide),
        out_specs=(wide, wide, P("t", batch), P("t"), P("t")),
        check_vma=False,
    )
```

```python
import jax
import jax.numpy as jnp
from jax import lax
from jax.experimental import pallas as pl
from jax.experimental.pallas import tpu as pltpu
from jax.sharding import Mesh, PartitionSpec as P

BF = jnp.bfloat16
F32 = jnp.float32
PARAMS = pltpu.CompilerParams(vmem_limit_bytes=20 * 1024 * 1024)
LARGE = pltpu.CompilerParams(vmem_limit_bytes=60 * 1024 * 1024)
ANY = pl.BlockSpec(memory_space=pl.ANY)
VMEM = pl.BlockSpec(memory_space=pltpu.VMEM)
HBM = pl.BlockSpec(memory_space=pltpu.HBM)
EXTRA = 128
BRIEF = pl.CostEstimate(flops=1000, bytes_accessed=1000, transcendentals=0)


def gate_body(first_ref, pre_ref, gamma_ref, cot_ref, gpre_ref, *scratch):
    bufs, sems = scratch[:3], scratch[3]
    rows, width = first_ref.shape
    lanes = gpre_ref.shape[1] - width
    tile = 512
    copies = []
    for j in range(width // tile):
        span = slice(j * tile, (j + 1) * tile)
        for n, ref in enumerate((first_ref, pre_ref, cot_ref)):
            copies.append(pltpu.make_async_copy(ref.at[:, span], bufs[n].at[:, span], sems.at[3 * j + n]))
            copies[-1].start()
    gpre_ref[96:, width:] = jnp.zeros((rows - 96, lanes), BF)
    for j in range(width // tile):
        span = slice(j * tile, (j + 1) * tile)
        for copy in copies[3 * j : 3 * j + 3]:
            copy.wait()
        gamma = gamma_ref[:, span]
        pre = bufs[1][:, span].astype(F32)
        gate = jnp.tanh(gamma * pre)
        hidden = bufs[2][:, span].astype(F32) * bufs[0][:, span].astype(F32)
        turn = pre * (1.0 - gate * gate)
        gpre = (hidden * (gate + gamma * turn)).astype(BF)
        gpre_ref[:, span] = gpre
        sums = jnp.sum(gpre.astype(F32), axis=0, keepdims=True), jnp.sum(hidden * pre * turn, axis=0, keepdims=True)
        for n, rest in enumerate(sums):
            for p in range(3):
                piece = rest.astype(BF)
                rest = rest - piece.astype(F32)
                for i in range(tile // lanes):
                    row = 48 * n + 16 * p + j * (tile // lanes) + i
                    gpre_ref[row : row + 1, width:] = piece[:, i * lanes : (i + 1) * lanes]


def gate_step(x_first, pre_act, gamma, cotangent):
    rows, width = x_first.shape
    buf = pltpu.VMEM((rows, width), BF)
    return pl.pallas_call(
        gate_body,
        in_specs=[ANY, ANY, VMEM, ANY],
        out_specs=VMEM,
        out_shape=jax.ShapeDtypeStruct((rows, width + EXTRA), BF),
        scratch_shapes=[buf, buf, buf, pltpu.SemaphoreType.DMA((3 * width // 512,))],
        compiler_params=LARGE,
        cost_estimate=pl.CostEstimate(flops=rows * width * 20, bytes_accessed=rows * width * 8, transcendentals=rows * width),
        name="gate",
    )(x_first, pre_act, gamma, cotangent)


def first_body(pre_ref, gamma_ref, cot_ref, out_ref):
    pre = pre_ref[...].astype(F32)
    out_ref[...] = (cot_ref[...].astype(F32) * (pre * jnp.tanh(gamma_ref[...] * pre))).astype(BF)


def first_step(pre_act, gamma, cotangent):
    rows, width = pre_act.shape
    tile = 512
    block = pl.BlockSpec((rows, tile), lambda j: (0, j))
    return pl.pallas_call(
        first_body,
        grid=(width // tile,),
        in_specs=[block, pl.BlockSpec((1, tile), lambda j: (0, j)), block],
        out_specs=block,
        out_shape=jax.ShapeDtypeStruct((rows, width), BF),
        compiler_params=LARGE,
        cost_estimate=BRIEF,
        name="first",
    )(pre_act, gamma, cotangent)


LAY = ((0, 0, 2), (1, 0, 2), (3, 0, 2), (2, 0, 1), (2, 1, 1))


def sample_rows(pieces, back, s, span):
    return [pieces[2 * n + s][:, span] for n, place in enumerate(LAY) if place[0] == back]


def load_weights(weights, grid_ref, sems):
    short = grid_ref.shape[0] // 8
    y, h = lax.axis_index("y"), lax.axis_index("h")
    moves = []
    for n, (back, start, size) in enumerate(LAY):
        place_y = lax.rem(y + 4 - back, 4)
        for s in range(size):
            block = place_y * 2 + ((start + s) ^ h)
            place = pl.ds(pl.multiple_of(block * short, short), short)
            source = weights[n].at[s * short : (s + 1) * short]
            moves.append(pltpu.make_async_copy(source, grid_ref.at[place], sems.at[2 * n + s]))
            moves[-1].start()
    return moves


def weight_body(*refs):
    pieces, cols_ref = refs[:10], refs[10]
    results, (out_ref, sems) = refs[11:15], refs[15:]
    pairs, owners, deep, rows = cols_ref.shape
    width = out_ref.shape[1] - EXTRA
    x, c, y = lax.axis_index("x"), lax.axis_index("c"), lax.axis_index("y")
    sends = []

    def hand_out(span):
        for k, result_ref in enumerate(results):
            block = pl.ds(pl.multiple_of(lax.rem(y + k, 4) * 2 * 64, 128), 128)
            sends.append(pltpu.make_async_copy(out_ref.at[block, span], result_ref.at[:, span], sems.at[len(sends)]))
            sends[-1].start()

    order = [(back, s) for back in range(4) for s in range(2)]
    total = 0.0
    for back, s in order:
        total = total + jnp.concatenate(sample_rows(pieces, back, s, slice(width, width + EXTRA))).astype(F32)
    for n in range(2):
        value = total[48 * n : 48 * n + 16] + total[48 * n + 16 : 48 * n + 32] + total[48 * n + 32 : 48 * n + 48]
        high = value.astype(BF)
        low = (value - high.astype(F32)).astype(BF)
        for b in range(pairs * deep // 64):
            out_ref[64 * b + 32 * n : 64 * b + 32 * n + 16, width:] = high
            out_ref[64 * b + 32 * n + 16 : 64 * b + 32 * n + 32, width:] = low
    hand_out(slice(width, width + EXTRA))
    tile = 512
    owner = [lax.rem(x + 4 - back, 4) * 2 + (s ^ c) for back, s in order]
    for j in range(width // tile):
        span = slice(j * tile, (j + 1) * tile)
        samples = jnp.concatenate(sum((sample_rows(pieces, back, s, span) for back, s in order), []))
        for p in range(pairs):
            grid = jnp.concatenate([cols_ref[p, a] for a in owner], axis=1)
            out_ref[p * deep : (p + 1) * deep, span] = jnp.dot(grid, samples, preferred_element_type=F32).astype(BF)
        hand_out(span)
    for send in sends:
        send.wait()


def weight_product(pieces, cols):
    wide = pieces[0].shape[1]
    pairs, _, deep, _ = cols.shape
    return pl.pallas_call(
        weight_body,
        in_specs=[VMEM] * 11,
        out_specs=[HBM] * 4,
        out_shape=[jax.ShapeDtypeStruct((pairs * deep // 4, wide), BF)] * 4,
        scratch_shapes=[
            pltpu.VMEM((pairs * deep, wide), BF),
            pltpu.SemaphoreType.DMA((4 + 4 * ((wide - EXTRA) // 512),)),
        ],
        compiler_params=pltpu.CompilerParams(vmem_limit_bytes=24 * 1024 * 1024),
        cost_estimate=BRIEF,
        name="weight_product",
    )(*pieces, cols)


def layer_body(*refs):
    pieces, weights, (out_ref, samples_ref, grid_ref, sems, more) = refs[:10], refs[10:15], refs[15:]
    width = grid_ref.shape[1]
    pairs, _, deep, rows = out_ref.shape
    x, c = lax.axis_index("x"), lax.axis_index("c")
    moves, copies = load_weights(weights, grid_ref, more), []
    for n, (back, start, size) in enumerate(LAY):
        for s in range(2):
            first = (2 * back + s) * rows + start * rows // 2
            source = pieces[2 * n + s].at[:, :width]
            copies.append(
                pltpu.make_async_copy(source, samples_ref.at[first : first + size * rows // 2], sems.at[2 * n + s])
            )
            copies[-1].start()
    for move in moves:
        move.wait()
    for n, (back, start, size) in enumerate(LAY):
        for s in range(2):
            copies[2 * n + s].wait()
        if size == 1 and start == 0:
            continue
        part = lax.dot_general(
            grid_ref[...],
            samples_ref[2 * back * rows : 2 * (back + 1) * rows],
            (((1,), (1,)), ((), ())),
            preferred_element_type=F32,
        )
        for s in range(2):
            owner = lax.rem(x + 4 - back, 4) * 2 + (s ^ c)
            for p in range(pairs):
                block = part[p * deep : (p + 1) * deep, s * rows : (s + 1) * rows]
                out_ref[p, owner] = block.astype(BF)


def layer_product(pieces, weights):
    rows = pieces[0].shape[0]
    width = weights[0].shape[1]
    deep = 4 * weights[0].shape[0]
    return pl.pallas_call(
        layer_body,
        in_specs=[HBM] * 15,
        out_specs=VMEM,
        out_shape=jax.ShapeDtypeStruct((2, 8, deep // 2, rows), BF),
        scratch_shapes=[
            pltpu.VMEM((8 * rows, width), BF),
            pltpu.VMEM((deep, width), BF),
            pltpu.SemaphoreType.DMA((10,)),
            pltpu.SemaphoreType.DMA((10,)),
        ],
        compiler_params=LARGE,
        cost_estimate=BRIEF,
        name="layer_product",
    )(*pieces, *weights)


def fold_body(one, two, three, four, keep_ref, send_ref, total_ref):
    short = keep_ref.shape[0]
    width = keep_ref.shape[1] - EXTRA
    h = lax.axis_index("h")
    total = one[...].astype(F32)
    for ref in (two, three, four):
        total = total + ref[...].astype(F32)
    total_ref[...] = total
    keep_ref[...] = total_ref[pl.ds(pl.multiple_of(h * short, short), short)]
    send_ref[:, :width] = total_ref[pl.ds(pl.multiple_of((1 - h) * short, short), short), :width].astype(BF)
    for n in range(2):
        value = total[32 * n : 32 * n + 16, width:] + total[32 * n + 16 : 32 * n + 32, width:]
        high = value.astype(BF)
        send_ref[32 * n : 32 * n + 16, width:] = high
        send_ref[32 * n + 16 : 32 * n + 32, width:] = (value - high.astype(F32)).astype(BF)


def fold_parts(parts):
    rows, width = parts[0].shape
    return pl.pallas_call(
        fold_body,
        in_specs=[VMEM] * 4,
        out_specs=[VMEM, VMEM],
        out_shape=[
            jax.ShapeDtypeStruct((rows // 2, width), F32),
            jax.ShapeDtypeStruct((rows // 2, width), BF),
        ],
        scratch_shapes=[pltpu.VMEM((rows, width), F32)],
        compiler_params=PARAMS,
        cost_estimate=BRIEF,
        name="fold",
    )(*parts)


def total_body(keep_ref, came_ref, out_ref, sums_ref):
    width = out_ref.shape[1]
    out_ref[...] = keep_ref[:, :width] + came_ref[:, :width].astype(F32)
    for n in range(2):
        both = keep_ref[32 * n : 32 * n + 32, width:] + came_ref[32 * n : 32 * n + 32, width:].astype(F32)
        sums_ref[n] = both[:16] + both[16:]


def total_parts(keep, came):
    rows, width = keep.shape
    return pl.pallas_call(
        total_body,
        in_specs=[VMEM, VMEM],
        out_specs=[VMEM, VMEM],
        out_shape=[
            jax.ShapeDtypeStruct((rows, width - EXTRA), F32),
            jax.ShapeDtypeStruct((2, 16, EXTRA), F32),
        ],
        compiler_params=PARAMS,
        cost_estimate=BRIEF,
        name="total",
    )(keep, came)


def finish_body(parts_ref, cot_ref, out_ref):
    owners, cols = parts_ref.shape[1], parts_ref.shape[3]
    total = parts_ref[0, :, 0].astype(F32) + parts_ref[1, :, 0].astype(F32)
    total = total.reshape(owners * cols, total.shape[2])
    out_ref[...] = (cot_ref[...].astype(F32) + total.T).astype(BF)


def finish(parts, cotangent):
    pairs, owners, blocks, cols, rows = parts.shape
    wide = owners * cols
    return pl.pallas_call(
        finish_body,
        grid=(blocks,),
        in_specs=[
            pl.BlockSpec((pairs, owners, 1, cols, rows), lambda j: (0, 0, j, 0, 0)),
            pl.BlockSpec((rows, wide), lambda j: (0, j)),
        ],
        out_specs=pl.BlockSpec((rows, wide), lambda j: (0, j)),
        out_shape=jax.ShapeDtypeStruct((rows, blocks * wide), BF),
        compiler_params=PARAMS,
        cost_estimate=BRIEF,
        name="finish",
    )(parts, cotangent)


def ahead(value, axis, size, steps):
    return lax.ppermute(value, axis, [(i, (i + steps) % size) for i in range(size)])


def swap(value, axis, size, bit):
    return lax.ppermute(value, axis, [(i, i ^ bit) for i in range(size)])


def ring_gather(value, axis):
    rows = value.shape[0]
    left, right = ahead(value, axis, 4, 1), ahead(value, axis, 4, 3)
    far_low = ahead(left[: rows // 2], axis, 4, 1)
    far_high = ahead(right[rows // 2 :], axis, 4, 3)
    return [value, left, right, far_low, far_high]


def shards(x_first, x_layer, pre_act, gamma, weight, cotangent):
    both = ("t", "x", "c")
    n_near, pairs = 8, 2
    samples, half = x_first.shape
    cols = weight.shape[1]
    blocks = half // (n_near * cols)
    gamma = gamma[None, :]

    by_owner = x_layer.T.reshape(blocks, n_near, cols, samples).transpose(1, 0, 2, 3)
    by_owner = by_owner.reshape(n_near, blocks * cols, samples)
    sent = jnp.concatenate([by_owner] * pairs, axis=0)
    weight_bf = weight.T.astype(BF)
    x_first, sent, weight_bf = lax.optimization_barrier((x_first, sent, weight_bf))
    came = lax.all_to_all(sent, both, 0, 0, tiled=True).reshape(pairs, n_near, blocks * cols, samples)

    gpre = gate_step(x_first, pre_act, gamma, cotangent)
    own = ring_gather(gpre, "x")
    weight_two = jnp.concatenate([weight_bf, swap(weight_bf, "h", 2, 1)], axis=0)
    weights = ring_gather(weight_two, "y")
    grad_first = first_step(pre_act, gamma, cotangent)

    own, weights, came, grad_first = lax.optimization_barrier((own, weights, came, grad_first))
    pieces = []
    for piece in own:
        pieces += [piece, swap(piece, "c", 2, 1)]

    parts = weight_product(pieces, came)
    pieces, parts = lax.optimization_barrier((pieces, parts))
    weight_parts = [parts[0]] + [ahead(parts[k], "y", 4, k) for k in (1, 2, 3)]
    sent = layer_product(pieces, weights).reshape(pairs * n_near, blocks * cols, samples)
    layer_parts = lax.all_to_all(sent, both, 0, 0, tiled=True)
    kept, folded = fold_parts(weight_parts)
    grad_layer = finish(layer_parts.reshape(pairs, n_near, blocks, cols, samples), cotangent)
    kept, grad_layer = lax.optimization_barrier((kept, grad_layer))
    grad_weight, sums = total_parts(kept, swap(folded, "h", 2, 1))
    return grad_first, grad_layer, grad_weight.T, sums[0].reshape(half), sums[1].reshape(half)


def solution(mesh):
    fine = Mesh(mesh.devices.reshape(2, 4, 2, 4, 2), ("t", "y", "h", "x", "c"))
    batch = ("y", "h", "x", "c")
    wide = P(batch, "t")
    return jax.shard_map(
        shards,
        mesh=fine,
        in_specs=(wide, wide, wide, P("t"), P("t", batch), wide),
        out_specs=(wide, wide, P("t", batch), P("t"), P("t")),
        check_vma=False,
    )
```

```python
import jax
import jax.numpy as jnp
from jax import lax
from jax.experimental import pallas as pl
from jax.experimental.pallas import tpu as pltpu
from jax.sharding import Mesh, PartitionSpec as P

BF = jnp.bfloat16
F32 = jnp.float32
PARAMS = pltpu.CompilerParams(vmem_limit_bytes=20 * 1024 * 1024)
LARGE = pltpu.CompilerParams(vmem_limit_bytes=60 * 1024 * 1024)
ANY = pl.BlockSpec(memory_space=pl.ANY)
VMEM = pl.BlockSpec(memory_space=pltpu.VMEM)
HBM = pl.BlockSpec(memory_space=pltpu.HBM)
EXTRA = 128
BRIEF = pl.CostEstimate(flops=1000, bytes_accessed=1000, transcendentals=0)


def gate_body(first_ref, pre_ref, gamma_ref, cot_ref, gpre_ref, *scratch):
    bufs, sems = scratch[:3], scratch[3]
    rows, width = first_ref.shape
    lanes = gpre_ref.shape[1] - width
    tile = 512
    copies = []
    for j in range(width // tile):
        span = slice(j * tile, (j + 1) * tile)
        for n, ref in enumerate((first_ref, pre_ref, cot_ref)):
            copies.append(pltpu.make_async_copy(ref.at[:, span], bufs[n].at[:, span], sems.at[3 * j + n]))
            copies[-1].start()
    gpre_ref[96:, width:] = jnp.zeros((rows - 96, lanes), BF)
    for j in range(width // tile):
        span = slice(j * tile, (j + 1) * tile)
        for copy in copies[3 * j : 3 * j + 3]:
            copy.wait()
        gamma = gamma_ref[:, span]
        pre = bufs[1][:, span].astype(F32)
        gate = jnp.tanh(gamma * pre)
        hidden = bufs[2][:, span].astype(F32) * bufs[0][:, span].astype(F32)
        turn = pre * (1.0 - gate * gate)
        gpre = (hidden * (gate + gamma * turn)).astype(BF)
        gpre_ref[:, span] = gpre
        sums = jnp.sum(gpre.astype(F32), axis=0, keepdims=True), jnp.sum(hidden * pre * turn, axis=0, keepdims=True)
        for n, rest in enumerate(sums):
            for p in range(3):
                piece = rest.astype(BF)
                rest = rest - piece.astype(F32)
                for i in range(tile // lanes):
                    row = 48 * n + 16 * p + j * (tile // lanes) + i
                    gpre_ref[row : row + 1, width:] = piece[:, i * lanes : (i + 1) * lanes]


def gate_step(x_first, pre_act, gamma, cotangent):
    rows, width = x_first.shape
    buf = pltpu.VMEM((rows, width), BF)
    return pl.pallas_call(
        gate_body,
        in_specs=[ANY, ANY, VMEM, ANY],
        out_specs=VMEM,
        out_shape=jax.ShapeDtypeStruct((rows, width + EXTRA), BF),
        scratch_shapes=[buf, buf, buf, pltpu.SemaphoreType.DMA((3 * width // 512,))],
        compiler_params=LARGE,
        cost_estimate=pl.CostEstimate(flops=rows * width * 20, bytes_accessed=rows * width * 8, transcendentals=rows * width),
        name="gate",
    )(x_first, pre_act, gamma, cotangent)


def first_body(pre_ref, gamma_ref, cot_ref, out_ref):
    pre = pre_ref[...].astype(F32)
    out_ref[...] = (cot_ref[...].astype(F32) * (pre * jnp.tanh(gamma_ref[...] * pre))).astype(BF)


def first_step(pre_act, gamma, cotangent):
    rows, width = pre_act.shape
    tile = 512
    block = pl.BlockSpec((rows, tile), lambda j: (0, j))
    return pl.pallas_call(
        first_body,
        grid=(width // tile,),
        in_specs=[block, pl.BlockSpec((1, tile), lambda j: (0, j)), block],
        out_specs=block,
        out_shape=jax.ShapeDtypeStruct((rows, width), BF),
        compiler_params=LARGE,
        cost_estimate=BRIEF,
        name="first",
    )(pre_act, gamma, cotangent)


LAY = ((0, 0, 2), (1, 0, 2), (3, 0, 2), (2, 0, 1), (2, 1, 1))


def sample_rows(pieces, back, s, span):
    return [pieces[2 * n + s][:, span] for n, place in enumerate(LAY) if place[0] == back]


def load_weights(weights, grid_ref, sems):
    short = grid_ref.shape[0] // 8
    y, h = lax.axis_index("y"), lax.axis_index("h")
    moves = []
    for n, (back, start, size) in enumerate(LAY):
        place_y = lax.rem(y + 4 - back, 4)
        for s in range(size):
            block = place_y * 2 + ((start + s) ^ h)
            place = pl.ds(pl.multiple_of(block * short, short), short)
            source = weights[n].at[s * short : (s + 1) * short]
            moves.append(pltpu.make_async_copy(source, grid_ref.at[place], sems.at[2 * n + s]))
            moves[-1].start()
    return moves


def weight_body(*refs):
    pieces, cols_ref = refs[:10], refs[10]
    results, (out_ref, sems) = refs[11:15], refs[15:]
    pairs, owners, deep, rows = cols_ref.shape
    width = out_ref.shape[1] - EXTRA
    x, c, y = lax.axis_index("x"), lax.axis_index("c"), lax.axis_index("y")
    sends = []

    def hand_out(span):
        for k, result_ref in enumerate(results):
            block = pl.ds(pl.multiple_of(lax.rem(y + k, 4) * 2 * 64, 128), 128)
            sends.append(pltpu.make_async_copy(out_ref.at[block, span], result_ref.at[:, span], sems.at[len(sends)]))
            sends[-1].start()

    order = [(back, s) for back in range(4) for s in range(2)]
    total = 0.0
    for back, s in order:
        total = total + jnp.concatenate(sample_rows(pieces, back, s, slice(width, width + EXTRA))).astype(F32)
    for n in range(2):
        value = total[48 * n : 48 * n + 16] + total[48 * n + 16 : 48 * n + 32] + total[48 * n + 32 : 48 * n + 48]
        high = value.astype(BF)
        low = (value - high.astype(F32)).astype(BF)
        for b in range(pairs * deep // 64):
            out_ref[64 * b + 32 * n : 64 * b + 32 * n + 16, width:] = high
            out_ref[64 * b + 32 * n + 16 : 64 * b + 32 * n + 32, width:] = low
    hand_out(slice(width, width + EXTRA))
    tile = 512
    owner = [lax.rem(x + 4 - back, 4) * 2 + (s ^ c) for back, s in order]
    for j in range(width // tile):
        span = slice(j * tile, (j + 1) * tile)
        samples = jnp.concatenate(sum((sample_rows(pieces, back, s, span) for back, s in order), []))
        for p in range(pairs):
            grid = jnp.concatenate([cols_ref[p, a] for a in owner], axis=1)
            out_ref[p * deep : (p + 1) * deep, span] = jnp.dot(grid, samples, preferred_element_type=F32).astype(BF)
        hand_out(span)
    for send in sends:
        send.wait()


def weight_product(pieces, cols):
    wide = pieces[0].shape[1]
    pairs, _, deep, _ = cols.shape
    return pl.pallas_call(
        weight_body,
        in_specs=[VMEM] * 11,
        out_specs=[HBM] * 4,
        out_shape=[jax.ShapeDtypeStruct((pairs * deep // 4, wide), BF)] * 4,
        scratch_shapes=[
            pltpu.VMEM((pairs * deep, wide), BF),
            pltpu.SemaphoreType.DMA((4 + 4 * ((wide - EXTRA) // 512),)),
        ],
        compiler_params=pltpu.CompilerParams(vmem_limit_bytes=24 * 1024 * 1024),
        cost_estimate=BRIEF,
        name="weight_product",
    )(*pieces, cols)


def layer_body(*refs):
    pieces, weights, (out_ref, samples_ref, grid_ref, sems, more) = refs[:10], refs[10:15], refs[15:]
    width = grid_ref.shape[1]
    pairs, _, deep, rows = out_ref.shape
    x, c = lax.axis_index("x"), lax.axis_index("c")
    moves, copies = load_weights(weights, grid_ref, more), []
    for n, (back, start, size) in enumerate(LAY):
        for s in range(2):
            first = (2 * back + s) * rows + start * rows // 2
            source = pieces[2 * n + s].at[:, :width]
            copies.append(
                pltpu.make_async_copy(source, samples_ref.at[first : first + size * rows // 2], sems.at[2 * n + s])
            )
            copies[-1].start()
    for move in moves:
        move.wait()
    for n, (back, start, size) in enumerate(LAY):
        for s in range(2):
            copies[2 * n + s].wait()
        if size == 1 and start == 0:
            continue
        part = lax.dot_general(
            grid_ref[...],
            samples_ref[2 * back * rows : 2 * (back + 1) * rows],
            (((1,), (1,)), ((), ())),
            preferred_element_type=F32,
        )
        for s in range(2):
            owner = lax.rem(x + 4 - back, 4) * 2 + (s ^ c)
            for p in range(pairs):
                block = part[p * deep : (p + 1) * deep, s * rows : (s + 1) * rows]
                out_ref[p, owner] = block.astype(BF)


def layer_product(pieces, weights):
    rows = pieces[0].shape[0]
    width = weights[0].shape[1]
    deep = 4 * weights[0].shape[0]
    return pl.pallas_call(
        layer_body,
        in_specs=[HBM] * 15,
        out_specs=VMEM,
        out_shape=jax.ShapeDtypeStruct((2, 8, deep // 2, rows), BF),
        scratch_shapes=[
            pltpu.VMEM((8 * rows, width), BF),
            pltpu.VMEM((deep, width), BF),
            pltpu.SemaphoreType.DMA((10,)),
            pltpu.SemaphoreType.DMA((10,)),
        ],
        compiler_params=LARGE,
        cost_estimate=BRIEF,
        name="layer_product",
    )(*pieces, *weights)


def fold_body(one, two, three, four, keep_ref, send_ref, total_ref):
    short = keep_ref.shape[0]
    width = keep_ref.shape[1] - EXTRA
    h = lax.axis_index("h")
    total = one[...].astype(F32)
    for ref in (two, three, four):
        total = total + ref[...].astype(F32)
    total_ref[...] = total
    keep_ref[...] = total_ref[pl.ds(pl.multiple_of(h * short, short), short)]
    send_ref[:, :width] = total_ref[pl.ds(pl.multiple_of((1 - h) * short, short), short), :width].astype(BF)
    for n in range(2):
        value = total[32 * n : 32 * n + 16, width:] + total[32 * n + 16 : 32 * n + 32, width:]
        high = value.astype(BF)
        send_ref[32 * n : 32 * n + 16, width:] = high
        send_ref[32 * n + 16 : 32 * n + 32, width:] = (value - high.astype(F32)).astype(BF)


def fold_parts(parts):
    rows, width = parts[0].shape
    return pl.pallas_call(
        fold_body,
        in_specs=[VMEM] * 4,
        out_specs=[VMEM, VMEM],
        out_shape=[
            jax.ShapeDtypeStruct((rows // 2, width), F32),
            jax.ShapeDtypeStruct((rows // 2, width), BF),
        ],
        scratch_shapes=[pltpu.VMEM((rows, width), F32)],
        compiler_params=PARAMS,
        cost_estimate=BRIEF,
        name="fold",
    )(*parts)


def total_body(keep_ref, came_ref, out_ref, sums_ref):
    width = out_ref.shape[1]
    out_ref[...] = keep_ref[:, :width] + came_ref[:, :width].astype(F32)
    for n in range(2):
        both = keep_ref[32 * n : 32 * n + 32, width:] + came_ref[32 * n : 32 * n + 32, width:].astype(F32)
        sums_ref[n] = both[:16] + both[16:]


def total_parts(keep, came):
    rows, width = keep.shape
    return pl.pallas_call(
        total_body,
        in_specs=[VMEM, VMEM],
        out_specs=[VMEM, VMEM],
        out_shape=[
            jax.ShapeDtypeStruct((rows, width - EXTRA), F32),
            jax.ShapeDtypeStruct((2, 16, EXTRA), F32),
        ],
        compiler_params=PARAMS,
        cost_estimate=BRIEF,
        name="total",
    )(keep, came)


def finish_body(parts_ref, cot_ref, out_ref):
    owners, cols = parts_ref.shape[1], parts_ref.shape[3]
    total = parts_ref[0, :, 0].astype(F32) + parts_ref[1, :, 0].astype(F32)
    total = total.reshape(owners * cols, total.shape[2])
    out_ref[...] = (cot_ref[...].astype(F32) + total.T).astype(BF)


def finish(parts, cotangent):
    pairs, owners, blocks, cols, rows = parts.shape
    wide = owners * cols
    return pl.pallas_call(
        finish_body,
        grid=(blocks,),
        in_specs=[
            pl.BlockSpec((pairs, owners, 1, cols, rows), lambda j: (0, 0, j, 0, 0)),
            pl.BlockSpec((rows, wide), lambda j: (0, j)),
        ],
        out_specs=pl.BlockSpec((rows, wide), lambda j: (0, j)),
        out_shape=jax.ShapeDtypeStruct((rows, blocks * wide), BF),
        compiler_params=PARAMS,
        cost_estimate=BRIEF,
        name="finish",
    )(parts, cotangent)


def ahead(value, axis, size, steps):
    return lax.ppermute(value, axis, [(i, (i + steps) % size) for i in range(size)])


def swap(value, axis, size, bit):
    return lax.ppermute(value, axis, [(i, i ^ bit) for i in range(size)])


def ring_gather(value, axis):
    rows = value.shape[0]
    left, right = ahead(value, axis, 4, 1), ahead(value, axis, 4, 3)
    far_low = ahead(left[: rows // 2], axis, 4, 1)
    far_high = ahead(right[rows // 2 :], axis, 4, 3)
    return [value, left, right, far_low, far_high]


def shards(x_first, x_layer, pre_act, gamma, weight, cotangent):
    both = ("t", "x", "c")
    n_near, pairs = 8, 2
    samples, half = x_first.shape
    cols = weight.shape[1]
    blocks = half // (n_near * cols)
    gamma = gamma[None, :]

    by_owner = x_layer.T.reshape(blocks, n_near, cols, samples).transpose(1, 0, 2, 3)
    by_owner = by_owner.reshape(n_near, blocks * cols, samples)
    sent = jnp.concatenate([by_owner] * pairs, axis=0)
    weight_bf = weight.T.astype(BF)
    x_first, sent, weight_bf = lax.optimization_barrier((x_first, sent, weight_bf))
    came = lax.all_to_all(sent, both, 0, 0, tiled=True).reshape(pairs, n_near, blocks * cols, samples)

    gpre = gate_step(x_first, pre_act, gamma, cotangent)
    own = ring_gather(gpre, "x")
    weight_two = jnp.concatenate([weight_bf, swap(weight_bf, "h", 2, 1)], axis=0)
    weights = ring_gather(weight_two, "y")
    grad_first = first_step(pre_act, gamma, cotangent)

    own, weights, came, grad_first = lax.optimization_barrier((own, weights, came, grad_first))
    pieces = []
    for piece in own:
        pieces += [piece, swap(piece, "c", 2, 1)]

    parts = weight_product(pieces, came)
    pieces, parts = lax.optimization_barrier((pieces, parts))
    weight_parts = [parts[0]] + [ahead(parts[k], "y", 4, k) for k in (1, 2, 3)]
    sent = layer_product(pieces, weights).reshape(pairs * n_near, blocks * cols, samples)
    layer_parts = lax.all_to_all(sent, both, 0, 0, tiled=True)
    kept, folded = fold_parts(weight_parts)
    grad_layer = finish(layer_parts.reshape(pairs, n_near, blocks, cols, samples), cotangent)
    grad_weight, sums = total_parts(kept, swap(folded, "h", 2, 1))
    return grad_first, grad_layer, grad_weight.T, sums[0].reshape(half), sums[1].reshape(half)


def solution(mesh):
    fine = Mesh(mesh.devices.reshape(2, 4, 2, 4, 2), ("t", "y", "h", "x", "c"))
    batch = ("y", "h", "x", "c")
    wide = P(batch, "t")
    return jax.shard_map(
        shards,
        mesh=fine,
        in_specs=(wide, wide, wide, P("t"), P("t", batch), wide),
        out_specs=(wide, wide, P("t", batch), P("t"), P("t")),
        check_vma=False,
    )
```

```python
import jax
import jax.numpy as jnp
from jax import lax
from jax.experimental import pallas as pl
from jax.experimental.pallas import tpu as pltpu
from jax.sharding import Mesh, PartitionSpec as P

BF = jnp.bfloat16
F32 = jnp.float32
PARAMS = pltpu.CompilerParams(vmem_limit_bytes=20 * 1024 * 1024)
LARGE = pltpu.CompilerParams(vmem_limit_bytes=60 * 1024 * 1024)
ANY = pl.BlockSpec(memory_space=pl.ANY)
VMEM = pl.BlockSpec(memory_space=pltpu.VMEM)
HBM = pl.BlockSpec(memory_space=pltpu.HBM)
EXTRA = 128
BRIEF = pl.CostEstimate(flops=1000, bytes_accessed=1000, transcendentals=0)


def gate_body(first_ref, pre_ref, gamma_ref, cot_ref, gpre_ref, *scratch):
    bufs, sems = scratch[:3], scratch[3]
    rows, width = first_ref.shape
    lanes = gpre_ref.shape[1] - width
    tile = 512
    copies = []
    for j in range(width // tile):
        span = slice(j * tile, (j + 1) * tile)
        for n, ref in enumerate((first_ref, pre_ref, cot_ref)):
            copies.append(pltpu.make_async_copy(ref.at[:, span], bufs[n].at[:, span], sems.at[3 * j + n]))
            copies[-1].start()
    gpre_ref[96:, width:] = jnp.zeros((rows - 96, lanes), BF)
    for j in range(width // tile):
        span = slice(j * tile, (j + 1) * tile)
        for copy in copies[3 * j : 3 * j + 3]:
            copy.wait()
        gamma = gamma_ref[:, span]
        pre = bufs[1][:, span].astype(F32)
        gate = jnp.tanh(gamma * pre)
        hidden = bufs[2][:, span].astype(F32) * bufs[0][:, span].astype(F32)
        turn = pre * (1.0 - gate * gate)
        gpre = (hidden * (gate + gamma * turn)).astype(BF)
        gpre_ref[:, span] = gpre
        sums = jnp.sum(gpre.astype(F32), axis=0, keepdims=True), jnp.sum(hidden * pre * turn, axis=0, keepdims=True)
        for n, rest in enumerate(sums):
            for p in range(3):
                piece = rest.astype(BF)
                rest = rest - piece.astype(F32)
                for i in range(tile // lanes):
                    row = 48 * n + 16 * p + j * (tile // lanes) + i
                    gpre_ref[row : row + 1, width:] = piece[:, i * lanes : (i + 1) * lanes]


def gate_step(x_first, pre_act, gamma, cotangent):
    rows, width = x_first.shape
    buf = pltpu.VMEM((rows, width), BF)
    return pl.pallas_call(
        gate_body,
        in_specs=[ANY, ANY, VMEM, ANY],
        out_specs=VMEM,
        out_shape=jax.ShapeDtypeStruct((rows, width + EXTRA), BF),
        scratch_shapes=[buf, buf, buf, pltpu.SemaphoreType.DMA((3 * width // 512,))],
        compiler_params=LARGE,
        cost_estimate=pl.CostEstimate(flops=rows * width * 20, bytes_accessed=rows * width * 8, transcendentals=rows * width),
        name="gate",
    )(x_first, pre_act, gamma, cotangent)


def first_body(pre_ref, gamma_ref, cot_ref, out_ref):
    pre = pre_ref[...].astype(F32)
    out_ref[...] = (cot_ref[...].astype(F32) * (pre * jnp.tanh(gamma_ref[...] * pre))).astype(BF)


def first_step(pre_act, gamma, cotangent):
    rows, width = pre_act.shape
    tile = 512
    block = pl.BlockSpec((rows, tile), lambda j: (0, j))
    return pl.pallas_call(
        first_body,
        grid=(width // tile,),
        in_specs=[block, pl.BlockSpec((1, tile), lambda j: (0, j)), block],
        out_specs=block,
        out_shape=jax.ShapeDtypeStruct((rows, width), BF),
        compiler_params=LARGE,
        cost_estimate=BRIEF,
        name="first",
    )(pre_act, gamma, cotangent)


LAY = ((0, 0, 2), (1, 0, 2), (3, 0, 2), (2, 0, 1), (2, 1, 1))


def sample_rows(pieces, back, s, span):
    return [pieces[2 * n + s][:, span] for n, place in enumerate(LAY) if place[0] == back]


def load_weights(weights, grid_ref, sems):
    short = grid_ref.shape[0] // 8
    y, h = lax.axis_index("y"), lax.axis_index("h")
    moves = []
    for n, (back, start, size) in enumerate(LAY):
        place_y = lax.rem(y + 4 - back, 4)
        for s in range(size):
            block = place_y * 2 + ((start + s) ^ h)
            place = pl.ds(pl.multiple_of(block * short, short), short)
            source = weights[n].at[s * short : (s + 1) * short]
            moves.append(pltpu.make_async_copy(source, grid_ref.at[place], sems.at[2 * n + s]))
            moves[-1].start()
    return moves


def weight_body(*refs):
    pieces, cols_ref = refs[:10], refs[10]
    results, (out_ref, sems) = refs[11:15], refs[15:]
    pairs, owners, deep, rows = cols_ref.shape
    width = out_ref.shape[1] - EXTRA
    x, c, y = lax.axis_index("x"), lax.axis_index("c"), lax.axis_index("y")
    sends = []

    def hand_out(span):
        for k, result_ref in enumerate(results):
            block = pl.ds(pl.multiple_of(lax.rem(y + k, 4) * 2 * 64, 128), 128)
            sends.append(pltpu.make_async_copy(out_ref.at[block, span], result_ref.at[:, span], sems.at[len(sends)]))
            sends[-1].start()

    order = [(back, s) for back in range(4) for s in range(2)]
    total = 0.0
    for back, s in order:
        total = total + jnp.concatenate(sample_rows(pieces, back, s, slice(width, width + EXTRA))).astype(F32)
    for n in range(2):
        value = total[48 * n : 48 * n + 16] + total[48 * n + 16 : 48 * n + 32] + total[48 * n + 32 : 48 * n + 48]
        high = value.astype(BF)
        low = (value - high.astype(F32)).astype(BF)
        for b in range(pairs * deep // 64):
            out_ref[64 * b + 32 * n : 64 * b + 32 * n + 16, width:] = high
            out_ref[64 * b + 32 * n + 16 : 64 * b + 32 * n + 32, width:] = low
    hand_out(slice(width, width + EXTRA))
    tile = 512
    owner = [lax.rem(x + 4 - back, 4) * 2 + (s ^ c) for back, s in order]
    for j in range(width // tile):
        span = slice(j * tile, (j + 1) * tile)
        samples = jnp.concatenate(sum((sample_rows(pieces, back, s, span) for back, s in order), []))
        for p in range(pairs):
            grid = jnp.concatenate([cols_ref[p, a] for a in owner], axis=1)
            out_ref[p * deep : (p + 1) * deep, span] = jnp.dot(grid, samples, preferred_element_type=F32).astype(BF)
        hand_out(span)
    for send in sends:
        send.wait()


def weight_product(pieces, cols):
    wide = pieces[0].shape[1]
    pairs, _, deep, _ = cols.shape
    return pl.pallas_call(
        weight_body,
        in_specs=[VMEM] * 11,
        out_specs=[HBM] * 4,
        out_shape=[jax.ShapeDtypeStruct((pairs * deep // 4, wide), BF)] * 4,
        scratch_shapes=[
            pltpu.VMEM((pairs * deep, wide), BF),
            pltpu.SemaphoreType.DMA((4 + 4 * ((wide - EXTRA) // 512),)),
        ],
        compiler_params=pltpu.CompilerParams(vmem_limit_bytes=24 * 1024 * 1024),
        cost_estimate=BRIEF,
        name="weight_product",
    )(*pieces, cols)


def layer_body(*refs):
    pieces, weights, (out_ref, samples_ref, grid_ref, sems, more) = refs[:10], refs[10:15], refs[15:]
    width = grid_ref.shape[1]
    pairs, _, deep, rows = out_ref.shape
    x, c = lax.axis_index("x"), lax.axis_index("c")
    moves, copies = load_weights(weights, grid_ref, more), []
    for n, (back, start, size) in enumerate(LAY):
        for s in range(2):
            first = (2 * back + s) * rows + start * rows // 2
            source = pieces[2 * n + s].at[:, :width]
            copies.append(
                pltpu.make_async_copy(source, samples_ref.at[first : first + size * rows // 2], sems.at[2 * n + s])
            )
            copies[-1].start()
    for move in moves:
        move.wait()
    for n, (back, start, size) in enumerate(LAY):
        for s in range(2):
            copies[2 * n + s].wait()
        if size == 1 and start == 0:
            continue
        part = lax.dot_general(
            grid_ref[...],
            samples_ref[2 * back * rows : 2 * (back + 1) * rows],
            (((1,), (1,)), ((), ())),
            preferred_element_type=F32,
        )
        for s in range(2):
            owner = lax.rem(x + 4 - back, 4) * 2 + (s ^ c)
            for p in range(pairs):
                block = part[p * deep : (p + 1) * deep, s * rows : (s + 1) * rows]
                out_ref[p, owner] = block.astype(BF)


def layer_product(pieces, weights):
    rows = pieces[0].shape[0]
    width = weights[0].shape[1]
    deep = 4 * weights[0].shape[0]
    return pl.pallas_call(
        layer_body,
        in_specs=[HBM] * 15,
        out_specs=VMEM,
        out_shape=jax.ShapeDtypeStruct((2, 8, deep // 2, rows), BF),
        scratch_shapes=[
            pltpu.VMEM((8 * rows, width), BF),
            pltpu.VMEM((deep, width), BF),
            pltpu.SemaphoreType.DMA((10,)),
            pltpu.SemaphoreType.DMA((10,)),
        ],
        compiler_params=LARGE,
        cost_estimate=BRIEF,
        name="layer_product",
    )(*pieces, *weights)


def fold_body(one, two, three, four, keep_ref, send_ref, total_ref):
    short = keep_ref.shape[0]
    width = keep_ref.shape[1] - EXTRA
    h = lax.axis_index("h")
    total = one[...].astype(F32)
    for ref in (two, three, four):
        total = total + ref[...].astype(F32)
    total_ref[...] = total
    keep_ref[...] = total_ref[pl.ds(pl.multiple_of(h * short, short), short)]
    send_ref[:, :width] = total_ref[pl.ds(pl.multiple_of((1 - h) * short, short), short), :width].astype(BF)
    for n in range(2):
        value = total[32 * n : 32 * n + 16, width:] + total[32 * n + 16 : 32 * n + 32, width:]
        high = value.astype(BF)
        send_ref[32 * n : 32 * n + 16, width:] = high
        send_ref[32 * n + 16 : 32 * n + 32, width:] = (value - high.astype(F32)).astype(BF)


def fold_parts(parts):
    rows, width = parts[0].shape
    return pl.pallas_call(
        fold_body,
        in_specs=[VMEM] * 4,
        out_specs=[VMEM, VMEM],
        out_shape=[
            jax.ShapeDtypeStruct((rows // 2, width), F32),
            jax.ShapeDtypeStruct((rows // 2, width), BF),
        ],
        scratch_shapes=[pltpu.VMEM((rows, width), F32)],
        compiler_params=PARAMS,
        cost_estimate=BRIEF,
        name="fold",
    )(*parts)


def total_body(keep_ref, came_ref, out_ref, sums_ref):
    width = out_ref.shape[1]
    out_ref[...] = keep_ref[:, :width] + came_ref[:, :width].astype(F32)
    for n in range(2):
        both = keep_ref[32 * n : 32 * n + 32, width:] + came_ref[32 * n : 32 * n + 32, width:].astype(F32)
        sums_ref[n] = both[:16] + both[16:]


def total_parts(keep, came):
    rows, width = keep.shape
    return pl.pallas_call(
        total_body,
        in_specs=[VMEM, VMEM],
        out_specs=[VMEM, VMEM],
        out_shape=[
            jax.ShapeDtypeStruct((rows, width - EXTRA), F32),
            jax.ShapeDtypeStruct((2, 16, EXTRA), F32),
        ],
        compiler_params=PARAMS,
        cost_estimate=BRIEF,
        name="total",
    )(keep, came)


def finish_body(parts_ref, cot_ref, out_ref):
    owners, cols = parts_ref.shape[1], parts_ref.shape[3]
    total = parts_ref[0, :, 0].astype(F32) + parts_ref[1, :, 0].astype(F32)
    total = total.reshape(owners * cols, total.shape[2])
    out_ref[...] = (cot_ref[...].astype(F32) + total.T).astype(BF)


def finish(parts, cotangent):
    pairs, owners, blocks, cols, rows = parts.shape
    wide = owners * cols
    return pl.pallas_call(
        finish_body,
        grid=(blocks,),
        in_specs=[
            pl.BlockSpec((pairs, owners, 1, cols, rows), lambda j: (0, 0, j, 0, 0)),
            pl.BlockSpec((rows, wide), lambda j: (0, j)),
        ],
        out_specs=pl.BlockSpec((rows, wide), lambda j: (0, j)),
        out_shape=jax.ShapeDtypeStruct((rows, blocks * wide), BF),
        compiler_params=PARAMS,
        cost_estimate=BRIEF,
        name="finish",
    )(parts, cotangent)


def ahead(value, axis, size, steps):
    return lax.ppermute(value, axis, [(i, (i + steps) % size) for i in range(size)])


def swap(value, axis, size, bit):
    return lax.ppermute(value, axis, [(i, i ^ bit) for i in range(size)])


def ring_gather(value, axis):
    rows = value.shape[0]
    left, right = ahead(value, axis, 4, 1), ahead(value, axis, 4, 3)
    far_low = ahead(left[: rows // 2], axis, 4, 1)
    far_high = ahead(right[rows // 2 :], axis, 4, 3)
    return [value, left, right, far_low, far_high]


def shards(x_first, x_layer, pre_act, gamma, weight, cotangent):
    both = ("t", "x", "c")
    n_near, pairs = 8, 2
    samples, half = x_first.shape
    cols = weight.shape[1]
    blocks = half // (n_near * cols)
    gamma = gamma[None, :]

    by_owner = x_layer.T.reshape(blocks, n_near, cols, samples).transpose(1, 0, 2, 3)
    by_owner = by_owner.reshape(n_near, blocks * cols, samples)
    sent = jnp.concatenate([by_owner] * pairs, axis=0)
    weight_bf = weight.T.astype(BF)
    x_first, sent, weight_bf = lax.optimization_barrier((x_first, sent, weight_bf))
    came = lax.all_to_all(sent, both, 0, 0, tiled=True).reshape(pairs, n_near, blocks * cols, samples)

    gpre = gate_step(x_first, pre_act, gamma, cotangent)
    own = ring_gather(gpre, "x")
    weight_two = jnp.concatenate([weight_bf, swap(weight_bf, "h", 2, 1)], axis=0)
    weights = ring_gather(weight_two, "y")
    grad_first = first_step(pre_act, gamma, cotangent)

    own, came, grad_first = lax.optimization_barrier((own, came, grad_first))
    pieces = []
    for piece in own:
        pieces += [piece, swap(piece, "c", 2, 1)]

    parts = weight_product(pieces, came)
    pieces, parts = lax.optimization_barrier((pieces, parts))
    weight_parts = [parts[0]] + [ahead(parts[k], "y", 4, k) for k in (1, 2, 3)]
    sent = layer_product(pieces, weights).reshape(pairs * n_near, blocks * cols, samples)
    layer_parts = lax.all_to_all(sent, both, 0, 0, tiled=True)
    kept, folded = fold_parts(weight_parts)
    grad_layer = finish(layer_parts.reshape(pairs, n_near, blocks, cols, samples), cotangent)
    grad_weight, sums = total_parts(kept, swap(folded, "h", 2, 1))
    return grad_first, grad_layer, grad_weight.T, sums[0].reshape(half), sums[1].reshape(half)


def solution(mesh):
    fine = Mesh(mesh.devices.reshape(2, 4, 2, 4, 2), ("t", "y", "h", "x", "c"))
    batch = ("y", "h", "x", "c")
    wide = P(batch, "t")
    return jax.shard_map(
        shards,
        mesh=fine,
        in_specs=(wide, wide, wide, P("t"), P("t", batch), wide),
        out_specs=(wide, wide, P("t", batch), P("t"), P("t")),
        check_vma=False,
    )
```

```python
import jax
import jax.numpy as jnp
from jax import lax
from jax.experimental import pallas as pl
from jax.experimental.pallas import tpu as pltpu
from jax.sharding import Mesh, PartitionSpec as P

BF = jnp.bfloat16
F32 = jnp.float32
PARAMS = pltpu.CompilerParams(vmem_limit_bytes=20 * 1024 * 1024)
LARGE = pltpu.CompilerParams(vmem_limit_bytes=60 * 1024 * 1024)
ANY = pl.BlockSpec(memory_space=pl.ANY)
VMEM = pl.BlockSpec(memory_space=pltpu.VMEM)
HBM = pl.BlockSpec(memory_space=pltpu.HBM)
EXTRA = 128
BRIEF = pl.CostEstimate(flops=1000, bytes_accessed=1000, transcendentals=0)


def gate_body(first_ref, pre_ref, gamma_ref, cot_ref, gpre_ref, *scratch):
    bufs, sems = scratch[:3], scratch[3]
    rows, width = first_ref.shape
    lanes = gpre_ref.shape[1] - width
    tile = 512
    copies = []
    for j in range(width // tile):
        span = slice(j * tile, (j + 1) * tile)
        for n, ref in enumerate((first_ref, pre_ref, cot_ref)):
            copies.append(pltpu.make_async_copy(ref.at[:, span], bufs[n].at[:, span], sems.at[3 * j + n]))
            copies[-1].start()
    gpre_ref[96:, width:] = jnp.zeros((rows - 96, lanes), BF)
    for j in range(width // tile):
        span = slice(j * tile, (j + 1) * tile)
        for copy in copies[3 * j : 3 * j + 3]:
            copy.wait()
        gamma = gamma_ref[:, span]
        pre = bufs[1][:, span].astype(F32)
        gate = jnp.tanh(gamma * pre)
        hidden = bufs[2][:, span].astype(F32) * bufs[0][:, span].astype(F32)
        turn = pre * (1.0 - gate * gate)
        gpre = (hidden * (gate + gamma * turn)).astype(BF)
        gpre_ref[:, span] = gpre
        sums = jnp.sum(gpre.astype(F32), axis=0, keepdims=True), jnp.sum(hidden * pre * turn, axis=0, keepdims=True)
        for n, rest in enumerate(sums):
            for p in range(3):
                piece = rest.astype(BF)
                rest = rest - piece.astype(F32)
                for i in range(tile // lanes):
                    row = 48 * n + 16 * p + j * (tile // lanes) + i
                    gpre_ref[row : row + 1, width:] = piece[:, i * lanes : (i + 1) * lanes]


def gate_step(x_first, pre_act, gamma, cotangent):
    rows, width = x_first.shape
    buf = pltpu.VMEM((rows, width), BF)
    return pl.pallas_call(
        gate_body,
        in_specs=[ANY, ANY, VMEM, ANY],
        out_specs=VMEM,
        out_shape=jax.ShapeDtypeStruct((rows, width + EXTRA), BF),
        scratch_shapes=[buf, buf, buf, pltpu.SemaphoreType.DMA((3 * width // 512,))],
        compiler_params=LARGE,
        cost_estimate=pl.CostEstimate(flops=rows * width * 20, bytes_accessed=rows * width * 8, transcendentals=rows * width),
        name="gate",
    )(x_first, pre_act, gamma, cotangent)


def first_body(pre_ref, gamma_ref, cot_ref, out_ref):
    pre = pre_ref[...].astype(F32)
    out_ref[...] = (cot_ref[...].astype(F32) * (pre * jnp.tanh(gamma_ref[...] * pre))).astype(BF)


def first_step(pre_act, gamma, cotangent):
    rows, width = pre_act.shape
    tile = 512
    block = pl.BlockSpec((rows, tile), lambda j: (0, j))
    return pl.pallas_call(
        first_body,
        grid=(width // tile,),
        in_specs=[block, pl.BlockSpec((1, tile), lambda j: (0, j)), block],
        out_specs=block,
        out_shape=jax.ShapeDtypeStruct((rows, width), BF),
        compiler_params=LARGE,
        cost_estimate=BRIEF,
        name="first",
    )(pre_act, gamma, cotangent)


LAY = ((0, 0, 2), (1, 0, 2), (3, 0, 2), (2, 0, 1), (2, 1, 1))


def sample_rows(pieces, back, s, span):
    return [pieces[2 * n + s][:, span] for n, place in enumerate(LAY) if place[0] == back]


def load_weights(weights, grid_ref, sems):
    short = grid_ref.shape[0] // 8
    y, h = lax.axis_index("y"), lax.axis_index("h")
    moves = []
    for k in range(4):
        place_y = lax.rem(y + 4 - k, 4)
        for s in range(2):
            place = pl.ds(pl.multiple_of((place_y * 2 + (s ^ h)) * short, short), short)
            source = weights[k].at[s * short : (s + 1) * short]
            moves.append(pltpu.make_async_copy(source, grid_ref.at[place], sems.at[2 * k + s]))
            moves[-1].start()
    return moves


def weight_body(*refs):
    pieces, cols_ref = refs[:10], refs[10]
    results, (out_ref, sems) = refs[11:15], refs[15:]
    pairs, owners, deep, rows = cols_ref.shape
    width = out_ref.shape[1] - EXTRA
    x, c, y = lax.axis_index("x"), lax.axis_index("c"), lax.axis_index("y")
    sends = []

    def hand_out(span):
        for k, result_ref in enumerate(results):
            block = pl.ds(pl.multiple_of(lax.rem(y + k, 4) * 2 * 64, 128), 128)
            sends.append(pltpu.make_async_copy(out_ref.at[block, span], result_ref.at[:, span], sems.at[len(sends)]))
            sends[-1].start()

    order = [(back, s) for back in range(4) for s in range(2)]
    total = 0.0
    for back, s in order:
        total = total + jnp.concatenate(sample_rows(pieces, back, s, slice(width, width + EXTRA))).astype(F32)
    for n in range(2):
        value = total[48 * n : 48 * n + 16] + total[48 * n + 16 : 48 * n + 32] + total[48 * n + 32 : 48 * n + 48]
        high = value.astype(BF)
        low = (value - high.astype(F32)).astype(BF)
        for b in range(pairs * deep // 64):
            out_ref[64 * b + 32 * n : 64 * b + 32 * n + 16, width:] = high
            out_ref[64 * b + 32 * n + 16 : 64 * b + 32 * n + 32, width:] = low
    hand_out(slice(width, width + EXTRA))
    tile = 512
    owner = [lax.rem(x + 4 - back, 4) * 2 + (s ^ c) for back, s in order]
    for j in range(width // tile):
        span = slice(j * tile, (j + 1) * tile)
        samples = jnp.concatenate(sum((sample_rows(pieces, back, s, span) for back, s in order), []))
        for p in range(pairs):
            grid = jnp.concatenate([cols_ref[p, a] for a in owner], axis=1)
            out_ref[p * deep : (p + 1) * deep, span] = jnp.dot(grid, samples, preferred_element_type=F32).astype(BF)
        hand_out(span)
    for send in sends:
        send.wait()


def weight_product(pieces, cols):
    wide = pieces[0].shape[1]
    pairs, _, deep, _ = cols.shape
    return pl.pallas_call(
        weight_body,
        in_specs=[VMEM] * 11,
        out_specs=[HBM] * 4,
        out_shape=[jax.ShapeDtypeStruct((pairs * deep // 4, wide), BF)] * 4,
        scratch_shapes=[
            pltpu.VMEM((pairs * deep, wide), BF),
            pltpu.SemaphoreType.DMA((4 + 4 * ((wide - EXTRA) // 512),)),
        ],
        compiler_params=pltpu.CompilerParams(vmem_limit_bytes=24 * 1024 * 1024),
        cost_estimate=BRIEF,
        name="weight_product",
    )(*pieces, cols)


def layer_body(*refs):
    pieces, weights, (out_ref, samples_ref, grid_ref, sems, more) = refs[:10], refs[10:14], refs[14:]
    width = grid_ref.shape[1]
    pairs, _, deep, rows = out_ref.shape
    x, c = lax.axis_index("x"), lax.axis_index("c")
    moves, copies = load_weights(weights, grid_ref, more), []
    for n, (back, start, size) in enumerate(LAY):
        for s in range(2):
            first = (2 * back + s) * rows + start * rows // 2
            source = pieces[2 * n + s].at[:, :width]
            copies.append(
                pltpu.make_async_copy(source, samples_ref.at[first : first + size * rows // 2], sems.at[2 * n + s])
            )
            copies[-1].start()
    for move in moves:
        move.wait()
    for n, (back, start, size) in enumerate(LAY):
        for s in range(2):
            copies[2 * n + s].wait()
        if size == 1 and start == 0:
            continue
        part = lax.dot_general(
            grid_ref[...],
            samples_ref[2 * back * rows : 2 * (back + 1) * rows],
            (((1,), (1,)), ((), ())),
            preferred_element_type=F32,
        )
        for s in range(2):
            owner = lax.rem(x + 4 - back, 4) * 2 + (s ^ c)
            for p in range(pairs):
                block = part[p * deep : (p + 1) * deep, s * rows : (s + 1) * rows]
                out_ref[p, owner] = block.astype(BF)


def layer_product(pieces, weights):
    rows = pieces[0].shape[0]
    width = weights[0].shape[1]
    deep = 4 * weights[0].shape[0]
    return pl.pallas_call(
        layer_body,
        in_specs=[HBM] * 14,
        out_specs=VMEM,
        out_shape=jax.ShapeDtypeStruct((2, 8, deep // 2, rows), BF),
        scratch_shapes=[
            pltpu.VMEM((8 * rows, width), BF),
            pltpu.VMEM((deep, width), BF),
            pltpu.SemaphoreType.DMA((10,)),
            pltpu.SemaphoreType.DMA((8,)),
        ],
        compiler_params=LARGE,
        cost_estimate=BRIEF,
        name="layer_product",
    )(*pieces, *weights)


def fold_body(one, two, three, four, keep_ref, send_ref, total_ref):
    short = keep_ref.shape[0]
    width = keep_ref.shape[1] - EXTRA
    h = lax.axis_index("h")
    total = one[...].astype(F32)
    for ref in (two, three, four):
        total = total + ref[...].astype(F32)
    total_ref[...] = total
    keep_ref[...] = total_ref[pl.ds(pl.multiple_of(h * short, short), short)]
    send_ref[:, :width] = total_ref[pl.ds(pl.multiple_of((1 - h) * short, short), short), :width].astype(BF)
    for n in range(2):
        value = total[32 * n : 32 * n + 16, width:] + total[32 * n + 16 : 32 * n + 32, width:]
        high = value.astype(BF)
        send_ref[32 * n : 32 * n + 16, width:] = high
        send_ref[32 * n + 16 : 32 * n + 32, width:] = (value - high.astype(F32)).astype(BF)


def fold_parts(parts):
    rows, width = parts[0].shape
    return pl.pallas_call(
        fold_body,
        in_specs=[VMEM] * 4,
        out_specs=[VMEM, VMEM],
        out_shape=[
            jax.ShapeDtypeStruct((rows // 2, width), F32),
            jax.ShapeDtypeStruct((rows // 2, width), BF),
        ],
        scratch_shapes=[pltpu.VMEM((rows, width), F32)],
        compiler_params=PARAMS,
        cost_estimate=BRIEF,
        name="fold",
    )(*parts)


def total_body(keep_ref, came_ref, out_ref, sums_ref):
    width = out_ref.shape[1]
    out_ref[...] = keep_ref[:, :width] + came_ref[:, :width].astype(F32)
    for n in range(2):
        both = keep_ref[32 * n : 32 * n + 32, width:] + came_ref[32 * n : 32 * n + 32, width:].astype(F32)
        sums_ref[n] = both[:16] + both[16:]


def total_parts(keep, came):
    rows, width = keep.shape
    return pl.pallas_call(
        total_body,
        in_specs=[VMEM, VMEM],
        out_specs=[VMEM, VMEM],
        out_shape=[
            jax.ShapeDtypeStruct((rows, width - EXTRA), F32),
            jax.ShapeDtypeStruct((2, 16, EXTRA), F32),
        ],
        compiler_params=PARAMS,
        cost_estimate=BRIEF,
        name="total",
    )(keep, came)


def finish_body(parts_ref, cot_ref, out_ref):
    owners, cols = parts_ref.shape[1], parts_ref.shape[3]
    total = parts_ref[0, :, 0].astype(F32) + parts_ref[1, :, 0].astype(F32)
    total = total.reshape(owners * cols, total.shape[2])
    out_ref[...] = (cot_ref[...].astype(F32) + total.T).astype(BF)


def finish(parts, cotangent):
    pairs, owners, blocks, cols, rows = parts.shape
    wide = owners * cols
    return pl.pallas_call(
        finish_body,
        grid=(blocks,),
        in_specs=[
            pl.BlockSpec((pairs, owners, 1, cols, rows), lambda j: (0, 0, j, 0, 0)),
            pl.BlockSpec((rows, wide), lambda j: (0, j)),
        ],
        out_specs=pl.BlockSpec((rows, wide), lambda j: (0, j)),
        out_shape=jax.ShapeDtypeStruct((rows, blocks * wide), BF),
        compiler_params=PARAMS,
        cost_estimate=BRIEF,
        name="finish",
    )(parts, cotangent)


def ahead(value, axis, size, steps):
    return lax.ppermute(value, axis, [(i, (i + steps) % size) for i in range(size)])


def swap(value, axis, size, bit):
    return lax.ppermute(value, axis, [(i, i ^ bit) for i in range(size)])


def ring_gather(value, axis):
    rows = value.shape[0]
    left, right = ahead(value, axis, 4, 1), ahead(value, axis, 4, 3)
    far_low = ahead(left[: rows // 2], axis, 4, 1)
    far_high = ahead(right[rows // 2 :], axis, 4, 3)
    return [value, left, right, far_low, far_high]


def shards(x_first, x_layer, pre_act, gamma, weight, cotangent):
    both = ("t", "x", "c")
    n_near, pairs = 8, 2
    samples, half = x_first.shape
    cols = weight.shape[1]
    blocks = half // (n_near * cols)
    gamma = gamma[None, :]

    by_owner = x_layer.T.reshape(blocks, n_near, cols, samples).transpose(1, 0, 2, 3)
    by_owner = by_owner.reshape(n_near, blocks * cols, samples)
    sent = jnp.concatenate([by_owner] * pairs, axis=0)
    weight_bf = weight.T.astype(BF)
    x_first, sent, weight_bf = lax.optimization_barrier((x_first, sent, weight_bf))
    came = lax.all_to_all(sent, both, 0, 0, tiled=True).reshape(pairs, n_near, blocks * cols, samples)

    gpre = gate_step(x_first, pre_act, gamma, cotangent)
    own = ring_gather(gpre, "x")
    weight_two = jnp.concatenate([weight_bf, swap(weight_bf, "h", 2, 1)], axis=0)
    weights = [weight_two] + [ahead(weight_two, "y", 4, k) for k in (1, 2, 3)]
    grad_first = first_step(pre_act, gamma, cotangent)

    own, weights, came, grad_first = lax.optimization_barrier((own, weights, came, grad_first))
    pieces = []
    for piece in own:
        pieces += [piece, swap(piece, "c", 2, 1)]

    parts = weight_product(pieces, came)
    pieces, parts = lax.optimization_barrier((pieces, parts))
    weight_parts = [parts[0]] + [ahead(parts[k], "y", 4, k) for k in (1, 2, 3)]
    sent = layer_product(pieces, weights).reshape(pairs * n_near, blocks * cols, samples)
    layer_parts = lax.all_to_all(sent, both, 0, 0, tiled=True)
    kept, folded = fold_parts(weight_parts)
    grad_layer = finish(layer_parts.reshape(pairs, n_near, blocks, cols, samples), cotangent)
    grad_weight, sums = total_parts(kept, swap(folded, "h", 2, 1))
    return grad_first, grad_layer, grad_weight.T, sums[0].reshape(half), sums[1].reshape(half)


def solution(mesh):
    fine = Mesh(mesh.devices.reshape(2, 4, 2, 4, 2), ("t", "y", "h", "x", "c"))
    batch = ("y", "h", "x", "c")
    wide = P(batch, "t")
    return jax.shard_map(
        shards,
        mesh=fine,
        in_specs=(wide, wide, wide, P("t"), P("t", batch), wide),
        out_specs=(wide, wide, P("t", batch), P("t"), P("t")),
        check_vma=False,
    )
```

```python
import jax
import jax.numpy as jnp
from jax import lax
from jax.experimental import pallas as pl
from jax.experimental.pallas import tpu as pltpu
from jax.sharding import Mesh, PartitionSpec as P

BF = jnp.bfloat16
F32 = jnp.float32
PARAMS = pltpu.CompilerParams(vmem_limit_bytes=20 * 1024 * 1024)
LARGE = pltpu.CompilerParams(vmem_limit_bytes=60 * 1024 * 1024)
ANY = pl.BlockSpec(memory_space=pl.ANY)
VMEM = pl.BlockSpec(memory_space=pltpu.VMEM)
HBM = pl.BlockSpec(memory_space=pltpu.HBM)
EXTRA = 128
BRIEF = pl.CostEstimate(flops=1000, bytes_accessed=1000, transcendentals=0)


def gate_body(first_ref, pre_ref, gamma_ref, cot_ref, gpre_ref, *scratch):
    bufs, rows_ref, sems = scratch[:3], scratch[3], scratch[4]
    rows, width = first_ref.shape
    lanes = gpre_ref.shape[1] - width
    tile = 512
    copies = []
    for j in range(width // tile):
        span = slice(j * tile, (j + 1) * tile)
        for n, ref in enumerate((first_ref, pre_ref, cot_ref)):
            copies.append(pltpu.make_async_copy(ref.at[:, span], bufs[n].at[:, span], sems.at[3 * j + n]))
            copies[-1].start()
    rows_ref[96:] = jnp.zeros((rows - 96, lanes), F32)
    for j in range(width // tile):
        span = slice(j * tile, (j + 1) * tile)
        for copy in copies[3 * j : 3 * j + 3]:
            copy.wait()
        gamma = gamma_ref[:, span]
        pre = bufs[1][:, span].astype(F32)
        gate = jnp.tanh(gamma * pre)
        hidden = bufs[2][:, span].astype(F32) * bufs[0][:, span].astype(F32)
        turn = pre * (1.0 - gate * gate)
        gpre = (hidden * (gate + gamma * turn)).astype(BF)
        gpre_ref[:, span] = gpre
        sums = jnp.sum(gpre.astype(F32), axis=0, keepdims=True), jnp.sum(hidden * pre * turn, axis=0, keepdims=True)
        for n, rest in enumerate(sums):
            for p in range(3):
                piece = rest.astype(BF).astype(F32)
                rest = rest - piece
                for i in range(tile // lanes):
                    row = 48 * n + 16 * p + j * (tile // lanes) + i
                    rows_ref[row : row + 1] = piece[:, i * lanes : (i + 1) * lanes]
    gpre_ref[:, width:] = rows_ref[...].astype(BF)


def gate_step(x_first, pre_act, gamma, cotangent):
    rows, width = x_first.shape
    buf = pltpu.VMEM((rows, width), BF)
    return pl.pallas_call(
        gate_body,
        in_specs=[ANY, ANY, VMEM, ANY],
        out_specs=VMEM,
        out_shape=jax.ShapeDtypeStruct((rows, width + EXTRA), BF),
        scratch_shapes=[buf, buf, buf, pltpu.VMEM((rows, EXTRA), F32), pltpu.SemaphoreType.DMA((3 * width // 512,))],
        compiler_params=LARGE,
        cost_estimate=pl.CostEstimate(flops=rows * width * 20, bytes_accessed=rows * width * 8, transcendentals=rows * width),
        name="gate",
    )(x_first, pre_act, gamma, cotangent)


def first_body(pre_ref, gamma_ref, cot_ref, out_ref):
    pre = pre_ref[...].astype(F32)
    out_ref[...] = (cot_ref[...].astype(F32) * (pre * jnp.tanh(gamma_ref[...] * pre))).astype(BF)


def first_step(pre_act, gamma, cotangent):
    rows, width = pre_act.shape
    tile = 512
    block = pl.BlockSpec((rows, tile), lambda j: (0, j))
    return pl.pallas_call(
        first_body,
        grid=(width // tile,),
        in_specs=[block, pl.BlockSpec((1, tile), lambda j: (0, j)), block],
        out_specs=block,
        out_shape=jax.ShapeDtypeStruct((rows, width), BF),
        compiler_params=LARGE,
        cost_estimate=BRIEF,
        name="first",
    )(pre_act, gamma, cotangent)


LAY = ((0, 0, 2), (1, 0, 2), (3, 0, 2), (2, 0, 1), (2, 1, 1))


def sample_rows(pieces, back, s, span):
    return [pieces[2 * n + s][:, span] for n, place in enumerate(LAY) if place[0] == back]


def load_weights(weights, grid_ref, sems):
    short = grid_ref.shape[0] // 8
    y, h = lax.axis_index("y"), lax.axis_index("h")
    moves = []
    for n, (back, start, size) in enumerate(LAY):
        place_y = lax.rem(y + 4 - back, 4)
        for s in range(size):
            block = place_y * 2 + ((start + s) ^ h)
            place = pl.ds(pl.multiple_of(block * short, short), short)
            source = weights[n].at[s * short : (s + 1) * short]
            moves.append(pltpu.make_async_copy(source, grid_ref.at[place], sems.at[2 * n + s]))
            moves[-1].start()
    return moves


def weight_body(*refs):
    pieces, cols_ref = refs[:10], refs[10]
    results, (out_ref, sems) = refs[11:15], refs[15:]
    pairs, owners, deep, rows = cols_ref.shape
    width = out_ref.shape[1] - EXTRA
    x, c, y = lax.axis_index("x"), lax.axis_index("c"), lax.axis_index("y")
    sends = []

    def hand_out(span):
        for k, result_ref in enumerate(results):
            block = pl.ds(pl.multiple_of(lax.rem(y + k, 4) * 2 * 64, 128), 128)
            sends.append(pltpu.make_async_copy(out_ref.at[block, span], result_ref.at[:, span], sems.at[len(sends)]))
            sends[-1].start()

    order = [(back, s) for back in range(4) for s in range(2)]
    total = 0.0
    for back, s in order:
        total = total + jnp.concatenate(sample_rows(pieces, back, s, slice(width, width + EXTRA))).astype(F32)
    for n in range(2):
        value = total[48 * n : 48 * n + 16] + total[48 * n + 16 : 48 * n + 32] + total[48 * n + 32 : 48 * n + 48]
        high = value.astype(BF)
        low = (value - high.astype(F32)).astype(BF)
        for b in range(pairs * deep // 64):
            out_ref[64 * b + 32 * n : 64 * b + 32 * n + 16, width:] = high
            out_ref[64 * b + 32 * n + 16 : 64 * b + 32 * n + 32, width:] = low
    hand_out(slice(width, width + EXTRA))
    tile = 512
    owner = [lax.rem(x + 4 - back, 4) * 2 + (s ^ c) for back, s in order]
    for j in range(width // tile):
        span = slice(j * tile, (j + 1) * tile)
        samples = jnp.concatenate(sum((sample_rows(pieces, back, s, span) for back, s in order), []))
        for p in range(pairs):
            grid = jnp.concatenate([cols_ref[p, a] for a in owner], axis=1)
            out_ref[p * deep : (p + 1) * deep, span] = jnp.dot(grid, samples, preferred_element_type=F32).astype(BF)
        hand_out(span)
    for send in sends:
        send.wait()


def weight_product(pieces, cols):
    wide = pieces[0].shape[1]
    pairs, _, deep, _ = cols.shape
    return pl.pallas_call(
        weight_body,
        in_specs=[VMEM] * 11,
        out_specs=[HBM] * 4,
        out_shape=[jax.ShapeDtypeStruct((pairs * deep // 4, wide), BF)] * 4,
        scratch_shapes=[
            pltpu.VMEM((pairs * deep, wide), BF),
            pltpu.SemaphoreType.DMA((4 + 4 * ((wide - EXTRA) // 512),)),
        ],
        compiler_params=pltpu.CompilerParams(vmem_limit_bytes=24 * 1024 * 1024),
        cost_estimate=BRIEF,
        name="weight_product",
    )(*pieces, cols)


def layer_body(*refs):
    pieces, weights, (out_ref, samples_ref, grid_ref, sems, more) = refs[:10], refs[10:15], refs[15:]
    width = grid_ref.shape[1]
    pairs, _, deep, rows = out_ref.shape
    x, c = lax.axis_index("x"), lax.axis_index("c")
    moves, copies = load_weights(weights, grid_ref, more), []
    for n, (back, start, size) in enumerate(LAY):
        for s in range(2):
            first = (2 * back + s) * rows + start * rows // 2
            source = pieces[2 * n + s].at[:, :width]
            copies.append(
                pltpu.make_async_copy(source, samples_ref.at[first : first + size * rows // 2], sems.at[2 * n + s])
            )
            copies[-1].start()
    for move in moves:
        move.wait()
    for n, (back, start, size) in enumerate(LAY):
        for s in range(2):
            copies[2 * n + s].wait()
        if size == 1 and start == 0:
            continue
        part = lax.dot_general(
            grid_ref[...],
            samples_ref[2 * back * rows : 2 * (back + 1) * rows],
            (((1,), (1,)), ((), ())),
            preferred_element_type=F32,
        )
        for s in range(2):
            owner = lax.rem(x + 4 - back, 4) * 2 + (s ^ c)
            for p in range(pairs):
                block = part[p * deep : (p + 1) * deep, s * rows : (s + 1) * rows]
                out_ref[p, owner] = block.astype(BF)


def layer_product(pieces, weights):
    rows = pieces[0].shape[0]
    width = weights[0].shape[1]
    deep = 4 * weights[0].shape[0]
    return pl.pallas_call(
        layer_body,
        in_specs=[HBM] * 15,
        out_specs=VMEM,
        out_shape=jax.ShapeDtypeStruct((2, 8, deep // 2, rows), BF),
        scratch_shapes=[
            pltpu.VMEM((8 * rows, width), BF),
            pltpu.VMEM((deep, width), BF),
            pltpu.SemaphoreType.DMA((10,)),
            pltpu.SemaphoreType.DMA((10,)),
        ],
        compiler_params=LARGE,
        cost_estimate=BRIEF,
        name="layer_product",
    )(*pieces, *weights)


def fold_body(one, two, three, four, keep_ref, send_ref, total_ref):
    short = keep_ref.shape[0]
    width = keep_ref.shape[1] - EXTRA
    h = lax.axis_index("h")
    total = one[...].astype(F32)
    for ref in (two, three, four):
        total = total + ref[...].astype(F32)
    total_ref[...] = total
    keep_ref[...] = total_ref[pl.ds(pl.multiple_of(h * short, short), short)]
    send_ref[:, :width] = total_ref[pl.ds(pl.multiple_of((1 - h) * short, short), short), :width].astype(BF)
    for n in range(2):
        value = total[32 * n : 32 * n + 16, width:] + total[32 * n + 16 : 32 * n + 32, width:]
        high = value.astype(BF)
        send_ref[32 * n : 32 * n + 16, width:] = high
        send_ref[32 * n + 16 : 32 * n + 32, width:] = (value - high.astype(F32)).astype(BF)


def fold_parts(parts):
    rows, width = parts[0].shape
    return pl.pallas_call(
        fold_body,
        in_specs=[VMEM] * 4,
        out_specs=[VMEM, VMEM],
        out_shape=[
            jax.ShapeDtypeStruct((rows // 2, width), F32),
            jax.ShapeDtypeStruct((rows // 2, width), BF),
        ],
        scratch_shapes=[pltpu.VMEM((rows, width), F32)],
        compiler_params=PARAMS,
        cost_estimate=BRIEF,
        name="fold",
    )(*parts)


def total_body(keep_ref, came_ref, out_ref, sums_ref):
    width = out_ref.shape[1]
    out_ref[...] = keep_ref[:, :width] + came_ref[:, :width].astype(F32)
    for n in range(2):
        both = keep_ref[32 * n : 32 * n + 32, width:] + came_ref[32 * n : 32 * n + 32, width:].astype(F32)
        sums_ref[n] = both[:16] + both[16:]


def total_parts(keep, came):
    rows, width = keep.shape
    return pl.pallas_call(
        total_body,
        in_specs=[VMEM, VMEM],
        out_specs=[VMEM, VMEM],
        out_shape=[
            jax.ShapeDtypeStruct((rows, width - EXTRA), F32),
            jax.ShapeDtypeStruct((2, 16, EXTRA), F32),
        ],
        compiler_params=PARAMS,
        cost_estimate=BRIEF,
        name="total",
    )(keep, came)


def finish_body(parts_ref, cot_ref, out_ref):
    owners, cols = parts_ref.shape[1], parts_ref.shape[3]
    total = parts_ref[0, :, 0].astype(F32) + parts_ref[1, :, 0].astype(F32)
    total = total.reshape(owners * cols, total.shape[2])
    out_ref[...] = (cot_ref[...].astype(F32) + total.T).astype(BF)


def finish(parts, cotangent):
    pairs, owners, blocks, cols, rows = parts.shape
    wide = owners * cols
    return pl.pallas_call(
        finish_body,
        grid=(blocks,),
        in_specs=[
            pl.BlockSpec((pairs, owners, 1, cols, rows), lambda j: (0, 0, j, 0, 0)),
            pl.BlockSpec((rows, wide), lambda j: (0, j)),
        ],
        out_specs=pl.BlockSpec((rows, wide), lambda j: (0, j)),
        out_shape=jax.ShapeDtypeStruct((rows, blocks * wide), BF),
        compiler_params=PARAMS,
        cost_estimate=BRIEF,
        name="finish",
    )(parts, cotangent)


def ahead(value, axis, size, steps):
    return lax.ppermute(value, axis, [(i, (i + steps) % size) for i in range(size)])


def swap(value, axis, size, bit):
    return lax.ppermute(value, axis, [(i, i ^ bit) for i in range(size)])


def ring_gather(value, axis):
    rows = value.shape[0]
    left, right = ahead(value, axis, 4, 1), ahead(value, axis, 4, 3)
    far_low = ahead(left[: rows // 2], axis, 4, 1)
    far_high = ahead(right[rows // 2 :], axis, 4, 3)
    return [value, left, right, far_low, far_high]


def shards(x_first, x_layer, pre_act, gamma, weight, cotangent):
    both = ("t", "x", "c")
    n_near, pairs = 8, 2
    samples, half = x_first.shape
    cols = weight.shape[1]
    blocks = half // (n_near * cols)
    gamma = gamma[None, :]

    by_owner = x_layer.T.reshape(blocks, n_near, cols, samples).transpose(1, 0, 2, 3)
    by_owner = by_owner.reshape(n_near, blocks * cols, samples)
    sent = jnp.concatenate([by_owner] * pairs, axis=0)
    weight_bf = weight.T.astype(BF)
    x_first, sent, weight_bf = lax.optimization_barrier((x_first, sent, weight_bf))
    came = lax.all_to_all(sent, both, 0, 0, tiled=True).reshape(pairs, n_near, blocks * cols, samples)

    gpre = gate_step(x_first, pre_act, gamma, cotangent)
    own = ring_gather(gpre, "x")
    weight_two = jnp.concatenate([weight_bf, swap(weight_bf, "h", 2, 1)], axis=0)
    weights = ring_gather(weight_two, "y")
    grad_first = first_step(pre_act, gamma, cotangent)

    own, weights, came, grad_first = lax.optimization_barrier((own, weights, came, grad_first))
    pieces = []
    for piece in own:
        pieces += [piece, swap(piece, "c", 2, 1)]

    parts = weight_product(pieces, came)
    pieces, parts = lax.optimization_barrier((pieces, parts))
    weight_parts = [parts[0]] + [ahead(parts[k], "y", 4, k) for k in (1, 2, 3)]
    sent = layer_product(pieces, weights).reshape(pairs * n_near, blocks * cols, samples)
    layer_parts = lax.all_to_all(sent, both, 0, 0, tiled=True)
    kept, folded = fold_parts(weight_parts)
    grad_layer = finish(layer_parts.reshape(pairs, n_near, blocks, cols, samples), cotangent)
    grad_weight, sums = total_parts(kept, swap(folded, "h", 2, 1))
    return grad_first, grad_layer, grad_weight.T, sums[0].reshape(half), sums[1].reshape(half)


def solution(mesh):
    fine = Mesh(mesh.devices.reshape(2, 4, 2, 4, 2), ("t", "y", "h", "x", "c"))
    batch = ("y", "h", "x", "c")
    wide = P(batch, "t")
    return jax.shard_map(
        shards,
        mesh=fine,
        in_specs=(wide, wide, wide, P("t"), P("t", batch), wide),
        out_specs=(wide, wide, P("t", batch), P("t"), P("t")),
        check_vma=False,
    )
```
